32 devices in a mesh: seq: 2 (over core), mp: 4 (over y, x), dp: 4 (over z).
Axes of the slice: x: 2, y: 2, z: 4, core: 2. Of those that a mesh axis runs over, the one named last changes fastest.
Arguments:
- tokens: bfloat16 [2048, 8, 1024], P('seq', 'dp'), may hold values from -6 to 6
- lengths: int32 [8], P('dp'), may hold values from 512 to 2048, as said below
- mixer_gain: bfloat16 [1024], replicated, may hold values from 0.099609375 to 1.8984375
- project_weight: bfloat16 [1024, 4, 512], P(None, 'mp'), may hold values from -0.1875 to 0.1875
- filter_weight: bfloat16 [4, 4, 512], P(None, 'mp'), may hold values from -3 to 3
- rank_down: bfloat16 [1024, 16], replicated, may hold values from -0.1875 to 0.1875
- rank_up: bfloat16 [16, 4, 128], P(None, 'mp'), may hold values from -1.5 to 1.5
- decay_bias: float32 [4, 128], P('mp'), may hold values from -1 to 6
- gate_weight: bfloat16 [1024, 1024], P(None, 'mp'), may hold values from -0.1875 to 0.1875
- head_gain: bfloat16 [256], replicated, may hold values from 0.099609375 to 1.8984375
- output_weight: bfloat16 [1024, 1024], P('mp'), may hold values from -0.1875 to 0.1875
- channel_gain: bfloat16 [1024], replicated, may hold values from 0.099609375 to 1.8984375
- hidden_gate: bfloat16 [1024, 2816], P(None, 'mp'), may hold values from -0.1875 to 0.1875
- hidden_up: bfloat16 [1024, 2816], P(None, 'mp'), may hold values from -0.1875 to 0.1875
- hidden_down: bfloat16 [2816, 1024], P('mp'), may hold values from -0.109375 to 0.109375
- cotangent: bfloat16 [2048, 8, 1024], P('seq', 'dp'), may hold values from -6 to 6
Outputs:
- output: bfloat16 [2048, 8, 1024], P(('seq', 'mp'), 'dp')
- tokens_grad: float32 [2048, 8, 1024], P(('seq', 'mp'), 'dp')
- mixer_gain_grad: float32 [1024], replicated
- project_grad: float32 [1024, 4, 512], P(('seq', 'dp'), 'mp')
- filter_grad: float32 [4, 4, 512], P(None, 'mp', ('seq', 'dp'))
- rank_down_grad: float32 [1024, 16], replicated
- rank_up_grad: float32 [16, 4, 128], P(None, 'mp', ('seq', 'dp'))
- decay_bias_grad: float32 [4, 128], P('mp', ('seq', 'dp'))
- gate_grad: float32 [1024, 1024], P(('seq', 'dp'), 'mp')
- head_gain_grad: float32 [256], replicated
- output_weight_grad: float32 [1024, 1024], P('mp', ('seq', 'dp'))
- channel_gain_grad: float32 [1024], replicated
- hidden_gate_grad: float32 [1024, 2816], P(('seq', 'dp'), 'mp')
- hidden_up_grad: float32 [1024, 2816], P(('seq', 'dp'), 'mp')
- hidden_down_grad: float32 [2816, 1024], P('mp', ('seq', 'dp'))
The draws below stay inside these ranges and needn't reach their ends.
Inputs may be any that keep to these rules, and one draw needn't show every extreme that they name: Sequence s holds its valid positions 0 .. lengths[s] - 1 first; among each 2 consecutive sequences (those of one index of dp) one has all 2048 positions valid.
All inputs are finite; a program needn't handle non-finite values.
Results may differ from the reference program's by a relative error of at most 0.038.
Values may be sent and summed in bfloat16 or wider, within the bound.
A program may use at most 192 MiB of HBM per device.

```python
import jax
import jax.numpy as jnp
from jax import lax

D = 1024
H = 4
DK = 128
DV = 256
RANK = 16
FF = 2816
CONV = 4
BLOCK = 64
SEQS_DP = 2
C3 = 512
LENGTH = 2048
SEQUENCES = 8


def draw_lengths(key, part):
    key = jax.random.fold_in(key, 7)
    key_lengths, key_choice = jax.random.split(key)
    drawn = jax.random.randint(key_lengths, (SEQUENCES,), LENGTH // 4, LENGTH + 1)
    groups = SEQUENCES // SEQS_DP
    chosen = jax.random.randint(key_choice, (groups, 1), 0, SEQS_DP)
    slot_index = lax.broadcasted_iota(jnp.int32, (groups, SEQS_DP), 1)
    complete = jnp.where(slot_index == chosen, LENGTH, drawn.reshape(groups, SEQS_DP))
    return complete.reshape(SEQUENCES).astype(jnp.int32)


def shard_levels(own_key, dims, shards, smallest, top_value):
    factor_of, own = 1.0, jax.random.fold_in(own_key, 6)
    for position, shards_of in shards:
        draws = jnp.exp(jax.random.uniform(jax.random.fold_in(own, position), (shards_of,), jnp.float32, smallest / len(shards), top_value / len(shards)))
        factor_of = factor_of * jnp.repeat(draws, dims[position] // shards_of).reshape([-1 if axis == position else 1 for axis in range(len(dims))])
    return factor_of


def gaussian(stream_key, shape, scale, most, cuts=(), held_as=jnp.bfloat16):
    factor_of = shard_levels(stream_key, shape, cuts, -0.22, 0.18) if cuts else 1.0
    values = jax.random.normal(stream_key, shape, jnp.float32) * scale * factor_of
    return jnp.minimum(jnp.maximum(values, -most), most).astype(held_as)


def setup_inputs(seed: int = 0) -> dict:
    seeds = jax.random.split(jax.random.key(seed), 17)
    return {
        "tokens": gaussian(seeds[0], (LENGTH, SEQUENCES, D), 1.0, 6.0, ((0, 2), (1, 4))),
        "lengths": draw_lengths(jax.random.fold_in(seeds[16], 71), 0),
        "mixer_gain": jnp.clip(1.0 + 0.18 * jax.random.normal(seeds[2], (D,), jnp.float32), 0.099609375, 1.8984375).astype(jnp.bfloat16),
        "project_weight": gaussian(seeds[3], (D, H, C3), D ** -0.5, 0.1875, ((1, 4),)),
        "filter_weight": gaussian(seeds[4], (CONV, H, C3), CONV ** -0.5, 3.0, ((1, 4),)),
        "rank_down": gaussian(seeds[5], (D, RANK), D ** -0.5, 0.1875),
        "rank_up": gaussian(seeds[6], (RANK, H, DK), RANK ** -0.5, 1.5, ((1, 4),)),
        "decay_bias": jnp.clip(-1.0 + 7.0 * jax.random.uniform(seeds[7], (H, DK), jnp.float32) ** shard_levels(seeds[7], (H, DK), ((0, 4),), -0.2, 0.2), -1.0, 6.0),
        "gate_weight": gaussian(seeds[8], (D, H * DV), D ** -0.5, 0.1875, ((1, 4),)),
        "head_gain": jnp.clip(1.0 + 0.18 * jax.random.normal(seeds[9], (DV,), jnp.float32), 0.099609375, 1.8984375).astype(jnp.bfloat16),
        "output_weight": gaussian(seeds[10], (H * DV, D), (H * DV) ** -0.5, 0.1875, ((0, 4),)),
        "channel_gain": jnp.clip(1.0 + 0.18 * jax.random.normal(seeds[11], (D,), jnp.float32), 0.099609375, 1.8984375).astype(jnp.bfloat16),
        "hidden_gate": gaussian(seeds[12], (D, FF), D ** -0.5, 0.1875, ((1, 4),)),
        "hidden_up": gaussian(seeds[13], (D, FF), D ** -0.5, 0.1875, ((1, 4),)),
        "hidden_down": gaussian(seeds[14], (FF, D), FF ** -0.5, 0.109375, ((0, 4),)),
        "cotangent": gaussian(seeds[15], (LENGTH, SEQUENCES, D), 1.0, 6.0, ((0, 2), (1, 4))),
    }


@jax.custom_vjp
def low(v):
    return lax.optimization_barrier(v.astype(jnp.bfloat16)).astype(jnp.float32)

@jax.custom_vjp
def low_back(v):
    return v

def low_keep(v):
    return (low(v), None)

def low_pass(kept, grad):
    return (grad,)

def back_keep(v):
    return (v, None)

def back_low(kept, grad):
    return (low(grad),)
low.defvjp(low_keep, low_pass)
low_back.defvjp(back_keep, back_low)
EPS_NORM = 1e-06
EPS_HEAD = 1e-05
GATE_NORMALIZER = 16.0
HIGHEST = lax.Precision.HIGHEST

def precise(form, left, right):
    return jnp.einsum(form, left, right, precision=HIGHEST, preferred_element_type=jnp.float32)

def normalize(values, gain, epsilon):
    return values * lax.rsqrt(lax.optimization_barrier(jnp.mean(values * values, axis=-1, keepdims=True)) + epsilon) * gain

def block_mix(memory, pieces):
    queries, key_rows, value_rows, decay_rows = pieces
    cumulative = jnp.cumsum(decay_rows, axis=0)
    size_here = queries.shape[0]
    causal = lax.broadcasted_iota(jnp.int32, (size_here, size_here), 0) >= lax.broadcasted_iota(jnp.int32, (size_here, size_here), 1)
    lifted = queries * jnp.exp(cumulative)
    lowered = key_rows * jnp.exp(-cumulative)
    scores = jnp.where(causal, precise('ik,jk->ij', lifted, lowered), 0.0)
    mixed = precise('ij,jv->iv', scores, value_rows) + precise('ik,kv->iv', lifted, memory)
    last_row = cumulative[-1]
    tails = key_rows * jnp.exp(last_row[None, :] - cumulative)
    carried = jnp.exp(last_row)[:, None] * memory + precise('ik,iv->kv', tails, value_rows)
    return (carried, mixed)

def head_mix(queries, key_rows, value_rows, decay_rows):
    block_count = queries.shape[0] // BLOCK

    def in_blocks(values):
        return values.reshape(block_count, BLOCK, values.shape[-1])
    start_memory = jnp.zeros((queries.shape[-1], value_rows.shape[-1]), jnp.float32)
    _, mixed = lax.scan(jax.checkpoint(block_mix), start_memory, (in_blocks(queries), in_blocks(key_rows), in_blocks(value_rows), in_blocks(decay_rows)))
    return mixed.reshape(queries.shape[0], -1)

def layer(sequence, valid, mixer_gain, project_weight, filter_weight, rank_down, rank_up, decay_bias, gate_weight, head_gain, output_weight, channel_gain, hidden_gate, hidden_up, hidden_down):
    length_here = sequence.shape[0]
    heads = project_weight.shape[1]
    key_width = rank_up.shape[2]
    normed = low(normalize(sequence, mixer_gain, EPS_NORM))
    projected = low(low_back(precise('td,dhc->thc', normed, project_weight)))
    padding = jnp.zeros((CONV - 1,) + projected.shape[1:], jnp.float32)
    extended = jnp.concatenate([padding, projected], axis=0)
    filtered = filter_weight[0] * extended[0:length_here]
    for offset in range(1, CONV):
        filtered = filtered + filter_weight[offset] * extended[offset:offset + length_here]
    convolved = low(jax.nn.silu(filtered))
    queries = convolved[..., :key_width]
    key_rows = convolved[..., key_width:2 * key_width]
    value_rows = convolved[..., 2 * key_width:]
    low_rank = low(precise('td,dr->tr', normed, rank_down))
    logit = precise('tr,rhk->thk', low_rank, rank_up) + decay_bias
    decay_rows = jax.nn.log_sigmoid(logit) / GATE_NORMALIZER
    head_out = jax.vmap(head_mix, in_axes=1, out_axes=1)(queries, key_rows, value_rows, decay_rows) * key_width ** (-0.5)
    head_normed = normalize(head_out, head_gain, EPS_HEAD)
    out_gate = low_back(precise('td,dhv->thv', normed, gate_weight.reshape(gate_weight.shape[0], heads, -1)))
    gated = low(head_normed * jax.nn.silu(out_gate)).reshape(length_here, -1)
    mixer_out = low_back(precise('tv,vd->td', gated, output_weight))
    residual = sequence + mixer_out
    ffn_normed = low(normalize(residual, channel_gain, EPS_NORM))
    gate_rows = low_back(precise('td,df->tf', ffn_normed, hidden_gate))
    up_rows = low_back(precise('td,df->tf', ffn_normed, hidden_up))
    hidden = low(jax.nn.silu(gate_rows) * up_rows)
    result = residual + precise('tf,fd->td', hidden, hidden_down)
    return jnp.where(valid[:, None], result, 0.0)

def reference(tokens, lengths, mixer_gain, project_weight, filter_weight, rank_down, rank_up, decay_bias, gate_weight, head_gain, output_weight, channel_gain, hidden_gate, hidden_up, hidden_down, cotangent):
    weights = tuple((member.astype(jnp.float32) for member in (mixer_gain, project_weight, filter_weight, rank_down, rank_up, decay_bias, gate_weight, head_gain, output_weight, channel_gain, hidden_gate, hidden_up, hidden_down)))
    positions = lax.broadcasted_iota(jnp.int32, (LENGTH,), 0)

    def per_sequence(totals, inputs):
        sequence, length_one, grad_rows = inputs
        valid = positions < length_one

        def forward(sequence_in, *params):
            return layer(sequence_in, valid, *params)
        result, pull = jax.vjp(forward, sequence, *weights)
        grads = pull(grad_rows)
        totals = tuple((running + added for running, added in zip(totals, grads[1:])))
        return (totals, (result, grads[0]))
    start_totals = tuple((jnp.zeros_like(member) for member in weights))
    totals, (results, token_grads) = lax.scan(per_sequence, start_totals, (jnp.moveaxis(tokens.astype(jnp.float32), 1, 0), lengths.astype(jnp.int32), jnp.moveaxis(cotangent.astype(jnp.float32), 1, 0)))
    output = jnp.moveaxis(results, 0, 1).astype(jnp.bfloat16)
    tokens_grad = jnp.moveaxis(token_grads, 0, 1)
    return (output, tokens_grad, totals[0], totals[1], totals[2], totals[3], totals[4], totals[5], totals[6], totals[7], totals[8], totals[9], totals[10], totals[11], totals[12])
```

```python
import functools

import jax
import jax.numpy as jnp
from jax import lax
from jax.experimental import pallas as pl
from jax.experimental.pallas import tpu as pltpu
from jax.sharding import PartitionSpec as P

CONV = 4
EDGE = CONV - 1
CHUNK = 128
STEP = 256
EPS_NORM = 1e-06
EPS_HEAD = 1e-05
GATE_NORMALIZER = 16.0
HIGHEST = lax.Precision.HIGHEST
BF16 = jnp.bfloat16
F32 = jnp.float32
VMEM_LIMIT = 56 * 2**20


def mm(left, right):
    return lax.dot_general(left, right, (((1,), (0,)), ((), ())), preferred_element_type=F32)


def mm_nt(left, right):
    return lax.dot_general(left, right, (((1,), (1,)), ((), ())), preferred_element_type=F32)


def mm_tn(left, right):
    return lax.dot_general(left, right, (((0,), (0,)), ((), ())), preferred_element_type=F32)


def sigmoid(values):
    return 1.0 / (1.0 + jnp.exp(-values))


def whole(shape):
    return pl.BlockSpec(shape, lambda *_: (0,) * len(shape))


def rows_of(size, width):
    return pl.BlockSpec((size, width), lambda i, *_: (i, 0))


def call(body, grid, in_specs, out_specs, out_shape, scratch, flops, moved, prefetch=0):
    return pl.pallas_call(
        body,
        grid_spec=pltpu.PrefetchScalarGridSpec(
            num_scalar_prefetch=prefetch,
            grid=grid,
            in_specs=in_specs,
            out_specs=out_specs,
            scratch_shapes=scratch,
        ),
        out_shape=out_shape,
        compiler_params=pltpu.CompilerParams(
            dimension_semantics=("arbitrary",), vmem_limit_bytes=VMEM_LIMIT
        ),
        cost_estimate=pl.CostEstimate(flops=flops, bytes_accessed=moved, transcendentals=0),
    )


def shape_of(shape, dtype):
    return jax.ShapeDtypeStruct(shape, dtype)


def project_body(tok, gain, w_proj, w_gate, w_rank, normed, projected, out_gate, low_rank):
    rows = tok[...].astype(F32)
    inverse = lax.rsqrt(jnp.mean(rows * rows, axis=-1, keepdims=True) + EPS_NORM)
    rounded = (rows * inverse * gain[...]).astype(BF16)
    normed[...] = rounded
    projected[...] = mm(rounded, w_proj[...]).astype(BF16)
    out_gate[...] = mm(rounded, w_gate[...]).astype(BF16)
    low_rank[...] = mm(rounded, w_rank[...]).astype(BF16)


def project(tok, gain, w_proj, w_gate, w_rank):
    length, width = tok.shape
    c3, dv, rank = w_proj.shape[1], w_gate.shape[1], w_rank.shape[1]
    return call(
        project_body,
        (length // STEP,),
        [
            rows_of(STEP, width),
            whole((1, width)),
            whole((width, c3)),
            whole((width, dv)),
            whole((width, rank)),
        ],
        [rows_of(STEP, width), rows_of(STEP, c3), rows_of(STEP, dv), rows_of(STEP, rank)],
        [
            shape_of((length, width), BF16),
            shape_of((length, c3), BF16),
            shape_of((length, dv), BF16),
            shape_of((length, rank), BF16),
        ],
        [],
        2 * length * width * (c3 + dv + rank),
        length * (2 * width + c3 + dv) * 2 + width * (c3 + dv) * 2,
    )(tok, gain, w_proj, w_gate, w_rank)


def triangle(lower):
    row = lax.broadcasted_iota(jnp.int32, (CHUNK, CHUNK), 0)
    column = lax.broadcasted_iota(jnp.int32, (CHUNK, CHUNK), 1)
    return row >= column if lower else row <= column


def running_sum(values, lower):
    ones = triangle(lower).astype(F32)
    return lax.dot_general(
        ones, values, (((1,), (0,)), ((), ())), precision=HIGHEST, preferred_element_type=F32
    )


def filter_rows(buffer, taps, count):
    total = taps[0:1, :] * buffer[pl.ds(8 - EDGE, count), :]
    for offset in range(1, CONV):
        total = total + taps[offset : offset + 1, :] * buffer[pl.ds(8 - EDGE + offset, count), :]
    return total


def forward_body(
    projected, halo, low_rank, taps_in, rank_up, bias,
    head_local, query_profile, cumulative, states, before, end_state, total_decay,
    extended, memory, preceding,
):
    step = pl.program_id(0)

    @pl.when(step == 0)
    def _():
        extended[0:8, :] = halo[...]
        memory[...] = jnp.zeros_like(memory)
        preceding[...] = jnp.zeros_like(preceding)

    @pl.when(step > 0)
    def _():
        extended[0:8, :] = extended[STEP : STEP + 8, :]

    extended[8 : 8 + STEP, :] = projected[...].astype(F32)
    filtered = filter_rows(extended, taps_in[...], STEP)
    convolved = (filtered * sigmoid(filtered)).astype(BF16)
    logit = mm(low_rank[...], rank_up[...]) + bias[...]
    decay = (jnp.minimum(logit, 0.0) - jnp.log1p(jnp.exp(-jnp.abs(logit)))) / GATE_NORMALIZER
    width = rank_up.shape[1]
    causal = triangle(True)
    for part in range(STEP // CHUNK):
        rows = slice(part * CHUNK, (part + 1) * CHUNK)
        queries = convolved[rows, :width].astype(F32)
        keys = convolved[rows, width : 2 * width].astype(F32)
        values = convolved[rows, 2 * width :]
        total = running_sum(decay[rows], True)
        middle, last = total[CHUNK // 2 - 1 : CHUNK // 2], total[CHUNK - 1 : CHUNK]
        lifted = (queries * jnp.exp(total - middle)).astype(BF16)
        lowered = (keys * jnp.exp(middle - total)).astype(BF16)
        scores = jnp.where(causal, mm_nt(lifted, lowered), 0.0).astype(BF16)
        entry = memory[...]
        entry_low = entry.astype(BF16)
        states[part] = entry_low
        profile = queries * jnp.exp(total)
        head_local[rows, :] = mm(scores, values) + mm_nt(profile.astype(BF16), entry_low)
        query_profile[rows, :] = (profile * jnp.exp(preceding[...])).astype(BF16)
        cumulative[rows, :] = total
        tails = (keys * jnp.exp(last - total)).astype(BF16)
        memory[...] = entry * jnp.exp(last) + mm_tn(values, tails)
        before[pl.ds(step * (STEP // CHUNK) + part, 1), :] = preceding[...]
        preceding[...] = preceding[...] + last
    end_state[...] = memory[...]
    total_decay[...] = preceding[...]


def forward_mix(projected, halo, low_rank, taps, rank_up, bias, dv):
    length, c3 = projected.shape
    rank, dk = rank_up.shape
    chunks = length // CHUNK
    per_step = STEP // CHUNK
    return call(
        forward_body,
        (length // STEP,),
        [
            rows_of(STEP, c3),
            whole((8, c3)),
            rows_of(STEP, rank),
            whole(taps.shape),
            whole((rank, dk)),
            whole((1, dk)),
        ],
        [
            rows_of(STEP, dv),
            rows_of(STEP, dk),
            rows_of(STEP, dk),
            pl.BlockSpec((per_step, dv, dk), lambda i: (i, 0, 0)),
            whole((chunks, dk)),
            whole((dv, dk)),
            whole((1, dk)),
        ],
        [
            shape_of((length, dv), F32),
            shape_of((length, dk), BF16),
            shape_of((length, dk), F32),
            shape_of((chunks, dv, dk), BF16),
            shape_of((chunks, dk), F32),
            shape_of((dv, dk), F32),
            shape_of((1, dk), F32),
        ],
        [
            pltpu.VMEM((STEP + 8, c3), F32),
            pltpu.VMEM((dv, dk), F32),
            pltpu.VMEM((1, dk), F32),
        ],
        2 * length * (4 * dk * dv + dk * dk) * 8,
        length * (c3 * 2 + dv * 4 + dk * 6) + chunks * dv * dk * 2,
    )(projected, halo, low_rank, taps, rank_up, bias)


def head_rows(head_local, query_profile, entering, scale):
    return (head_local + mm_nt(query_profile, entering.astype(BF16))) * scale


def gate_body(head_local, query_profile, entering, out_gate, gain, gated):
    scale = query_profile.shape[1] ** (-0.5)
    head = head_rows(head_local[...], query_profile[...], entering[...], scale)
    inverse = lax.rsqrt(jnp.mean(head * head, axis=-1, keepdims=True) + EPS_HEAD)
    logits = out_gate[...].astype(F32)
    gated[...] = (head * inverse * gain[...] * (logits * sigmoid(logits))).astype(BF16)


def gate(head_local, query_profile, entering, out_gate, gain):
    length, dv = head_local.shape
    dk = query_profile.shape[1]
    return call(
        gate_body,
        (length // STEP,),
        [
            rows_of(STEP, dv),
            rows_of(STEP, dk),
            whole((dv, dk)),
            rows_of(STEP, dv),
            whole((1, dv)),
        ],
        rows_of(STEP, dv),
        shape_of((length, dv), BF16),
        [],
        2 * length * dk * dv * 4,
        length * (dv * 8 + dk * 2),
    )(head_local, query_profile, entering, out_gate, gain)


def ffn_body(
    mine, g0, g1, g2, g3, w0, w1, w2, w3, tok, gain, w_gate, w_up, w_down, upstream,
    normed, hidden, grad_gate, grad_up, out_part, grad_part, own_residual, gain_grad,
):
    del mine
    step = pl.program_id(0)
    mixed = mm(g0[...], w0[...]) + mm(g1[...], w1[...])
    mixed = mixed + mm(g2[...], w2[...]) + mm(g3[...], w3[...])
    residual = tok[...].astype(F32) + mixed

    @pl.when(step == 0)
    def _():
        own_residual[...] = residual
        gain_grad[...] = jnp.zeros_like(gain_grad)

    inverse = lax.rsqrt(jnp.mean(residual * residual, axis=-1, keepdims=True) + EPS_NORM)
    unit = residual * inverse
    rounded = (unit * gain[...]).astype(BF16)
    normed[...] = rounded
    gate_rows = mm(rounded, w_gate[...])
    up_rows = mm(rounded, w_up[...])
    share = sigmoid(gate_rows)
    swished = gate_rows * share
    hidden_rows = (swished * up_rows).astype(BF16)
    hidden[...] = hidden_rows
    out_part[0] = mm(hidden_rows, w_down[...]).astype(BF16)
    grad_hidden = mm_nt(upstream[...], w_down[...])
    slope = share * (1.0 + gate_rows * (1.0 - share))
    grad_gate_rows = (grad_hidden * up_rows * slope).astype(BF16)
    grad_up_rows = (grad_hidden * swished).astype(BF16)
    grad_gate[...] = grad_gate_rows
    grad_up[...] = grad_up_rows
    grad_rows = mm_nt(grad_gate_rows, w_gate[...]) + mm_nt(grad_up_rows, w_up[...])
    grad_part[0] = grad_rows.astype(BF16)
    gain_grad[...] += jnp.sum(grad_rows * unit, axis=0, keepdims=True)


def feed_forward(mine, gathered, weights, tok, gain, w_gate, w_up, w_down, upstream):
    length, width = tok.shape
    dv, units = gathered[0].shape[1], w_gate.shape[1]
    quarter = length // 4

    def natural(size, columns):
        return pl.BlockSpec((size, columns), lambda i, m: (i ^ m[0], 0))

    slot = pl.BlockSpec((1, quarter, width), lambda i, m: (i, 0, 0))
    return call(
        ffn_body,
        (4,),
        [natural(quarter, dv)] * 4
        + [whole((dv, width))] * 4
        + [
            natural(quarter, width),
            whole((1, width)),
            whole((width, units)),
            whole((width, units)),
            whole((units, width)),
            natural(quarter, width),
        ],
        [
            natural(quarter, width),
            natural(quarter, units),
            natural(quarter, units),
            natural(quarter, units),
            slot,
            slot,
            whole((quarter, width)),
            whole((1, width)),
        ],
        [
            shape_of((length, width), BF16),
            shape_of((length, units), BF16),
            shape_of((length, units), BF16),
            shape_of((length, units), BF16),
            shape_of((4, quarter, width), BF16),
            shape_of((4, quarter, width), BF16),
            shape_of((quarter, width), F32),
            shape_of((1, width), F32),
        ],
        [],
        2 * length * width * (4 * dv + 6 * units),
        length * (6 * width + 3 * units) * 2 + 3 * units * width * 2 + 4 * dv * width * 2,
        prefetch=1,
    )(mine, *gathered, *weights, tok, gain, w_gate, w_up, w_down, upstream)


def ungate_body(
    mine, r0, r1, r2, r3, head_local, query_profile, entering, out_gate, gain,
    grad_out_gate, grad_head, state_grad, gain_grad,
):
    step = pl.program_id(0)

    @pl.when(step == 0)
    def _():
        state_grad[...] = jnp.zeros_like(state_grad)
        gain_grad[...] = jnp.zeros_like(gain_grad)

    source = step ^ mine[0]
    grad_gated = jnp.where(
        source < 2,
        jnp.where(source == 0, r0[...], r1[...]),
        jnp.where(source == 2, r2[...], r3[...]),
    ).astype(F32)
    scale = query_profile.shape[1] ** (-0.5)
    head = head_rows(head_local[...], query_profile[...], entering[...], scale)
    inverse = lax.rsqrt(jnp.mean(head * head, axis=-1, keepdims=True) + EPS_HEAD)
    unit = head * inverse
    logits = out_gate[...].astype(F32)
    share = sigmoid(logits)
    slope = share * (1.0 + logits * (1.0 - share))
    grad_out_gate[...] = (grad_gated * unit * gain[...] * slope).astype(BF16)
    grad_normed = grad_gated * (logits * share)
    gain_grad[...] += jnp.sum(grad_normed * unit, axis=0, keepdims=True)
    scaled = grad_normed * gain[...]
    through = inverse * (scaled - unit * jnp.mean(scaled * unit, axis=-1, keepdims=True))
    rounded = (through * scale).astype(BF16)
    grad_head[...] = rounded
    state_grad[...] += mm_tn(rounded, query_profile[...])


def ungate(mine, received, head_local, query_profile, entering, out_gate, gain):
    length, dv = head_local.shape
    dk = query_profile.shape[1]
    quarter = length // 4
    return call(
        ungate_body,
        (4,),
        [whole((quarter, dv))] * 4
        + [
            rows_of(quarter, dv),
            rows_of(quarter, dk),
            whole((dv, dk)),
            rows_of(quarter, dv),
            whole((1, dv)),
        ],
        [rows_of(quarter, dv), rows_of(quarter, dv), whole((dv, dk)), whole((1, dv))],
        [
            shape_of((length, dv), BF16),
            shape_of((length, dv), BF16),
            shape_of((dv, dk), F32),
            shape_of((1, dv), F32),
        ],
        [],
        2 * length * dk * dv * 8,
        length * (dv * 12 + dk * 2),
        prefetch=1,
    )(mine, *received, head_local, query_profile, entering, out_gate, gain)


def backward_body(
    projected, earlier, halo, low_rank, taps_in, rank_up, bias, cumulative, states, before,
    entering, leaving, grad_head,
    grad_projected, grad_low_rank, first_rows, filter_grad, rank_up_grad, bias_grad,
    extended, grad_extended, upstream,
):
    back = pl.program_id(0)
    step = pl.num_programs(0) - 1 - back
    per_step = STEP // CHUNK

    @pl.when(back == 0)
    def _():
        upstream[...] = leaving[...]
        grad_extended[STEP : STEP + 8, :] = jnp.zeros_like(grad_extended[STEP : STEP + 8, :])
        filter_grad[...] = jnp.zeros_like(filter_grad)
        rank_up_grad[...] = jnp.zeros_like(rank_up_grad)
        bias_grad[...] = jnp.zeros_like(bias_grad)

    @pl.when(back > 0)
    def _():
        grad_extended[STEP : STEP + 8, :] = grad_extended[0:8, :]

    @pl.when(step == 0)
    def _():
        extended[0:8, :] = halo[...]

    @pl.when(step > 0)
    def _():
        extended[0:8, :] = earlier[...].astype(F32)[8:16, :]

    extended[8 : 8 + STEP, :] = projected[...].astype(F32)
    taps = taps_in[...]
    filtered = filter_rows(extended, taps, STEP)
    share = sigmoid(filtered)
    convolved = (filtered * share).astype(BF16)
    slope = share * (1.0 + filtered * (1.0 - share))
    logit = mm(low_rank[...], rank_up[...]) + bias[...]
    width = rank_up.shape[1]
    causal = triangle(True)
    logit_grads = [None] * per_step
    for part in reversed(range(per_step)):
        rows = slice(part * CHUNK, (part + 1) * CHUNK)
        queries = convolved[rows, :width].astype(F32)
        keys = convolved[rows, width : 2 * width].astype(F32)
        values = convolved[rows, 2 * width :]
        grad_rows = grad_head[rows, :]
        total = cumulative[rows, :]
        middle, last = total[CHUNK // 2 - 1 : CHUNK // 2], total[CHUNK - 1 : CHUNK]
        lift, lower = jnp.exp(total - middle), jnp.exp(middle - total)
        inner, outer, whole_decay = jnp.exp(total), jnp.exp(last - total), jnp.exp(last)
        lifted, lowered = (queries * lift).astype(BF16), (keys * lower).astype(BF16)
        profile, tails = (queries * inner).astype(BF16), (keys * outer).astype(BF16)
        previous = before[pl.ds(step * per_step + part, 1), :]
        state = states[part].astype(F32) + entering[...] * jnp.exp(previous)
        scores = jnp.where(causal, mm_nt(lifted, lowered), 0.0).astype(BF16)
        grad_scores = jnp.where(causal, mm_nt(grad_rows, values), 0.0).astype(BF16)
        later = upstream[...]
        later_low = later.astype(BF16)
        grad_values = mm_tn(scores, grad_rows) + mm_nt(tails, later_low)
        grad_lifted = mm(grad_scores, lowered)
        grad_lowered = mm_tn(grad_scores, lifted)
        grad_profile = mm(grad_rows, state.astype(BF16))
        grad_tails = mm(values, later_low)
        upstream[...] = later * whole_decay + mm_tn(grad_rows, profile)
        tail_terms = tails.astype(F32) * grad_tails
        grad_total = (
            lifted.astype(F32) * grad_lifted
            - lowered.astype(F32) * grad_lowered
            + profile.astype(F32) * grad_profile
            - tail_terms
        )
        grad_last = jnp.sum(tail_terms, axis=0, keepdims=True) + whole_decay * jnp.sum(
            later * state, axis=0, keepdims=True
        )
        grad_decay = running_sum(grad_total, False) + grad_last
        logit_grads[part] = grad_decay / GATE_NORMALIZER * sigmoid(-logit[rows])
        grad_extended[rows, :width] = (grad_lifted * lift + grad_profile * inner) * slope[rows, :width]
        grad_extended[rows, width : 2 * width] = (
            grad_lowered * lower + grad_tails * outer
        ) * slope[rows, width : 2 * width]
        grad_extended[rows, 2 * width :] = grad_values * slope[rows, 2 * width :]
    logit_grad = jnp.concatenate(logit_grads, axis=0)
    logit_low = logit_grad.astype(BF16)
    bias_grad[...] += jnp.sum(logit_grad, axis=0, keepdims=True)
    rank_up_grad[...] += mm_tn(low_rank[...], logit_low)
    grad_low_rank[...] = mm_nt(logit_low, rank_up[...]).astype(BF16)
    total_rows = taps[EDGE : EDGE + 1, :] * grad_extended[0:STEP, :]
    for offset in range(EDGE):
        total_rows = total_rows + taps[offset : offset + 1, :] * grad_extended[
            pl.ds(EDGE - offset, STEP), :
        ]
    grad_projected[...] = total_rows.astype(BF16)
    grad_filtered = grad_extended[0:STEP, :]
    for offset in range(CONV):
        filter_grad[offset : offset + 1, :] += jnp.sum(
            grad_filtered * extended[pl.ds(8 - EDGE + offset, STEP), :], axis=0, keepdims=True
        )
    first_rows[...] = grad_extended[0:8, :]


def backward_mix(
    projected, halo, low_rank, taps, rank_up, bias, cumulative, states, before, entering,
    leaving, grad_head,
):
    length, c3 = projected.shape
    rank, dk = rank_up.shape
    dv = grad_head.shape[1]
    chunks, per_step, steps = length // CHUNK, STEP // CHUNK, length // STEP

    def reverse(size, width):
        return pl.BlockSpec((size, width), lambda i: (steps - 1 - i, 0))

    return call(
        backward_body,
        (steps,),
        [
            reverse(STEP, c3),
            pl.BlockSpec(
                (16, c3), lambda i: (jnp.maximum((steps - 1 - i) * (STEP // 16) - 1, 0), 0)
            ),
            whole((8, c3)),
            reverse(STEP, rank),
            whole(taps.shape),
            whole((rank, dk)),
            whole((1, dk)),
            reverse(STEP, dk),
            pl.BlockSpec((per_step, dv, dk), lambda i: (steps - 1 - i, 0, 0)),
            whole((chunks, dk)),
            whole((dv, dk)),
            whole((dv, dk)),
            reverse(STEP, dv),
        ],
        [
            reverse(STEP, c3),
            reverse(STEP, rank),
            whole((8, c3)),
            whole(taps.shape),
            whole((rank, dk)),
            whole((1, dk)),
        ],
        [
            shape_of((length, c3), BF16),
            shape_of((length, rank), BF16),
            shape_of((8, c3), F32),
            shape_of(taps.shape, F32),
            shape_of((rank, dk), F32),
            shape_of((1, dk), F32),
        ],
        [
            pltpu.VMEM((STEP + 8, c3), F32),
            pltpu.VMEM((STEP + 8, c3), F32),
            pltpu.VMEM((dv, dk), F32),
        ],
        2 * length * (12 * dk * dv) * 8,
        length * (c3 * 4 + dk * 4 + dv * 2) + chunks * dv * dk * 2,
    )(
        projected, projected, halo, low_rank, taps, rank_up, bias, cumulative, states, before,
        entering, leaving, grad_head,
    )


def input_grad_body(
    mine, grad_projected, grad_out_gate, grad_low_rank, w_proj, w_gate, w_rank, normed,
    parts, gain_grad,
):
    del mine

    @pl.when(pl.program_id(0) == 0)
    def _():
        gain_grad[...] = jnp.zeros_like(gain_grad)

    total = mm_nt(grad_projected[...], w_proj[...]) + mm_nt(grad_out_gate[...], w_gate[...])
    total = total + mm_nt(grad_low_rank[...], w_rank[...])
    parts[0] = total.astype(BF16)
    gain_grad[...] += jnp.sum(total * normed[...].astype(F32), axis=0, keepdims=True)


def input_grad(mine, grad_projected, grad_out_gate, grad_low_rank, w_proj, w_gate, w_rank, normed):
    length, width = normed.shape
    c3, dv, rank = w_proj.shape[1], w_gate.shape[1], w_rank.shape[1]
    quarter = length // 4

    def natural(columns):
        return pl.BlockSpec((quarter, columns), lambda i, m: (i ^ m[0], 0))

    return call(
        input_grad_body,
        (4,),
        [
            natural(c3),
            natural(dv),
            natural(rank),
            whole((width, c3)),
            whole((width, dv)),
            whole((width, rank)),
            natural(width),
        ],
        [pl.BlockSpec((1, quarter, width), lambda i, m: (i, 0, 0)), whole((1, width))],
        [shape_of((4, quarter, width), BF16), shape_of((1, width), F32)],
        [],
        2 * length * width * (c3 + dv + rank),
        length * (2 * width + c3 + dv) * 2 + width * (c3 + dv) * 2,
        prefetch=1,
    )(mine, grad_projected, grad_out_gate, grad_low_rank, w_proj, w_gate, w_rank, normed)


ACROSS = [(i, i ^ 1) for i in range(4)]
DOWN = [(i, i ^ 2) for i in range(4)]
OPPOSITE = [(i, i ^ 3) for i in range(4)]


def gather_relative(block):
    half = block.shape[0] // 2
    across = lax.ppermute(block, "mp", ACROSS)
    down = lax.ppermute(block, "mp", DOWN)
    first = lax.ppermute(across[:half], "mp", DOWN)
    second = lax.ppermute(down[half:], "mp", ACROSS)
    return [block, across, down, jnp.concatenate([first, second], axis=0)]


def scatter_relative(parts):
    half = parts.shape[1] // 2
    via_across = lax.ppermute(parts[3, :half], "mp", ACROSS)
    via_down = lax.ppermute(parts[3, half:], "mp", DOWN)
    across_a = lax.ppermute(parts[1, :half], "mp", ACROSS)
    down_b = lax.ppermute(parts[2, half:], "mp", DOWN)
    across_b = lax.ppermute(parts[1, half:] + via_down, "mp", ACROSS)
    down_a = lax.ppermute(parts[2, :half] + via_across, "mp", DOWN)
    across = jnp.concatenate([across_a, across_b], axis=0).astype(F32)
    down = jnp.concatenate([down_a, down_b], axis=0).astype(F32)
    return parts[0].astype(F32) + across + down


def passed_along(block, axis, distance):
    devices = range(lax.axis_size(axis))
    route = [(i - distance, i) for i in devices if i - distance in devices]
    return lax.ppermute(block, axis, route)


def chain_states(decay, state, backward):
    count, mine = lax.axis_size("seq"), lax.axis_index("seq")
    if count == 2:
        return passed_along(state, "seq", -1 if backward else 1)
    decays, states = lax.all_gather(decay, "seq"), lax.all_gather(state, "seq")
    if backward:
        decays, states, mine = decays[::-1], states[::-1], count - 1 - mine

    def hop(position, subtotal):
        longer = subtotal * jnp.exp(decays[position]) + states[position]
        return jnp.where(position < mine, longer, subtotal)

    return lax.fori_loop(0, count - 1, hop, jnp.zeros_like(state))


def sum_shards(grad):
    if lax.axis_size("seq") != 2 or lax.axis_size("dp") != 4:
        total = lax.psum_scatter(grad, ("seq", "dp"), scatter_dimension=0, tiled=True)
        return total[0].astype(F32)
    side, place = lax.axis_index("seq"), lax.axis_index("dp")
    other = lax.dynamic_slice_in_dim(grad, (1 - side) * 4, 4, 0)
    kept = lax.dynamic_slice_in_dim(grad, side * 4, 4, 0)
    kept = kept + lax.ppermute(other, "seq", [(0, 1), (1, 0)])
    upward, downward = None, None
    for turn in range(1, 4):
        above = lax.dynamic_index_in_dim(kept, jnp.minimum(place + 4 - turn, 3), 0, False)
        below = lax.dynamic_index_in_dim(kept, jnp.maximum(place - 4 + turn, 0), 0, False)
        if turn > 1:
            above, below = above + upward, below + downward
        upward = lax.ppermute(above, "dp", [(i, i + 1) for i in range(turn)])
        downward = lax.ppermute(below, "dp", [(3 - i, 2 - i) for i in range(turn)])
    mine = lax.dynamic_index_in_dim(kept, place, 0, False)
    return mine.astype(F32) + upward.astype(F32) + downward.astype(F32)


def sum_over(values, axes):
    for axis in axes:
        count = lax.axis_size(axis)
        if count & (count - 1) or count > 4:
            values = lax.psum(values, axis)
            continue
        distance = 1
        while distance < count:
            values = values + lax.ppermute(values, axis, [(i, i ^ distance) for i in range(count)])
            distance *= 2
    return values


def on_device(
    tokens, lengths, mixer_gain, project_weight, filter_weight, rank_down, rank_up, decay_bias,
    gate_weight, head_gain, output_weight, channel_gain, hidden_gate, hidden_up, hidden_down,
    cotangent,
):
    length, sequences, width = tokens.shape
    shards = lax.axis_size("seq") * lax.axis_size("dp")
    shard = lax.axis_index("seq") * lax.axis_size("dp") + lax.axis_index("dp")
    me = lax.axis_index("mp")
    mine = me.astype(jnp.int32).reshape(1)
    own_rows = length // lax.axis_size("mp")
    w_proj = project_weight[:, 0]
    taps = filter_weight[:, 0].astype(F32)
    rank_up_here = rank_up[:, 0]
    bias = decay_bias.astype(F32)
    mixer_gain_f = mixer_gain.astype(F32)[None]
    channel_gain_f = channel_gain.astype(F32)[None]
    head_gain_f = head_gain.astype(F32)[None]
    dv = gate_weight.shape[1]
    positions = lax.axis_index("seq") * length + lax.broadcasted_iota(jnp.int32, (length, 1), 0)

    edge_tokens = passed_along(tokens[length - EDGE :], "seq", 1)
    edge_f = edge_tokens.astype(F32)
    edge_inverse = lax.rsqrt(jnp.mean(edge_f * edge_f, axis=-1, keepdims=True) + EPS_NORM)
    edge_normed = (edge_f * edge_inverse * mixer_gain_f).astype(BF16)
    edge_projected = jnp.einsum(
        "psd,dc->psc", edge_normed, w_proj, preferred_element_type=F32
    ).astype(BF16)
    halos = jnp.pad(edge_projected.astype(F32), ((8 - EDGE, 0), (0, 0), (0, 0)))

    output_weights = gather_relative(output_weight)
    turns = range(sequences)
    toks = [tokens[:, s] for s in turns]
    masks = [positions < lengths[s] for s in turns]
    upstreams = [jnp.where(masks[s], cotangent[:, s], jnp.zeros((), BF16)) for s in turns]
    fronts = [project(toks[s], mixer_gain_f, w_proj, gate_weight, rank_down) for s in turns]
    mixes = []
    for s in turns:
        _, projected, _, low_rank = fronts[s]
        mixes.append(forward_mix(projected, halos[:, s], low_rank, taps, rank_up_here, bias, dv))
    enterings = [chain_states(mixes[s][6], mixes[s][5], False) for s in turns]
    gateds, gathered = [], []
    for s in turns:
        gateds.append(gate(mixes[s][0], mixes[s][1], enterings[s], fronts[s][2], head_gain_f))
        gathered.append(gather_relative(gateds[s]))
    ffns = [
        feed_forward(
            mine, gathered[s], output_weights, toks[s], channel_gain_f, hidden_gate, hidden_up,
            hidden_down, upstreams[s],
        )
        for s in turns
    ]

    grad_residuals, grad_mixers, backs = [], [], []
    for s in turns:
        residual = ffns[s][6]
        grad_normed = scatter_relative(ffns[s][5])
        inverse = lax.rsqrt(jnp.mean(residual * residual, axis=-1, keepdims=True) + EPS_NORM)
        unit = residual * inverse
        scaled = grad_normed * channel_gain_f
        through = inverse * (scaled - unit * jnp.mean(scaled * unit, axis=-1, keepdims=True))
        own_upstream = lax.dynamic_slice_in_dim(upstreams[s], me * own_rows, own_rows, 0)
        grad_residual = own_upstream.astype(F32) + through
        grad_mixer = grad_residual.astype(BF16)
        grad_residuals.append(grad_residual)
        grad_mixers.append(grad_mixer)
        pieces = [mm_nt(grad_mixer, weight).astype(BF16) for weight in output_weights]
        received = [
            pieces[0],
            lax.ppermute(pieces[1], "mp", ACROSS),
            lax.ppermute(pieces[2], "mp", DOWN),
            lax.ppermute(pieces[3], "mp", OPPOSITE),
        ]
        grad_out_gate, grad_head, state_grad, head_gain_part = ungate(
            mine, received, mixes[s][0], mixes[s][1], enterings[s], fronts[s][2], head_gain_f
        )
        leaving = chain_states(mixes[s][6], state_grad, True)
        grads = backward_mix(
            fronts[s][1], halos[:, s], fronts[s][3], taps, rank_up_here, bias, mixes[s][2],
            mixes[s][3], mixes[s][4], enterings[s], leaving, grad_head,
        )
        first = grads[2]
        edge = jnp.concatenate(
            [
                sum(taps[j : j + 1] * first[i - j : i - j + 1] for j in range(i + 1))
                for i in range(EDGE)
            ],
            axis=0,
        )
        edge = passed_along(edge, "seq", -1)
        grad_projected = grads[0]
        tail = grad_projected[length - 16 :].astype(F32) + jnp.pad(edge, ((16 - EDGE, 0), (0, 0)))
        grad_projected = lax.dynamic_update_slice_in_dim(
            grad_projected, tail.astype(BF16), length - 16, 0
        )
        parts, mixer_gain_part = input_grad(
            mine, grad_projected, grad_out_gate, grads[1], w_proj, gate_weight, rank_down,
            fronts[s][0],
        )
        backs.append((grad_projected, grad_out_gate, grads, head_gain_part, parts, mixer_gain_part))

    def weight_grad(lefts, rights):
        return sum(mm_tn(left, right) for left, right in zip(lefts, rights))

    def in_shards(grad):
        return grad.astype(BF16).reshape(shards, width // shards, grad.shape[-1])

    hidden_grads = jnp.stack(
        [
            in_shards(weight_grad([f[0] for f in ffns], [f[2] for f in ffns])),
            in_shards(weight_grad([f[0] for f in ffns], [f[3] for f in ffns])),
            in_shards(weight_grad(upstreams, [f[1] for f in ffns])),
        ],
        axis=1,
    )
    hidden_grads = sum_shards(hidden_grads)

    output_parts = []
    for slot in range(4):
        own_gated = [
            lax.dynamic_slice_in_dim(gathered[s][slot], me * own_rows, own_rows, 0) for s in turns
        ]
        output_parts.append(weight_grad(grad_mixers, own_gated).astype(BF16))
    output_grad = scatter_relative(jnp.stack(output_parts))
    normed_rows = [front[0] for front in fronts]
    mixer_grads = jnp.concatenate(
        [
            in_shards(weight_grad(normed_rows, [b[0] for b in backs])),
            in_shards(weight_grad(normed_rows, [b[1] for b in backs])),
            in_shards(output_grad),
        ],
        axis=-1,
    )
    mixer_grads = sum_shards(mixer_grads)
    c3 = w_proj.shape[1]

    rank_down_part = weight_grad(normed_rows, [b[2][1] for b in backs])
    shared = [
        sum(b[5] for b in backs)[0] / mixer_gain_f[0],
        sum(f[7] for f in ffns)[0],
        sum(b[3] for b in backs)[0],
        rank_down_part.reshape(-1),
    ]
    local = [
        sum(b[2][3] for b in backs).reshape(-1),
        sum(b[2][4] for b in backs).reshape(-1),
        sum(b[2][5] for b in backs).reshape(-1),
    ]
    shared_size = sum(part.shape[0] for part in shared)
    small = sum_over(jnp.concatenate(shared + local), ("seq", "dp"))
    shared_sum = sum_over(small[:shared_size], ("mp",))

    def take(values, start, shape):
        count = 1
        for size in shape:
            count *= size
        return lax.slice_in_dim(values, start, start + count).reshape(shape)

    def own(values):
        share = values.shape[-1] // shards
        return lax.dynamic_slice_in_dim(values, shard * share, share, values.ndim - 1)

    mixer_gain_grad = take(shared_sum, 0, (width,))
    channel_gain_grad = take(shared_sum, width, (width,))
    head_gain_grad = take(shared_sum, 2 * width, (dv,))
    rank_down_grad = take(shared_sum, 2 * width + dv, rank_down.shape)
    filter_grad = own(take(small, shared_size, filter_weight.shape))
    start = shared_size + filter_weight.size
    rank_up_grad = own(take(small, start, rank_up.shape))
    decay_bias_grad = own(take(small, start + rank_up.size, decay_bias.shape))

    outputs, token_grads = [], []
    for s in turns:
        ffn_out = scatter_relative(ffns[s][4])
        own_mask = lax.dynamic_slice_in_dim(masks[s], me * own_rows, own_rows, 0)
        outputs.append(jnp.where(own_mask, ffns[s][6] + ffn_out, 0.0).astype(BF16))
        grad_normed = scatter_relative(backs[s][4])
        rows = lax.dynamic_slice_in_dim(toks[s], me * own_rows, own_rows, 0).astype(F32)
        inverse = lax.rsqrt(jnp.mean(rows * rows, axis=-1, keepdims=True) + EPS_NORM)
        unit = rows * inverse
        scaled = grad_normed * mixer_gain_f
        through = inverse * (scaled - unit * jnp.mean(scaled * unit, axis=-1, keepdims=True))
        token_grads.append(grad_residuals[s] + through)
    return (
        jnp.stack(outputs, axis=1),
        jnp.stack(token_grads, axis=1),
        mixer_gain_grad,
        mixer_grads[:, None, :c3],
        filter_grad,
        rank_down_grad,
        rank_up_grad,
        decay_bias_grad,
        mixer_grads[:, c3 : c3 + dv],
        head_gain_grad,
        mixer_grads[:, c3 + dv :].T,
        channel_gain_grad,
        hidden_grads[0],
        hidden_grads[1],
        hidden_grads[2].T,
    )


def solution(mesh):
    in_specs = (
        P("seq", "dp", None),
        P("dp"),
        P(),
        P(None, "mp", None),
        P(None, "mp", None),
        P(),
        P(None, "mp", None),
        P("mp", None),
        P(None, "mp"),
        P(),
        P("mp", None),
        P(),
        P(None, "mp"),
        P(None, "mp"),
        P("mp", None),
        P("seq", "dp", None),
    )
    out_specs = (
        P(("seq", "mp"), "dp", None),
        P(("seq", "mp"), "dp", None),
        P(),
        P(("seq", "dp"), "mp", None),
        P(None, "mp", ("seq", "dp")),
        P(),
        P(None, "mp", ("seq", "dp")),
        P("mp", ("seq", "dp")),
        P(("seq", "dp"), "mp"),
        P(),
        P("mp", ("seq", "dp")),
        P(),
        P(("seq", "dp"), "mp"),
        P(("seq", "dp"), "mp"),
        P("mp", ("seq", "dp")),
    )
    return jax.shard_map(
        on_device, mesh=mesh, in_specs=in_specs, out_specs=out_specs, check_vma=False
    )
```

```python
import functools

import jax
import jax.numpy as jnp
from jax import lax
from jax.experimental import pallas as pl
from jax.experimental.pallas import tpu as pltpu
from jax.sharding import PartitionSpec as P

CONV = 4
EDGE = CONV - 1
CHUNK = 128
STEP = 256
EPS_NORM = 1e-06
EPS_HEAD = 1e-05
GATE_NORMALIZER = 16.0
HIGHEST = lax.Precision.HIGHEST
BF16 = jnp.bfloat16
F32 = jnp.float32
VMEM_LIMIT = 56 * 2**20


def mm(left, right):
    return lax.dot_general(left, right, (((1,), (0,)), ((), ())), preferred_element_type=F32)


def mm_nt(left, right):
    return lax.dot_general(left, right, (((1,), (1,)), ((), ())), preferred_element_type=F32)


def mm_tn(left, right):
    return lax.dot_general(left, right, (((0,), (0,)), ((), ())), preferred_element_type=F32)


def sigmoid(values):
    return 1.0 / (1.0 + jnp.exp(-values))


def whole(shape):
    return pl.BlockSpec(shape, lambda *_: (0,) * len(shape))


def rows_of(size, width):
    return pl.BlockSpec((size, width), lambda i, *_: (i, 0))


def call(body, grid, in_specs, out_specs, out_shape, scratch, flops, moved, prefetch=0):
    return pl.pallas_call(
        body,
        grid_spec=pltpu.PrefetchScalarGridSpec(
            num_scalar_prefetch=prefetch,
            grid=grid,
            in_specs=in_specs,
            out_specs=out_specs,
            scratch_shapes=scratch,
        ),
        out_shape=out_shape,
        compiler_params=pltpu.CompilerParams(
            dimension_semantics=("arbitrary",), vmem_limit_bytes=VMEM_LIMIT
        ),
        cost_estimate=pl.CostEstimate(flops=flops, bytes_accessed=moved, transcendentals=0),
    )


def shape_of(shape, dtype):
    return jax.ShapeDtypeStruct(shape, dtype)


def project_body(
    places, tok_in, cot_in, gain, w_proj, w_gate, w_rank,
    tok, upstream, normed, projected, out_gate, low_rank,
):
    step = pl.program_id(0)
    sequences, count, _ = tok.shape
    total = sequences * count
    row = lax.broadcasted_iota(jnp.int32, (total, total), 0)
    column = lax.broadcasted_iota(jnp.int32, (total, total), 1)
    source = (row % count) * sequences + row // count
    order = jnp.where(column == source, 1.0, 0.0).astype(BF16)
    rows = mm(order, tok_in[...])
    grads = mm(order, cot_in[...])
    first = places[sequences] + step * count
    position = first + lax.broadcasted_iota(jnp.int32, (count, 1), 0)
    inverse = lax.rsqrt(jnp.mean(rows * rows, axis=-1, keepdims=True) + EPS_NORM)
    rounded = (rows * inverse * gain[...]).astype(BF16)
    projected_rows = mm(rounded, w_proj[...]).astype(BF16)
    gate_rows = mm(rounded, w_gate[...]).astype(BF16)
    rank_rows = mm(rounded, w_rank[...]).astype(BF16)
    for s in range(sequences):
        part = slice(s * count, (s + 1) * count)
        tok[s] = rows[part].astype(BF16)
        upstream[s] = jnp.where(position < places[s], grads[part], 0.0).astype(BF16)
        normed[s] = rounded[part]
        projected[s] = projected_rows[part]
        out_gate[s] = gate_rows[part]
        low_rank[s] = rank_rows[part]


def rows3(sequences, size, width):
    return pl.BlockSpec((sequences, size, width), lambda i, *_: (0, i, 0))


def project(places, tok, cot, sequences, gain, w_proj, w_gate, w_rank):
    length, width = tok.shape[0] // sequences, tok.shape[1]
    c3, dv, rank = w_proj.shape[1], w_gate.shape[1], w_rank.shape[1]
    widths = (width, width, width, c3, dv, rank)
    return call(
        project_body,
        (length // CHUNK,),
        [
            rows_of(CHUNK * sequences, width),
            rows_of(CHUNK * sequences, width),
            whole((1, width)),
            whole((width, c3)),
            whole((width, dv)),
            whole((width, rank)),
        ],
        [rows3(sequences, CHUNK, w) for w in widths],
        [shape_of((sequences, length, w), BF16) for w in widths],
        [],
        2 * sequences * length * width * (c3 + dv + rank + 512),
        sequences * length * (5 * width + c3 + dv) * 2 + width * (c3 + dv) * 2,
        prefetch=1,
    )(places, tok, cot, gain, w_proj, w_gate, w_rank)


def triangle(lower):
    row = lax.broadcasted_iota(jnp.int32, (CHUNK, CHUNK), 0)
    column = lax.broadcasted_iota(jnp.int32, (CHUNK, CHUNK), 1)
    return row >= column if lower else row <= column


def running_sum(values, lower):
    ones = triangle(lower).astype(F32)
    return lax.dot_general(
        ones, values, (((1,), (0,)), ((), ())), precision=HIGHEST, preferred_element_type=F32
    )


def filter_rows(buffer, taps, count):
    total = taps[0:1, :] * buffer[pl.ds(8 - EDGE, count), :]
    for offset in range(1, CONV):
        total = total + taps[offset : offset + 1, :] * buffer[pl.ds(8 - EDGE + offset, count), :]
    return total


def forward_body(
    projected, halo, low_rank, taps_in, rank_up, bias,
    head_local, query_profile, cumulative, states, before, end_state, total_decay,
    extended, memory, preceding,
):
    step = pl.program_id(0)
    sequences = projected.shape[0]

    @pl.when(step == 0)
    def _():
        extended[:, 0:8, :] = halo[...]
        memory[...] = jnp.zeros_like(memory)
        preceding[...] = jnp.zeros_like(preceding)

    @pl.when(step > 0)
    def _():
        extended[:, 0:8, :] = extended[:, STEP : STEP + 8, :]

    width = rank_up.shape[1]
    causal = triangle(True)
    for s in range(sequences):
        extended[s, 8 : 8 + STEP, :] = projected[s].astype(F32)
        filtered = filter_rows(extended.at[s], taps_in[...], STEP)
        convolved = (filtered * sigmoid(filtered)).astype(BF16)
        logit = mm(low_rank[s], rank_up[...]) + bias[...]
        decay = (jnp.minimum(logit, 0.0) - jnp.log1p(jnp.exp(-jnp.abs(logit)))) / GATE_NORMALIZER
        for part in range(STEP // CHUNK):
            rows = slice(part * CHUNK, (part + 1) * CHUNK)
            queries = convolved[rows, :width].astype(F32)
            keys = convolved[rows, width : 2 * width].astype(F32)
            values = convolved[rows, 2 * width :]
            total = running_sum(decay[rows], True)
            middle, last = total[CHUNK // 2 - 1 : CHUNK // 2], total[CHUNK - 1 : CHUNK]
            lifted = (queries * jnp.exp(total - middle)).astype(BF16)
            lowered = (keys * jnp.exp(middle - total)).astype(BF16)
            scores = jnp.where(causal, mm_nt(lifted, lowered), 0.0).astype(BF16)
            entry = memory[s]
            entry_low = entry.astype(BF16)
            states[s, part] = entry_low
            profile = queries * jnp.exp(total)
            head_local[s, rows, :] = mm(scores, values) + mm_nt(profile.astype(BF16), entry_low)
            gone = preceding[s]
            query_profile[s, rows, :] = (profile * jnp.exp(gone)).astype(BF16)
            cumulative[s, rows, :] = total
            tails = (keys * jnp.exp(last - total)).astype(BF16)
            memory[s] = entry * jnp.exp(last) + mm_tn(values, tails)
            before[s, pl.ds(step * (STEP // CHUNK) + part, 1), :] = gone
            preceding[s] = gone + last
    end_state[...] = memory[...]
    total_decay[...] = preceding[...]


def forward_mix(projected, halo, low_rank, taps, rank_up, bias, dv):
    sequences, length, c3 = projected.shape
    rank, dk = rank_up.shape
    chunks = length // CHUNK
    per_step = STEP // CHUNK
    return call(
        forward_body,
        (length // STEP,),
        [
            rows3(sequences, STEP, c3),
            whole((sequences, 8, c3)),
            rows3(sequences, STEP, rank),
            whole(taps.shape),
            whole((rank, dk)),
            whole((1, dk)),
        ],
        [
            rows3(sequences, STEP, dv),
            rows3(sequences, STEP, dk),
            rows3(sequences, STEP, dk),
            pl.BlockSpec((sequences, per_step, dv, dk), lambda i: (0, i, 0, 0)),
            whole((sequences, chunks, dk)),
            whole((sequences, dv, dk)),
            whole((sequences, 1, dk)),
        ],
        [
            shape_of((sequences, length, dv), F32),
            shape_of((sequences, length, dk), BF16),
            shape_of((sequences, length, dk), F32),
            shape_of((sequences, chunks, dv, dk), BF16),
            shape_of((sequences, chunks, dk), F32),
            shape_of((sequences, dv, dk), F32),
            shape_of((sequences, 1, dk), F32),
        ],
        [
            pltpu.VMEM((sequences, STEP + 8, c3), F32),
            pltpu.VMEM((sequences, dv, dk), F32),
            pltpu.VMEM((sequences, 1, dk), F32),
        ],
        2 * sequences * length * (4 * dk * dv + dk * dk) * 8,
        sequences * (length * (c3 * 2 + dv * 4 + dk * 6) + chunks * dv * dk * 2),
    )(projected, halo, low_rank, taps, rank_up, bias)


def head_rows(head_local, query_profile, entering, scale):
    return (head_local + mm_nt(query_profile, entering.astype(BF16))) * scale


def gate_body(head_local, query_profile, entering, out_gate, gain, gated):
    scale = query_profile.shape[-1] ** (-0.5)
    for s in range(head_local.shape[0]):
        head = head_rows(head_local[s], query_profile[s], entering[s], scale)
        inverse = lax.rsqrt(jnp.mean(head * head, axis=-1, keepdims=True) + EPS_HEAD)
        logits = out_gate[s].astype(F32)
        gated[s] = (head * inverse * gain[...] * (logits * sigmoid(logits))).astype(BF16)


def gate(head_local, query_profile, entering, out_gate, gain):
    sequences, length, dv = head_local.shape
    dk = query_profile.shape[-1]
    return call(
        gate_body,
        (length // STEP,),
        [
            rows3(sequences, STEP, dv),
            rows3(sequences, STEP, dk),
            whole((sequences, dv, dk)),
            rows3(sequences, STEP, dv),
            whole((1, dv)),
        ],
        rows3(sequences, STEP, dv),
        shape_of((sequences, length, dv), BF16),
        [],
        2 * sequences * length * dk * dv * 4,
        sequences * length * (dv * 8 + dk * 2),
    )(head_local, query_profile, entering, out_gate, gain)


PIECE = 128
HALF = PIECE // 2


def ffn_body(
    gated, w_own, w_across, w_down_hop, w_far, tok, gain, w_gate, w_up, w_down, upstream,
    out_part, weight_grads, output_grads, grad_gated, own_residual, own_grad, gain_grad,
    g_across, g_down, g_far, tok_here, up_here, wg, wu, wd, normed, hidden, grad_gate, grad_up,
    out_stage, part, via_across, via_down, from_across, from_down, residual_here, grad_here,
    mixer_here, pieces, received, weight_stage, output_stage,
    load_sem, row_sem, ag_send, ag_recv, rs_send, rs_recv, back_send, back_recv, store_sem,
    stage_sem, last_sem,
):
    turns = up_here.shape[0]
    halves = 2
    width = tok_here.shape[-1]
    me = lax.axis_index("mp")
    across = me + 1 - 2 * (me % 2)
    down = (me + 2) % 4
    far = 3 - me
    MESH = pl.DeviceIdType.MESH

    def remote(source, target, send, recv, device):
        return pltpu.make_async_remote_copy(
            src_ref=source,
            dst_ref=target,
            send_sem=send,
            recv_sem=recv,
            device_id={"mp": device},
            device_id_type=MESH,
        )

    def load(index, source, target):
        return pltpu.make_async_copy(source, target, load_sem.at[index])

    def load_tok(turn):
        return pltpu.make_async_copy(
            tok.at[turn // halves, :, turn % halves], tok_here.at[turn % 2], row_sem.at[0, turn]
        )

    def load_up(turn):
        return pltpu.make_async_copy(
            upstream.at[turn // halves, :, turn % halves], up_here.at[turn], row_sem.at[1, turn]
        )

    def direct(turn, side):
        return remote(
            gated.at[turn // halves, :, turn % halves],
            (g_across, g_down)[side].at[turn],
            ag_send.at[side, turn],
            ag_recv.at[side, turn],
            (across, down)[side],
        )

    def relay(turn, side):
        cut = pl.ds(2 * side, 2)
        return remote(
            (g_across, g_down)[side].at[turn, cut],
            g_far.at[turn, cut],
            ag_send.at[2 + side, turn],
            ag_recv.at[2 + side, turn],
            (down, across)[side],
        )

    first, second = pl.ds(0, HALF), pl.ds(HALF, HALF)

    def scatter(turn, index):
        source, target, device = (
            (part.at[turn, far, first], via_across.at[turn], across),
            (part.at[turn, far, second], via_down.at[turn], down),
            (part.at[turn, across, first], from_across.at[turn, first], across),
            (part.at[turn, down, second], from_down.at[turn, second], down),
            (part.at[turn, across, second], from_across.at[turn, second], across),
            (part.at[turn, down, first], from_down.at[turn, first], down),
        )[index]
        return remote(source, target, rs_send.at[index, turn], rs_recv.at[index, turn], device)

    def give_back(turn, slot):
        return remote(
            pieces.at[turn, slot],
            received.at[turn, slot],
            back_send.at[slot, turn],
            back_recv.at[slot, turn],
            (me, across, down, far)[slot],
        )

    def store_out(turn):
        return pltpu.make_async_copy(
            out_stage.at[turn % 2],
            out_part.at[turn // halves, :, turn % halves],
            store_sem.at[turn],
        )

    barrier = pltpu.get_barrier_semaphore()
    loads = [load(0, w_gate, wg), load(1, w_up, wu), load(2, w_down, wd)]
    for copy in loads:
        copy.start()
    for turn in range(turns):
        if turn < 2:
            load_tok(turn).start()
        load_up(turn).start()
    for device in (across, down, far):
        pl.semaphore_signal(barrier, inc=1, device_id={"mp": device}, device_id_type=MESH)
    pl.semaphore_wait(barrier, 3)
    for side in range(2):
        direct(0, side).start()
    for side in range(2):
        direct(1, side).start()
    gain_grad[...] = jnp.zeros_like(gain_grad)
    for side in range(2):
        direct(0, side).wait_recv()
        relay(0, side).start()
    for copy in loads:
        copy.wait()

    def forward_and_back(turn):
        for side in range(2):

            @pl.when(turn + 1 < turns)
            def _():
                direct(turn + 1, side).wait_recv()
                relay(turn + 1, side).start()

            @pl.when(turn + 2 < turns)
            def _():
                direct(turn + 2, side).start()

        load_tok(turn).wait()
        load_up(turn).wait()
        for side in range(2):
            relay(turn, side).wait_recv()
        rows = 4 * PIECE

        def flat(values):
            return values.reshape(rows, values.shape[-1])

        mixed = mm(flat(gated[turn // halves, :, turn % halves]), w_own[...])
        mixed = mixed + mm(flat(g_across[turn]), w_across[...])
        mixed = mixed + mm(flat(g_down[turn]), w_down_hop[...])
        mixed = mixed + mm(flat(g_far[turn]), w_far[...])
        residual = flat(tok_here[turn % 2]).astype(F32) + mixed
        for quarter in range(4):

            @pl.when(me == quarter)
            def _():
                residual_here[turn] = residual[quarter * PIECE : (quarter + 1) * PIECE]

        inverse = lax.rsqrt(jnp.mean(residual * residual, axis=-1, keepdims=True) + EPS_NORM)
        unit = residual * inverse
        rounded = (unit * gain[...]).astype(BF16)
        normed[turn] = rounded
        gate_rows = mm(rounded, wg[...])
        up_rows = mm(rounded, wu[...])
        share = sigmoid(gate_rows)
        swished = gate_rows * share
        hidden_rows = (swished * up_rows).astype(BF16)
        hidden[turn] = hidden_rows
        grad_hidden = mm_nt(flat(up_here[turn]), wd[...])
        slope = share * (1.0 + gate_rows * (1.0 - share))
        grad_gate_rows = (grad_hidden * up_rows * slope).astype(BF16)
        grad_up_rows = (grad_hidden * swished).astype(BF16)
        grad_gate[turn] = grad_gate_rows
        grad_up[turn] = grad_up_rows
        grad_rows = mm_nt(grad_gate_rows, wg[...]) + mm_nt(grad_up_rows, wu[...])
        part[turn] = grad_rows.astype(BF16).reshape(4, PIECE, width)
        for index in range(4):
            scatter(turn, index).start()
        gain_grad[...] += jnp.sum(grad_rows * unit, axis=0, keepdims=True)

        @pl.when(turn >= 2)
        def _():
            store_out(turn - 2).wait()

        out_stage[turn % 2] = mm(hidden_rows, wd[...]).astype(BF16).reshape(4, PIECE, width)
        store_out(turn).start()

        @pl.when(turn + 2 < turns)
        def _():
            load_tok(turn + 2).start()

    def pass_on(turn):
        scatter(turn, 0).wait_recv()
        part[turn, down, 0:HALF] = part[turn, down, 0:HALF] + via_across[turn]
        scatter(turn, 5).start()
        scatter(turn, 1).wait_recv()
        part[turn, across, HALF:PIECE] = part[turn, across, HALF:PIECE] + via_down[turn]
        scatter(turn, 4).start()

    def collect(turn):
        for index in range(2, 6):
            scatter(turn, index).wait_recv()
        grad_normed = part[turn, me].astype(F32) + from_across[turn].astype(F32)
        grad_normed = grad_normed + from_down[turn].astype(F32)
        residual = residual_here[turn]
        inverse = lax.rsqrt(jnp.mean(residual * residual, axis=-1, keepdims=True) + EPS_NORM)
        unit = residual * inverse
        scaled = grad_normed * gain[...]
        through = inverse * (scaled - unit * jnp.mean(scaled * unit, axis=-1, keepdims=True))
        grad_residual = up_here[turn, me].astype(F32) + through
        grad_here[turn] = grad_residual
        grad_mixer = grad_residual.astype(BF16)
        mixer_here[turn] = grad_mixer
        for slot, weight in enumerate((w_own, w_across, w_down_hop, w_far)):
            piece = mm_nt(grad_mixer, weight[...]).astype(BF16)
            if slot == 0:
                received[turn, 0] = piece
            else:
                pieces[turn, slot] = piece
                give_back(turn, slot).start()

    def round_of(index, carry):
        @pl.when(index < turns)
        def _():
            forward_and_back(index)

        @pl.when(jnp.logical_and(index >= 1, index <= turns))
        def _():
            pass_on(index - 1)

        @pl.when(index >= 2)
        def _():
            collect(index - 2)

        return carry

    lax.fori_loop(0, turns + 2, round_of, 0)

    tile = weight_stage.shape[2]
    tiles = width // tile

    def store_weight(kind, index, slot):
        return pltpu.make_async_copy(
            weight_stage.at[slot, kind],
            weight_grads.at[kind, pl.ds(index * tile, tile)],
            stage_sem.at[slot, kind],
        )

    all_rows = turns * 4 * PIECE

    def weight_tile(index, carry):
        slot = index % 2
        columns = pl.ds(pl.multiple_of(index * tile, tile), tile)

        @pl.when(index >= 2)
        def _():
            for kind in range(3):
                store_weight(kind, index - 2, slot).wait()

        left = normed[:, :, columns].reshape(all_rows, tile)
        upper = up_here[:, :, :, columns].reshape(all_rows, tile)
        units = hidden.shape[-1]
        for kind, (one, other) in enumerate(
            ((left, grad_gate), (left, grad_up), (upper, hidden))
        ):
            weight_stage[slot, kind] = mm_tn(one, other[...].reshape(all_rows, units)).astype(BF16)
            store_weight(kind, index, slot).start()
        return carry

    lax.fori_loop(0, tiles, weight_tile, 0)
    mixer_rows = mixer_here[...].reshape(turns * PIECE, width)
    dv = gated.shape[-1]
    for slot in range(4):
        if slot == 0:
            blocks = [gated[t // halves, me, t % halves] for t in range(turns)]
        else:
            source = (None, g_across, g_down, g_far)[slot]
            blocks = [source[t, me] for t in range(turns)]
        rows = jnp.concatenate(blocks, axis=0)
        output_stage[slot] = mm_tn(mixer_rows, rows).astype(BF16)

    last = [
        pltpu.make_async_copy(residual_here, own_residual, last_sem.at[0]),
        pltpu.make_async_copy(grad_here, own_grad, last_sem.at[1]),
        pltpu.make_async_copy(output_stage, output_grads, last_sem.at[2]),
    ]
    for copy in last:
        copy.start()
    for turn in range(turns):
        for slot in range(1, 4):
            give_back(turn, slot).wait_recv()
        for slot in range(4):
            source = (me, across, down, far)[slot]
            pltpu.make_async_copy(
                received.at[turn, slot],
                grad_gated.at[turn // halves, source, turn % halves],
                last_sem.at[3 + turn * 4 + slot],
            ).start()
    for turn in range(turns):
        for slot in range(4):
            source = (me, across, down, far)[slot]
            pltpu.make_async_copy(
                received.at[turn, slot],
                grad_gated.at[turn // halves, source, turn % halves],
                last_sem.at[3 + turn * 4 + slot],
            ).wait()
        if turn >= turns - 2:
            store_out(turn).wait()
        for side in range(2):
            direct(turn, side).wait_send()
            relay(turn, side).wait_send()
        for index in range(6):
            scatter(turn, index).wait_send()
        for slot in range(1, 4):
            give_back(turn, slot).wait_send()
    for index in range(max(tiles - 2, 0), tiles):
        for kind in range(3):
            store_weight(kind, index, index % 2).wait()
    for copy in last:
        copy.wait()


def feed_forward(gated, weights, tok, gain, w_gate, w_up, w_down, upstream):
    sequences, length, width = tok.shape
    dv, units = gated.shape[-1], w_gate.shape[1]
    halves = length // 4 // PIECE
    turns = sequences * halves

    def pieces_of(values):
        return values.reshape(sequences, 4, halves, PIECE, values.shape[-1])

    anywhere = pl.BlockSpec(memory_space=pl.ANY)
    vmem = pl.BlockSpec(memory_space=pltpu.VMEM)
    dma = pltpu.SemaphoreType.DMA
    rows = 4 * PIECE
    outs = pl.pallas_call(
        ffn_body,
        in_specs=[vmem] * 5 + [anywhere, vmem] + [anywhere] * 4,
        out_specs=[anywhere] * 6 + [vmem],
        out_shape=[
            shape_of((sequences, 4, halves, PIECE, width), BF16),
            shape_of((3, width, units), BF16),
            shape_of((4, width, dv), BF16),
            shape_of((sequences, 4, halves, PIECE, dv), BF16),
            shape_of((turns, PIECE, width), F32),
            shape_of((turns, PIECE, width), F32),
            shape_of((1, width), F32),
        ],
        scratch_shapes=[
            pltpu.VMEM((turns, 4, PIECE, dv), BF16),
            pltpu.VMEM((turns, 4, PIECE, dv), BF16),
            pltpu.VMEM((turns, 4, PIECE, dv), BF16),
            pltpu.VMEM((2, 4, PIECE, width), BF16),
            pltpu.VMEM((turns, 4, PIECE, width), BF16),
            pltpu.VMEM((width, units), BF16),
            pltpu.VMEM((width, units), BF16),
            pltpu.VMEM((units, width), BF16),
            pltpu.VMEM((turns, rows, width), BF16),
            pltpu.VMEM((turns, rows, units), BF16),
            pltpu.VMEM((turns, rows, units), BF16),
            pltpu.VMEM((turns, rows, units), BF16),
            pltpu.VMEM((2, 4, PIECE, width), BF16),
            pltpu.VMEM((turns, 4, PIECE, width), BF16),
            pltpu.VMEM((turns, HALF, width), BF16),
            pltpu.VMEM((turns, HALF, width), BF16),
            pltpu.VMEM((turns, PIECE, width), BF16),
            pltpu.VMEM((turns, PIECE, width), BF16),
            pltpu.VMEM((turns, PIECE, width), F32),
            pltpu.VMEM((turns, PIECE, width), F32),
            pltpu.VMEM((turns, PIECE, width), BF16),
            pltpu.VMEM((turns, 4, PIECE, dv), BF16),
            pltpu.VMEM((turns, 4, PIECE, dv), BF16),
            pltpu.VMEM((2, 3, 256, units), BF16),
            pltpu.VMEM((4, width, dv), BF16),
            dma((3,)),
            dma((2, turns)),
            dma((4, turns)),
            dma((4, turns)),
            dma((6, turns)),
            dma((6, turns)),
            dma((4, turns)),
            dma((4, turns)),
            dma((turns,)),
            dma((2, 3)),
            dma((3 + 4 * turns,)),
        ],
        compiler_params=pltpu.CompilerParams(
            collective_id=0, has_side_effects=True, vmem_limit_bytes=64 * 2**20
        ),
        cost_estimate=pl.CostEstimate(
            flops=2 * sequences * length * width * (4 * dv + 9 * units),
            bytes_accessed=sequences * length * width * 8,
            transcendentals=0,
        ),
        name="feed_forward",
    )(pieces_of(gated), *weights, pieces_of(tok), gain, w_gate, w_up, w_down, pieces_of(upstream))
    out_part, weight_grads, output_grads, grad_gated, own_residual, own_grad, gain_grad = outs
    return (
        out_part.reshape(sequences, 4, length // 4, width),
        weight_grads,
        output_grads,
        grad_gated.reshape(sequences, length, dv),
        own_residual.reshape(sequences, length // 4, width),
        own_grad.reshape(sequences, length // 4, width),
        gain_grad,
    )


def ungate_body(
    grad_gated, head_local, query_profile, entering, out_gate, gain,
    grad_out_gate, grad_head, state_grad, gain_grad,
):
    step = pl.program_id(0)

    @pl.when(step == 0)
    def _():
        state_grad[...] = jnp.zeros_like(state_grad)
        gain_grad[...] = jnp.zeros_like(gain_grad)

    scale = query_profile.shape[-1] ** (-0.5)
    for s in range(head_local.shape[0]):
        upper = grad_gated[s].astype(F32)
        head = head_rows(head_local[s], query_profile[s], entering[s], scale)
        inverse = lax.rsqrt(jnp.mean(head * head, axis=-1, keepdims=True) + EPS_HEAD)
        unit = head * inverse
        logits = out_gate[s].astype(F32)
        share = sigmoid(logits)
        slope = share * (1.0 + logits * (1.0 - share))
        grad_out_gate[s] = (upper * unit * gain[...] * slope).astype(BF16)
        grad_normed = upper * (logits * share)
        gain_grad[...] += jnp.sum(grad_normed * unit, axis=0, keepdims=True)
        scaled = grad_normed * gain[...]
        through = inverse * (scaled - unit * jnp.mean(scaled * unit, axis=-1, keepdims=True))
        rounded = (through * scale).astype(BF16)
        grad_head[s] = rounded
        state_grad[s] += mm_tn(rounded, query_profile[s])


def ungate(grad_gated, head_local, query_profile, entering, out_gate, gain):
    sequences, length, dv = head_local.shape
    dk = query_profile.shape[-1]
    return call(
        ungate_body,
        (length // STEP,),
        [
            rows3(sequences, STEP, dv),
            rows3(sequences, STEP, dv),
            rows3(sequences, STEP, dk),
            whole((sequences, dv, dk)),
            rows3(sequences, STEP, dv),
            whole((1, dv)),
        ],
        [
            rows3(sequences, STEP, dv),
            rows3(sequences, STEP, dv),
            whole((sequences, dv, dk)),
            whole((1, dv)),
        ],
        [
            shape_of((sequences, length, dv), BF16),
            shape_of((sequences, length, dv), BF16),
            shape_of((sequences, dv, dk), F32),
            shape_of((1, dv), F32),
        ],
        [],
        2 * sequences * length * dk * dv * 8,
        sequences * length * (dv * 12 + dk * 2),
    )(grad_gated, head_local, query_profile, entering, out_gate, gain)


def backward_body(
    projected, earlier, halo, low_rank, taps_in, rank_up, bias, cumulative, states, before,
    entering, leaving, grad_head,
    grad_projected, grad_low_rank, first_rows, filter_grad, rank_up_grad, bias_grad,
    extended, grad_extended, upstream,
):
    back = pl.program_id(0)
    step = pl.num_programs(0) - 1 - back
    per_step = STEP // CHUNK
    sequences = projected.shape[0]

    @pl.when(back == 0)
    def _():
        upstream[...] = leaving[...]
        grad_extended[:, STEP : STEP + 8, :] = jnp.zeros_like(grad_extended[:, STEP : STEP + 8, :])
        filter_grad[...] = jnp.zeros_like(filter_grad)
        rank_up_grad[...] = jnp.zeros_like(rank_up_grad)
        bias_grad[...] = jnp.zeros_like(bias_grad)

    @pl.when(back > 0)
    def _():
        grad_extended[:, STEP : STEP + 8, :] = grad_extended[:, 0:8, :]

    @pl.when(step == 0)
    def _():
        extended[:, 0:8, :] = halo[...]

    @pl.when(step > 0)
    def _():
        extended[:, 0:8, :] = earlier[...].astype(F32)[:, 8:16, :]

    taps = taps_in[...]
    width = rank_up.shape[1]
    causal = triangle(True)
    for s in range(sequences):
        extended[s, 8 : 8 + STEP, :] = projected[s].astype(F32)
        filtered = filter_rows(extended.at[s], taps, STEP)
        share = sigmoid(filtered)
        convolved = (filtered * share).astype(BF16)
        slope = share * (1.0 + filtered * (1.0 - share))
        logit = mm(low_rank[s], rank_up[...]) + bias[...]
        logit_grads = [None] * per_step
        for part in reversed(range(per_step)):
            rows = slice(part * CHUNK, (part + 1) * CHUNK)
            queries = convolved[rows, :width].astype(F32)
            keys = convolved[rows, width : 2 * width].astype(F32)
            values = convolved[rows, 2 * width :]
            grad_rows = grad_head[s, rows, :]
            total = cumulative[s, rows, :]
            middle, last = total[CHUNK // 2 - 1 : CHUNK // 2], total[CHUNK - 1 : CHUNK]
            lift, lower = jnp.exp(total - middle), jnp.exp(middle - total)
            inner, outer, whole_decay = jnp.exp(total), jnp.exp(last - total), jnp.exp(last)
            lifted, lowered = (queries * lift).astype(BF16), (keys * lower).astype(BF16)
            profile, tails = (queries * inner).astype(BF16), (keys * outer).astype(BF16)
            previous = before[s, pl.ds(step * per_step + part, 1), :]
            state = states[s, part].astype(F32) + entering[s] * jnp.exp(previous)
            scores = jnp.where(causal, mm_nt(lifted, lowered), 0.0).astype(BF16)
            grad_scores = jnp.where(causal, mm_nt(grad_rows, values), 0.0).astype(BF16)
            later = upstream[s]
            later_low = later.astype(BF16)
            grad_values = mm_tn(scores, grad_rows) + mm_nt(tails, later_low)
            grad_lifted = mm(grad_scores, lowered)
            grad_lowered = mm_tn(grad_scores, lifted)
            grad_profile = mm(grad_rows, state.astype(BF16))
            grad_tails = mm(values, later_low)
            upstream[s] = later * whole_decay + mm_tn(grad_rows, profile)
            tail_terms = tails.astype(F32) * grad_tails
            grad_total = (
                lifted.astype(F32) * grad_lifted
                - lowered.astype(F32) * grad_lowered
                + profile.astype(F32) * grad_profile
                - tail_terms
            )
            grad_last = jnp.sum(tail_terms, axis=0, keepdims=True) + whole_decay * jnp.sum(
                later * state, axis=0, keepdims=True
            )
            grad_decay = running_sum(grad_total, False) + grad_last
            logit_grads[part] = grad_decay / GATE_NORMALIZER * sigmoid(-logit[rows])
            grad_extended[s, rows, :width] = (
                grad_lifted * lift + grad_profile * inner
            ) * slope[rows, :width]
            grad_extended[s, rows, width : 2 * width] = (
                grad_lowered * lower + grad_tails * outer
            ) * slope[rows, width : 2 * width]
            grad_extended[s, rows, 2 * width :] = grad_values * slope[rows, 2 * width :]
        logit_grad = jnp.concatenate(logit_grads, axis=0)
        logit_low = logit_grad.astype(BF16)
        bias_grad[...] += jnp.sum(logit_grad, axis=0, keepdims=True)
        rank_up_grad[...] += mm_tn(low_rank[s], logit_low)
        grad_low_rank[s] = mm_nt(logit_low, rank_up[...]).astype(BF16)
        total_rows = taps[EDGE : EDGE + 1, :] * grad_extended[s, 0:STEP, :]
        for offset in range(EDGE):
            total_rows = total_rows + taps[offset : offset + 1, :] * grad_extended[
                s, pl.ds(EDGE - offset, STEP), :
            ]
        grad_projected[s] = total_rows.astype(BF16)
        grad_filtered = grad_extended[s, 0:STEP, :]
        for offset in range(CONV):
            filter_grad[offset : offset + 1, :] += jnp.sum(
                grad_filtered * extended[s, pl.ds(8 - EDGE + offset, STEP), :],
                axis=0,
                keepdims=True,
            )
        first_rows[s] = grad_extended[s, 0:8, :]


def backward_mix(
    projected, halo, low_rank, taps, rank_up, bias, cumulative, states, before, entering,
    leaving, grad_head,
):
    sequences, length, c3 = projected.shape
    rank, dk = rank_up.shape
    dv = grad_head.shape[-1]
    chunks, per_step, steps = length // CHUNK, STEP // CHUNK, length // STEP

    def reverse(size, width):
        return pl.BlockSpec((sequences, size, width), lambda i: (0, steps - 1 - i, 0))

    return call(
        backward_body,
        (steps,),
        [
            reverse(STEP, c3),
            pl.BlockSpec(
                (sequences, 16, c3),
                lambda i: (0, jnp.maximum((steps - 1 - i) * (STEP // 16) - 1, 0), 0),
            ),
            whole((sequences, 8, c3)),
            reverse(STEP, rank),
            whole(taps.shape),
            whole((rank, dk)),
            whole((1, dk)),
            reverse(STEP, dk),
            pl.BlockSpec((sequences, per_step, dv, dk), lambda i: (0, steps - 1 - i, 0, 0)),
            whole((sequences, chunks, dk)),
            whole((sequences, dv, dk)),
            whole((sequences, dv, dk)),
            reverse(STEP, dv),
        ],
        [
            reverse(STEP, c3),
            reverse(STEP, rank),
            whole((sequences, 8, c3)),
            whole(taps.shape),
            whole((rank, dk)),
            whole((1, dk)),
        ],
        [
            shape_of((sequences, length, c3), BF16),
            shape_of((sequences, length, rank), BF16),
            shape_of((sequences, 8, c3), F32),
            shape_of(taps.shape, F32),
            shape_of((rank, dk), F32),
            shape_of((1, dk), F32),
        ],
        [
            pltpu.VMEM((sequences, STEP + 8, c3), F32),
            pltpu.VMEM((sequences, STEP + 8, c3), F32),
            pltpu.VMEM((sequences, dv, dk), F32),
        ],
        2 * sequences * length * (12 * dk * dv) * 8,
        sequences * (length * (c3 * 4 + dk * 4 + dv * 2) + chunks * dv * dk * 2),
    )(
        projected, projected, halo, low_rank, taps, rank_up, bias, cumulative, states, before,
        entering, leaving, grad_head,
    )


def input_grad_body(
    grad_projected, grad_out_gate, grad_low_rank, w_proj, w_gate, w_rank, normed,
    parts, gain_grad,
):
    @pl.when(pl.program_id(0) == 0)
    def _():
        gain_grad[...] = jnp.zeros_like(gain_grad)

    for s in range(normed.shape[0]):
        total = mm_nt(grad_projected[s], w_proj[...]) + mm_nt(grad_out_gate[s], w_gate[...])
        total = total + mm_nt(grad_low_rank[s], w_rank[...])
        parts[s] = total.astype(BF16)
        gain_grad[...] += jnp.sum(total * normed[s].astype(F32), axis=0, keepdims=True)


def input_grad(grad_projected, grad_out_gate, grad_low_rank, w_proj, w_gate, w_rank, normed):
    sequences, length, width = normed.shape
    c3, dv, rank = w_proj.shape[1], w_gate.shape[1], w_rank.shape[1]
    return call(
        input_grad_body,
        (length // STEP,),
        [
            rows3(sequences, STEP, c3),
            rows3(sequences, STEP, dv),
            rows3(sequences, STEP, rank),
            whole((width, c3)),
            whole((width, dv)),
            whole((width, rank)),
            rows3(sequences, STEP, width),
        ],
        [rows3(sequences, STEP, width), whole((1, width))],
        [shape_of((sequences, length, width), BF16), shape_of((1, width), F32)],
        [],
        2 * sequences * length * width * (c3 + dv + rank),
        sequences * length * (2 * width + c3 + dv) * 2 + width * (c3 + dv) * 2,
    )(grad_projected, grad_out_gate, grad_low_rank, w_proj, w_gate, w_rank, normed)


ACROSS = [(i, i ^ 1) for i in range(4)]
DOWN = [(i, i ^ 2) for i in range(4)]
OPPOSITE = [(i, i ^ 3) for i in range(4)]


def gather_relative(block):
    half = block.shape[0] // 2
    across = lax.ppermute(block, "mp", ACROSS)
    down = lax.ppermute(block, "mp", DOWN)
    first = lax.ppermute(across[:half], "mp", DOWN)
    second = lax.ppermute(down[half:], "mp", ACROSS)
    return [block, across, down, jnp.concatenate([first, second], axis=0)]


def scatter_rows(first, across, down, far):
    via_across = lax.ppermute(far[:1], "mp", ACROSS)
    via_down = lax.ppermute(far[1:], "mp", DOWN)
    across_a = lax.ppermute(across[:1], "mp", ACROSS)
    down_b = lax.ppermute(down[1:], "mp", DOWN)
    across_b = lax.ppermute(across[1:] + via_down, "mp", ACROSS)
    down_a = lax.ppermute(down[:1] + via_across, "mp", DOWN)
    across = jnp.concatenate([across_a, across_b], axis=0).astype(F32)
    down = jnp.concatenate([down_a, down_b], axis=0).astype(F32)
    return first.astype(F32) + across + down


def scatter_quarters(parts, me):
    return scatter_rows(
        *[lax.dynamic_index_in_dim(parts, me ^ slot, 1, False) for slot in range(4)]
    )


def passed_along(block, axis, distance):
    devices = range(lax.axis_size(axis))
    route = [(i - distance, i) for i in devices if i - distance in devices]
    return lax.ppermute(block, axis, route)


def chain_states(decay, state, backward):
    count, mine = lax.axis_size("seq"), lax.axis_index("seq")
    if count == 2:
        return passed_along(state, "seq", -1 if backward else 1)
    decays, states = lax.all_gather(decay, "seq"), lax.all_gather(state, "seq")
    if backward:
        decays, states, mine = decays[::-1], states[::-1], count - 1 - mine

    def hop(position, subtotal):
        longer = subtotal * jnp.exp(decays[position]) + states[position]
        return jnp.where(position < mine, longer, subtotal)

    return lax.fori_loop(0, count - 1, hop, jnp.zeros_like(state))


def sum_shards(grad):
    if lax.axis_size("seq") != 2 or lax.axis_size("dp") != 4:
        total = lax.psum_scatter(grad, ("seq", "dp"), scatter_dimension=0, tiled=True)
        return total[0].astype(F32)
    side, place = lax.axis_index("seq"), lax.axis_index("dp")
    other = lax.dynamic_slice_in_dim(grad, (1 - side) * 4, 4, 0)
    kept = lax.dynamic_slice_in_dim(grad, side * 4, 4, 0)
    kept = kept + lax.ppermute(other, "seq", [(0, 1), (1, 0)])
    upward, downward = None, None
    for turn in range(1, 4):
        above = lax.dynamic_index_in_dim(kept, jnp.minimum(place + 4 - turn, 3), 0, False)
        below = lax.dynamic_index_in_dim(kept, jnp.maximum(place - 4 + turn, 0), 0, False)
        if turn > 1:
            above, below = above + upward, below + downward
        upward = lax.ppermute(above, "dp", [(i, i + 1) for i in range(turn)])
        downward = lax.ppermute(below, "dp", [(3 - i, 2 - i) for i in range(turn)])
    mine = lax.dynamic_index_in_dim(kept, place, 0, False)
    return mine.astype(F32) + upward.astype(F32) + downward.astype(F32)


def sum_over(values, axes):
    for axis in axes:
        count = lax.axis_size(axis)
        if count & (count - 1) or count > 4:
            values = lax.psum(values, axis)
            continue
        distance = 1
        while distance < count:
            values = values + lax.ppermute(values, axis, [(i, i ^ distance) for i in range(count)])
            distance *= 2
    return values


def on_device(
    tokens, lengths, mixer_gain, project_weight, filter_weight, rank_down, rank_up, decay_bias,
    gate_weight, head_gain, output_weight, channel_gain, hidden_gate, hidden_up, hidden_down,
    cotangent,
):
    length, sequences, width = tokens.shape
    shards = lax.axis_size("seq") * lax.axis_size("dp")
    shard = lax.axis_index("seq") * lax.axis_size("dp") + lax.axis_index("dp")
    me = lax.axis_index("mp")
    own_rows = length // lax.axis_size("mp")
    w_proj = project_weight[:, 0]
    taps = filter_weight[:, 0].astype(F32)
    rank_up_here = rank_up[:, 0]
    bias = decay_bias.astype(F32)
    mixer_gain_f = mixer_gain.astype(F32)[None]
    channel_gain_f = channel_gain.astype(F32)[None]
    head_gain_f = head_gain.astype(F32)[None]
    dv = gate_weight.shape[1]
    places = jnp.concatenate(
        [lengths.astype(jnp.int32), (lax.axis_index("seq") * length).astype(jnp.int32).reshape(1)]
    )

    edge_tokens = passed_along(tokens[length - EDGE :], "seq", 1)
    edge_f = edge_tokens.astype(F32)
    edge_inverse = lax.rsqrt(jnp.mean(edge_f * edge_f, axis=-1, keepdims=True) + EPS_NORM)
    edge_normed = (edge_f * edge_inverse * mixer_gain_f).astype(BF16)
    edge_projected = jnp.einsum(
        "psd,dc->spc", edge_normed, w_proj, preferred_element_type=F32
    ).astype(BF16)
    halo = jnp.pad(edge_projected.astype(F32), ((0, 0), (8 - EDGE, 0), (0, 0)))

    output_weights = gather_relative(output_weight)
    tok, upstream, normed, projected, out_gate, low_rank = project(
        places,
        tokens.reshape(length * sequences, width),
        cotangent.reshape(length * sequences, width),
        sequences,
        mixer_gain_f,
        w_proj,
        gate_weight,
        rank_down,
    )
    head_local, query_profile, cumulative, states, before, end_state, total_decay = forward_mix(
        projected, halo, low_rank, taps, rank_up_here, bias, dv
    )
    entering = chain_states(total_decay, end_state, False)
    gated = gate(head_local, query_profile, entering, out_gate, head_gain_f)
    (
        out_part, hidden_grads, output_parts, grad_gated, residual, grad_residual,
        channel_gain_part,
    ) = feed_forward(
        gated, output_weights, tok, channel_gain_f, hidden_gate, hidden_up, hidden_down, upstream
    )
    grad_out_gate, grad_head, state_grad, head_gain_part = ungate(
        grad_gated, head_local, query_profile, entering, out_gate, head_gain_f
    )
    leaving = chain_states(total_decay, state_grad, True)
    (
        grad_projected, grad_low_rank, first_rows, filter_part, rank_up_part, bias_part,
    ) = backward_mix(
        projected, halo, low_rank, taps, rank_up_here, bias, cumulative, states, before,
        entering, leaving, grad_head,
    )
    edge = jnp.concatenate(
        [
            sum(taps[j : j + 1] * first_rows[:, i - j : i - j + 1] for j in range(i + 1))
            for i in range(EDGE)
        ],
        axis=1,
    )
    edge = passed_along(edge, "seq", -1)
    tail = grad_projected[:, length - 16 :].astype(F32)
    tail = tail + jnp.pad(edge, ((0, 0), (16 - EDGE, 0), (0, 0)))
    grad_projected = lax.dynamic_update_slice_in_dim(
        grad_projected, tail.astype(BF16), length - 16, 1
    )
    normed_parts, mixer_gain_part = input_grad(
        grad_projected, grad_out_gate, grad_low_rank, w_proj, gate_weight, rank_down, normed
    )

    def flat(values):
        return values.reshape(sequences * length, values.shape[-1])

    def in_shards(grad):
        return grad.astype(BF16).reshape(shards, width // shards, grad.shape[-1])

    hidden_grads = hidden_grads.reshape(3, shards, width // shards, hidden_grads.shape[-1])
    hidden_grads = sum_shards(hidden_grads.swapaxes(0, 1))
    halved = output_parts.reshape(4, 2, width // 2, dv)
    output_grad = scatter_rows(*[halved[slot] for slot in range(4)])
    mixer_grads = jnp.concatenate(
        [
            in_shards(mm_tn(flat(normed), flat(grad_projected))),
            in_shards(mm_tn(flat(normed), flat(grad_out_gate))),
            in_shards(output_grad.reshape(width, dv)),
        ],
        axis=-1,
    )
    mixer_grads = sum_shards(mixer_grads)
    c3 = w_proj.shape[1]

    shared = [
        mixer_gain_part[0] / mixer_gain_f[0],
        channel_gain_part[0],
        head_gain_part[0],
        mm_tn(flat(normed), flat(grad_low_rank)).reshape(-1),
    ]
    local = [filter_part.reshape(-1), rank_up_part.reshape(-1), bias_part.reshape(-1)]
    shared_size = sum(part.shape[0] for part in shared)
    small = sum_over(jnp.concatenate(shared + local), ("seq", "dp"))
    shared_sum = sum_over(small[:shared_size], ("mp",))

    def take(values, start, shape):
        count = 1
        for size in shape:
            count *= size
        return lax.slice_in_dim(values, start, start + count).reshape(shape)

    def own(values):
        share = values.shape[-1] // shards
        return lax.dynamic_slice_in_dim(values, shard * share, share, values.ndim - 1)

    mixer_gain_grad = take(shared_sum, 0, (width,))
    channel_gain_grad = take(shared_sum, width, (width,))
    head_gain_grad = take(shared_sum, 2 * width, (dv,))
    rank_down_grad = take(shared_sum, 2 * width + dv, rank_down.shape)
    filter_grad = own(take(small, shared_size, filter_weight.shape))
    start = shared_size + filter_weight.size
    rank_up_grad = own(take(small, start, rank_up.shape))
    decay_bias_grad = own(take(small, start + rank_up.size, decay_bias.shape))

    own_shape = (sequences, 4, own_rows, width)
    ffn_out = scatter_quarters(out_part, me)
    own_positions = lax.axis_index("seq") * length + me * own_rows
    own_positions = own_positions + lax.broadcasted_iota(jnp.int32, (1, own_rows, 1), 1)
    own_mask = own_positions < lengths[:, None, None]
    outputs = jnp.where(own_mask, residual + ffn_out, 0.0).astype(BF16)
    grad_normed = scatter_quarters(normed_parts.reshape(own_shape), me)
    rows = lax.dynamic_index_in_dim(tok.reshape(own_shape), me, 1, False).astype(F32)
    inverse = lax.rsqrt(jnp.mean(rows * rows, axis=-1, keepdims=True) + EPS_NORM)
    unit = rows * inverse
    scaled = grad_normed * mixer_gain_f
    through = inverse * (scaled - unit * jnp.mean(scaled * unit, axis=-1, keepdims=True))
    token_grads = grad_residual + through
    return (
        outputs.swapaxes(0, 1),
        token_grads.swapaxes(0, 1),
        mixer_gain_grad,
        mixer_grads[:, None, :c3],
        filter_grad,
        rank_down_grad,
        rank_up_grad,
        decay_bias_grad,
        mixer_grads[:, c3 : c3 + dv],
        head_gain_grad,
        mixer_grads[:, c3 + dv :].T,
        channel_gain_grad,
        hidden_grads[0],
        hidden_grads[1],
        hidden_grads[2].T,
    )


def solution(mesh):
    in_specs = (
        P("seq", "dp", None),
        P("dp"),
        P(),
        P(None, "mp", None),
        P(None, "mp", None),
        P(),
        P(None, "mp", None),
        P("mp", None),
        P(None, "mp"),
        P(),
        P("mp", None),
        P(),
        P(None, "mp"),
        P(None, "mp"),
        P("mp", None),
        P("seq", "dp", None),
    )
    out_specs = (
        P(("seq", "mp"), "dp", None),
        P(("seq", "mp"), "dp", None),
        P(),
        P(("seq", "dp"), "mp", None),
        P(None, "mp", ("seq", "dp")),
        P(),
        P(None, "mp", ("seq", "dp")),
        P("mp", ("seq", "dp")),
        P(("seq", "dp"), "mp"),
        P(),
        P("mp", ("seq", "dp")),
        P(),
        P(("seq", "dp"), "mp"),
        P(("seq", "dp"), "mp"),
        P("mp", ("seq", "dp")),
    )
    return jax.shard_map(
        on_device, mesh=mesh, in_specs=in_specs, out_specs=out_specs, check_vma=False
    )
```

```python
import functools

import jax
import jax.numpy as jnp
from jax import lax
from jax.experimental import pallas as pl
from jax.experimental.pallas import tpu as pltpu
from jax.sharding import PartitionSpec as P

CONV = 4
EDGE = CONV - 1
CHUNK = 128
STEP = 256
EPS_NORM = 1e-06
EPS_HEAD = 1e-05
GATE_NORMALIZER = 16.0
HIGHEST = lax.Precision.HIGHEST
BF16 = jnp.bfloat16
F32 = jnp.float32
VMEM_LIMIT = 56 * 2**20


def mm(left, right):
    return lax.dot_general(left, right, (((1,), (0,)), ((), ())), preferred_element_type=F32)


def mm_nt(left, right):
    return lax.dot_general(left, right, (((1,), (1,)), ((), ())), preferred_element_type=F32)


def mm_tn(left, right):
    return lax.dot_general(left, right, (((0,), (0,)), ((), ())), preferred_element_type=F32)


def sigmoid(values):
    return 1.0 / (1.0 + jnp.exp(-values))


def whole(shape):
    return pl.BlockSpec(shape, lambda *_: (0,) * len(shape))


def rows_of(size, width):
    return pl.BlockSpec((size, width), lambda i, *_: (i, 0))


def call(body, grid, in_specs, out_specs, out_shape, scratch, flops, moved, prefetch=0):
    return pl.pallas_call(
        body,
        grid_spec=pltpu.PrefetchScalarGridSpec(
            num_scalar_prefetch=prefetch,
            grid=grid,
            in_specs=in_specs,
            out_specs=out_specs,
            scratch_shapes=scratch,
        ),
        out_shape=out_shape,
        compiler_params=pltpu.CompilerParams(
            dimension_semantics=("arbitrary",), vmem_limit_bytes=VMEM_LIMIT
        ),
        cost_estimate=pl.CostEstimate(flops=flops, bytes_accessed=moved, transcendentals=0),
    )


def shape_of(shape, dtype):
    return jax.ShapeDtypeStruct(shape, dtype)


def project_body(
    places, tok_in, cot_in, gain, w_proj, w_gate, w_rank,
    tok, upstream, normed, projected, out_gate, low_rank,
):
    step = pl.program_id(0)
    sequences, count, _ = tok.shape
    total = sequences * count
    row = lax.broadcasted_iota(jnp.int32, (total, total), 0)
    column = lax.broadcasted_iota(jnp.int32, (total, total), 1)
    source = (row % count) * sequences + row // count
    order = jnp.where(column == source, 1.0, 0.0).astype(BF16)
    rows = mm(order, tok_in[...])
    grads = mm(order, cot_in[...])
    first = places[sequences] + step * count
    position = first + lax.broadcasted_iota(jnp.int32, (count, 1), 0)
    inverse = lax.rsqrt(jnp.mean(rows * rows, axis=-1, keepdims=True) + EPS_NORM)
    rounded = (rows * inverse * gain[...]).astype(BF16)
    projected_rows = mm(rounded, w_proj[...]).astype(BF16)
    gate_rows = mm(rounded, w_gate[...]).astype(BF16)
    rank_rows = mm(rounded, w_rank[...]).astype(BF16)
    for s in range(sequences):
        part = slice(s * count, (s + 1) * count)
        tok[s] = rows[part].astype(BF16)
        upstream[s] = jnp.where(position < places[s], grads[part], 0.0).astype(BF16)
        normed[s] = rounded[part]
        projected[s] = projected_rows[part]
        out_gate[s] = gate_rows[part]
        low_rank[s] = rank_rows[part]


def rows3(sequences, size, width):
    return pl.BlockSpec((sequences, size, width), lambda i, *_: (0, i, 0))


def project(places, tok, cot, sequences, gain, w_proj, w_gate, w_rank):
    length, width = tok.shape[0] // sequences, tok.shape[1]
    c3, dv, rank = w_proj.shape[1], w_gate.shape[1], w_rank.shape[1]
    widths = (width, width, width, c3, dv, rank)
    return call(
        project_body,
        (length // CHUNK,),
        [
            rows_of(CHUNK * sequences, width),
            rows_of(CHUNK * sequences, width),
            whole((1, width)),
            whole((width, c3)),
            whole((width, dv)),
            whole((width, rank)),
        ],
        [rows3(sequences, CHUNK, w) for w in widths],
        [shape_of((sequences, length, w), BF16) for w in widths],
        [],
        2 * sequences * length * width * (c3 + dv + rank + 512),
        sequences * length * (5 * width + c3 + dv) * 2 + width * (c3 + dv) * 2,
        prefetch=1,
    )(places, tok, cot, gain, w_proj, w_gate, w_rank)


def triangle(lower):
    row = lax.broadcasted_iota(jnp.int32, (CHUNK, CHUNK), 0)
    column = lax.broadcasted_iota(jnp.int32, (CHUNK, CHUNK), 1)
    return row >= column if lower else row <= column


def running_sum(values, lower):
    ones = triangle(lower).astype(F32)
    return lax.dot_general(
        ones, values, (((1,), (0,)), ((), ())), precision=HIGHEST, preferred_element_type=F32
    )


def filter_rows(buffer, taps, count):
    total = taps[0:1, :] * buffer[pl.ds(8 - EDGE, count), :]
    for offset in range(1, CONV):
        total = total + taps[offset : offset + 1, :] * buffer[pl.ds(8 - EDGE + offset, count), :]
    return total


def forward_body(
    projected, halo, low_rank, taps_in, rank_up, bias,
    head_local, query_profile, cumulative, states, before, end_state, total_decay,
    extended, memory, preceding,
):
    step = pl.program_id(0)
    sequences = projected.shape[0]

    @pl.when(step == 0)
    def _():
        extended[:, 0:8, :] = halo[...]
        memory[...] = jnp.zeros_like(memory)
        preceding[...] = jnp.zeros_like(preceding)

    @pl.when(step > 0)
    def _():
        extended[:, 0:8, :] = extended[:, STEP : STEP + 8, :]

    width = rank_up.shape[1]
    causal = triangle(True)
    for s in range(sequences):
        extended[s, 8 : 8 + STEP, :] = projected[s].astype(F32)
        filtered = filter_rows(extended.at[s], taps_in[...], STEP)
        convolved = (filtered * sigmoid(filtered)).astype(BF16)
        logit = mm(low_rank[s], rank_up[...]) + bias[...]
        decay = (jnp.minimum(logit, 0.0) - jnp.log1p(jnp.exp(-jnp.abs(logit)))) / GATE_NORMALIZER
        for part in range(STEP // CHUNK):
            rows = slice(part * CHUNK, (part + 1) * CHUNK)
            queries = convolved[rows, :width].astype(F32)
            keys = convolved[rows, width : 2 * width].astype(F32)
            values = convolved[rows, 2 * width :]
            total = running_sum(decay[rows], True)
            middle, last = total[CHUNK // 2 - 1 : CHUNK // 2], total[CHUNK - 1 : CHUNK]
            lifted = (queries * jnp.exp(total - middle)).astype(BF16)
            lowered = (keys * jnp.exp(middle - total)).astype(BF16)
            scores = jnp.where(causal, mm_nt(lifted, lowered), 0.0).astype(BF16)
            entry = memory[s]
            entry_low = entry.astype(BF16)
            states[s, part] = entry_low
            profile = queries * jnp.exp(total)
            head_local[s, rows, :] = mm(scores, values) + mm_nt(profile.astype(BF16), entry_low)
            gone = preceding[s]
            query_profile[s, rows, :] = (profile * jnp.exp(gone)).astype(BF16)
            cumulative[s, rows, :] = total
            tails = (keys * jnp.exp(last - total)).astype(BF16)
            memory[s] = entry * jnp.exp(last) + mm_tn(values, tails)
            before[s, pl.ds(step * (STEP // CHUNK) + part, 1), :] = gone
            preceding[s] = gone + last
    end_state[...] = memory[...]
    total_decay[...] = preceding[...]


def forward_mix(projected, halo, low_rank, taps, rank_up, bias, dv):
    sequences, length, c3 = projected.shape
    rank, dk = rank_up.shape
    chunks = length // CHUNK
    per_step = STEP // CHUNK
    return call(
        forward_body,
        (length // STEP,),
        [
            rows3(sequences, STEP, c3),
            whole((sequences, 8, c3)),
            rows3(sequences, STEP, rank),
            whole(taps.shape),
            whole((rank, dk)),
            whole((1, dk)),
        ],
        [
            rows3(sequences, STEP, dv),
            rows3(sequences, STEP, dk),
            rows3(sequences, STEP, dk),
            pl.BlockSpec((sequences, per_step, dv, dk), lambda i: (0, i, 0, 0)),
            whole((sequences, chunks, dk)),
            whole((sequences, dv, dk)),
            whole((sequences, 1, dk)),
        ],
        [
            shape_of((sequences, length, dv), F32),
            shape_of((sequences, length, dk), BF16),
            shape_of((sequences, length, dk), F32),
            shape_of((sequences, chunks, dv, dk), BF16),
            shape_of((sequences, chunks, dk), F32),
            shape_of((sequences, dv, dk), F32),
            shape_of((sequences, 1, dk), F32),
        ],
        [
            pltpu.VMEM((sequences, STEP + 8, c3), F32),
            pltpu.VMEM((sequences, dv, dk), F32),
            pltpu.VMEM((sequences, 1, dk), F32),
        ],
        2 * sequences * length * (4 * dk * dv + dk * dk) * 8,
        sequences * (length * (c3 * 2 + dv * 4 + dk * 6) + chunks * dv * dk * 2),
    )(projected, halo, low_rank, taps, rank_up, bias)


def head_rows(head_local, query_profile, entering, scale):
    return (head_local + mm_nt(query_profile, entering.astype(BF16))) * scale


def gate_body(head_local, query_profile, entering, out_gate, gain, gated, head_out):
    scale = query_profile.shape[-1] ** (-0.5)
    for s in range(head_local.shape[0]):
        head = head_rows(head_local[s], query_profile[s], entering[s], scale)
        head_out[s] = head.astype(BF16)
        inverse = lax.rsqrt(jnp.mean(head * head, axis=-1, keepdims=True) + EPS_HEAD)
        logits = out_gate[s].astype(F32)
        gated[s] = (head * inverse * gain[...] * (logits * sigmoid(logits))).astype(BF16)


def gate(head_local, query_profile, entering, out_gate, gain):
    sequences, length, dv = head_local.shape
    dk = query_profile.shape[-1]
    return call(
        gate_body,
        (length // STEP,),
        [
            rows3(sequences, STEP, dv),
            rows3(sequences, STEP, dk),
            whole((sequences, dv, dk)),
            rows3(sequences, STEP, dv),
            whole((1, dv)),
        ],
        [rows3(sequences, STEP, dv)] * 2,
        [shape_of((sequences, length, dv), BF16)] * 2,
        [],
        2 * sequences * length * dk * dv * 4,
        sequences * length * (dv * 10 + dk * 2),
    )(head_local, query_profile, entering, out_gate, gain)


PIECE = 128
HALF = PIECE // 2


def ffn_body(
    gated, w_own, w_across, w_down_hop, w_far, tok, gain, w_gate, w_up, w_down, upstream,
    out_part, weight_grads, output_grads, grad_gated, own_residual, own_grad, gain_grad,
    g_across, g_down, g_far, tok_here, up_here, wg, wu, wd, normed, hidden, grad_gate, grad_up,
    out_stage, part, via_across, via_down, from_across, from_down, residual_here, grad_here,
    mixer_here, pieces, received, weight_stage, output_stage,
    load_sem, row_sem, ag_send, ag_recv, rs_send, rs_recv, back_send, back_recv, store_sem,
    stage_sem, last_sem,
):
    turns = up_here.shape[0]
    halves = 2
    width = tok_here.shape[-1]
    me = lax.axis_index("mp")
    across = me + 1 - 2 * (me % 2)
    down = (me + 2) % 4
    far = 3 - me
    MESH = pl.DeviceIdType.MESH

    def remote(source, target, send, recv, device):
        return pltpu.make_async_remote_copy(
            src_ref=source,
            dst_ref=target,
            send_sem=send,
            recv_sem=recv,
            device_id={"mp": device},
            device_id_type=MESH,
        )

    def load(index, source, target):
        return pltpu.make_async_copy(source, target, load_sem.at[index])

    def load_tok(turn):
        return pltpu.make_async_copy(
            tok.at[turn // halves, :, turn % halves], tok_here.at[turn % 2], row_sem.at[0, turn]
        )

    def load_up(turn):
        return pltpu.make_async_copy(
            upstream.at[turn // halves, :, turn % halves], up_here.at[turn], row_sem.at[1, turn]
        )

    def direct(turn, side):
        return remote(
            gated.at[turn // halves, :, turn % halves],
            (g_across, g_down)[side].at[turn],
            ag_send.at[side, turn],
            ag_recv.at[side, turn],
            (across, down)[side],
        )

    def relay(turn, side):
        cut = pl.ds(2 * side, 2)
        return remote(
            (g_across, g_down)[side].at[turn, cut],
            g_far.at[turn, cut],
            ag_send.at[2 + side, turn],
            ag_recv.at[2 + side, turn],
            (down, across)[side],
        )

    first, second = pl.ds(0, HALF), pl.ds(HALF, HALF)

    def scatter(turn, index):
        source, target, device = (
            (part.at[turn, far, first], via_across.at[turn], across),
            (part.at[turn, far, second], via_down.at[turn], down),
            (part.at[turn, across, first], from_across.at[turn, first], across),
            (part.at[turn, down, second], from_down.at[turn, second], down),
            (part.at[turn, across, second], from_across.at[turn, second], across),
            (part.at[turn, down, first], from_down.at[turn, first], down),
        )[index]
        return remote(source, target, rs_send.at[index, turn], rs_recv.at[index, turn], device)

    def give_back(turn, slot):
        return remote(
            pieces.at[turn, slot],
            received.at[turn, slot],
            back_send.at[slot, turn],
            back_recv.at[slot, turn],
            (me, across, down, far)[slot],
        )

    def store_out(turn):
        return pltpu.make_async_copy(
            out_stage.at[turn % 2],
            out_part.at[turn // halves, :, turn % halves],
            store_sem.at[turn],
        )

    barrier = pltpu.get_barrier_semaphore()
    loads = [load(0, w_gate, wg), load(1, w_up, wu), load(2, w_down, wd)]
    for copy in loads:
        copy.start()
    for turn in range(turns):
        if turn < 2:
            load_tok(turn).start()
        load_up(turn).start()
    for device in (across, down, far):
        pl.semaphore_signal(barrier, inc=1, device_id={"mp": device}, device_id_type=MESH)
    pl.semaphore_wait(barrier, 3)
    for side in range(2):
        direct(0, side).start()
    for side in range(2):
        direct(1, side).start()
    gain_grad[...] = jnp.zeros_like(gain_grad)
    for side in range(2):
        direct(0, side).wait_recv()
        relay(0, side).start()
    for copy in loads:
        copy.wait()

    def forward_and_back(turn):
        for side in range(2):

            @pl.when(turn + 1 < turns)
            def _():
                direct(turn + 1, side).wait_recv()
                relay(turn + 1, side).start()

            @pl.when(turn + 2 < turns)
            def _():
                direct(turn + 2, side).start()

        load_tok(turn).wait()
        load_up(turn).wait()
        for side in range(2):
            relay(turn, side).wait_recv()
        rows = 4 * PIECE

        def flat(values):
            return values.reshape(rows, values.shape[-1])

        mixed = mm(flat(gated[turn // halves, :, turn % halves]), w_own[...])
        mixed = mixed + mm(flat(g_across[turn]), w_across[...])
        mixed = mixed + mm(flat(g_down[turn]), w_down_hop[...])
        mixed = mixed + mm(flat(g_far[turn]), w_far[...])
        residual = flat(tok_here[turn % 2]).astype(F32) + mixed
        for quarter in range(4):

            @pl.when(me == quarter)
            def _():
                residual_here[turn] = residual[quarter * PIECE : (quarter + 1) * PIECE]

        inverse = lax.rsqrt(jnp.mean(residual * residual, axis=-1, keepdims=True) + EPS_NORM)
        unit = residual * inverse
        rounded = (unit * gain[...]).astype(BF16)
        normed[turn] = rounded
        gate_rows = mm(rounded, wg[...])
        up_rows = mm(rounded, wu[...])
        share = sigmoid(gate_rows)
        swished = gate_rows * share
        hidden_rows = (swished * up_rows).astype(BF16)
        hidden[turn] = hidden_rows
        grad_hidden = mm_nt(flat(up_here[turn]), wd[...])
        slope = share * (1.0 + gate_rows * (1.0 - share))
        grad_gate_rows = (grad_hidden * up_rows * slope).astype(BF16)
        grad_up_rows = (grad_hidden * swished).astype(BF16)
        grad_gate[turn] = grad_gate_rows
        grad_up[turn] = grad_up_rows
        grad_rows = mm_nt(grad_gate_rows, wg[...]) + mm_nt(grad_up_rows, wu[...])
        part[turn] = grad_rows.astype(BF16).reshape(4, PIECE, width)
        for index in range(4):
            scatter(turn, index).start()
        gain_grad[...] += jnp.sum(grad_rows * unit, axis=0, keepdims=True)

        @pl.when(turn >= 2)
        def _():
            store_out(turn - 2).wait()

        out_stage[turn % 2] = mm(hidden_rows, wd[...]).astype(BF16).reshape(4, PIECE, width)
        store_out(turn).start()

        @pl.when(turn + 2 < turns)
        def _():
            load_tok(turn + 2).start()

    def pass_on(turn):
        scatter(turn, 0).wait_recv()
        part[turn, down, 0:HALF] = part[turn, down, 0:HALF] + via_across[turn]
        scatter(turn, 5).start()
        scatter(turn, 1).wait_recv()
        part[turn, across, HALF:PIECE] = part[turn, across, HALF:PIECE] + via_down[turn]
        scatter(turn, 4).start()

    def collect(turn):
        for index in range(2, 6):
            scatter(turn, index).wait_recv()
        grad_normed = part[turn, me].astype(F32) + from_across[turn].astype(F32)
        grad_normed = grad_normed + from_down[turn].astype(F32)
        residual = residual_here[turn]
        inverse = lax.rsqrt(jnp.mean(residual * residual, axis=-1, keepdims=True) + EPS_NORM)
        unit = residual * inverse
        scaled = grad_normed * gain[...]
        through = inverse * (scaled - unit * jnp.mean(scaled * unit, axis=-1, keepdims=True))
        grad_residual = up_here[turn, me].astype(F32) + through
        grad_here[turn] = grad_residual
        grad_mixer = grad_residual.astype(BF16)
        mixer_here[turn] = grad_mixer
        for slot, weight in enumerate((w_own, w_across, w_down_hop, w_far)):
            piece = mm_nt(grad_mixer, weight[...]).astype(BF16)
            if slot == 0:
                received[turn, 0] = piece
            else:
                pieces[turn, slot] = piece
                give_back(turn, slot).start()

    def round_of(index, carry):
        @pl.when(index < turns)
        def _():
            forward_and_back(index)

        @pl.when(jnp.logical_and(index >= 1, index <= turns))
        def _():
            pass_on(index - 1)

        @pl.when(index >= 2)
        def _():
            collect(index - 2)

        return carry

    lax.fori_loop(0, turns + 2, round_of, 0)

    tile = weight_stage.shape[2]
    tiles = width // tile

    def store_weight(kind, index, slot):
        return pltpu.make_async_copy(
            weight_stage.at[slot, kind],
            weight_grads.at[kind, pl.ds(index * tile, tile)],
            stage_sem.at[slot, kind],
        )

    all_rows = turns * 4 * PIECE

    def weight_tile(index, carry):
        slot = index % 2
        columns = pl.ds(pl.multiple_of(index * tile, tile), tile)

        @pl.when(index >= 2)
        def _():
            for kind in range(3):
                store_weight(kind, index - 2, slot).wait()

        left = normed[:, :, columns].reshape(all_rows, tile)
        upper = up_here[:, :, :, columns].reshape(all_rows, tile)
        units = hidden.shape[-1]
        for kind, (one, other) in enumerate(
            ((left, grad_gate), (left, grad_up), (upper, hidden))
        ):
            weight_stage[slot, kind] = mm_tn(one, other[...].reshape(all_rows, units)).astype(BF16)
            store_weight(kind, index, slot).start()
        return carry

    lax.fori_loop(0, tiles, weight_tile, 0)
    mixer_rows = mixer_here[...].reshape(turns * PIECE, width)
    dv = gated.shape[-1]
    for slot in range(4):
        if slot == 0:
            blocks = [gated[t // halves, me, t % halves] for t in range(turns)]
        else:
            source = (None, g_across, g_down, g_far)[slot]
            blocks = [source[t, me] for t in range(turns)]
        rows = jnp.concatenate(blocks, axis=0)
        output_stage[slot] = mm_tn(mixer_rows, rows).astype(BF16)

    last = [
        pltpu.make_async_copy(residual_here, own_residual, last_sem.at[0]),
        pltpu.make_async_copy(grad_here, own_grad, last_sem.at[1]),
        pltpu.make_async_copy(output_stage, output_grads, last_sem.at[2]),
    ]
    for copy in last:
        copy.start()
    for turn in range(turns):
        for slot in range(1, 4):
            give_back(turn, slot).wait_recv()
        for slot in range(4):
            source = (me, across, down, far)[slot]
            pltpu.make_async_copy(
                received.at[turn, slot],
                grad_gated.at[turn // halves, source, turn % halves],
                last_sem.at[3 + turn * 4 + slot],
            ).start()
    for turn in range(turns):
        for slot in range(4):
            source = (me, across, down, far)[slot]
            pltpu.make_async_copy(
                received.at[turn, slot],
                grad_gated.at[turn // halves, source, turn % halves],
                last_sem.at[3 + turn * 4 + slot],
            ).wait()
        if turn >= turns - 2:
            store_out(turn).wait()
        for side in range(2):
            direct(turn, side).wait_send()
            relay(turn, side).wait_send()
        for index in range(6):
            scatter(turn, index).wait_send()
        for slot in range(1, 4):
            give_back(turn, slot).wait_send()
    for index in range(max(tiles - 2, 0), tiles):
        for kind in range(3):
            store_weight(kind, index, index % 2).wait()
    for copy in last:
        copy.wait()


def feed_forward(gated, weights, tok, gain, w_gate, w_up, w_down, upstream):
    sequences, length, width = tok.shape
    dv, units = gated.shape[-1], w_gate.shape[1]
    halves = length // 4 // PIECE
    turns = sequences * halves

    def pieces_of(values):
        return values.reshape(sequences, 4, halves, PIECE, values.shape[-1])

    anywhere = pl.BlockSpec(memory_space=pl.ANY)
    vmem = pl.BlockSpec(memory_space=pltpu.VMEM)
    dma = pltpu.SemaphoreType.DMA
    rows = 4 * PIECE
    outs = pl.pallas_call(
        ffn_body,
        in_specs=[vmem] * 5 + [anywhere, vmem] + [anywhere] * 4,
        out_specs=[anywhere] * 6 + [vmem],
        out_shape=[
            shape_of((sequences, 4, halves, PIECE, width), BF16),
            shape_of((3, width, units), BF16),
            shape_of((4, width, dv), BF16),
            shape_of((sequences, 4, halves, PIECE, dv), BF16),
            shape_of((turns, PIECE, width), F32),
            shape_of((turns, PIECE, width), F32),
            shape_of((1, width), F32),
        ],
        scratch_shapes=[
            pltpu.VMEM((turns, 4, PIECE, dv), BF16),
            pltpu.VMEM((turns, 4, PIECE, dv), BF16),
            pltpu.VMEM((turns, 4, PIECE, dv), BF16),
            pltpu.VMEM((2, 4, PIECE, width), BF16),
            pltpu.VMEM((turns, 4, PIECE, width), BF16),
            pltpu.VMEM((width, units), BF16),
            pltpu.VMEM((width, units), BF16),
            pltpu.VMEM((units, width), BF16),
            pltpu.VMEM((turns, rows, width), BF16),
            pltpu.VMEM((turns, rows, units), BF16),
            pltpu.VMEM((turns, rows, units), BF16),
            pltpu.VMEM((turns, rows, units), BF16),
            pltpu.VMEM((2, 4, PIECE, width), BF16),
            pltpu.VMEM((turns, 4, PIECE, width), BF16),
            pltpu.VMEM((turns, HALF, width), BF16),
            pltpu.VMEM((turns, HALF, width), BF16),
            pltpu.VMEM((turns, PIECE, width), BF16),
            pltpu.VMEM((turns, PIECE, width), BF16),
            pltpu.VMEM((turns, PIECE, width), F32),
            pltpu.VMEM((turns, PIECE, width), F32),
            pltpu.VMEM((turns, PIECE, width), BF16),
            pltpu.VMEM((turns, 4, PIECE, dv), BF16),
            pltpu.VMEM((turns, 4, PIECE, dv), BF16),
            pltpu.VMEM((2, 3, 256, units), BF16),
            pltpu.VMEM((4, width, dv), BF16),
            dma((3,)),
            dma((2, turns)),
            dma((4, turns)),
            dma((4, turns)),
            dma((6, turns)),
            dma((6, turns)),
            dma((4, turns)),
            dma((4, turns)),
            dma((turns,)),
            dma((2, 3)),
            dma((3 + 4 * turns,)),
        ],
        compiler_params=pltpu.CompilerParams(
            collective_id=0, has_side_effects=True, vmem_limit_bytes=64 * 2**20
        ),
        cost_estimate=pl.CostEstimate(
            flops=2 * sequences * length * width * (4 * dv + 9 * units),
            bytes_accessed=sequences * length * width * 8,
            transcendentals=0,
        ),
        name="feed_forward",
    )(pieces_of(gated), *weights, pieces_of(tok), gain, w_gate, w_up, w_down, pieces_of(upstream))
    out_part, weight_grads, output_grads, grad_gated, own_residual, own_grad, gain_grad = outs
    return (
        out_part.reshape(sequences, 4, length // 4, width),
        weight_grads,
        output_grads,
        grad_gated.reshape(sequences, length, dv),
        own_residual,
        own_grad,
        gain_grad,
    )


SMALL = 48


def paired_sum(own, received, order):
    terms = [own.astype(F32)] + [received[index].astype(F32) for index in order]
    while len(terms) > 1:
        half = len(terms) // 2
        terms = [terms[index] + terms[index + half] for index in range(half)]
    return terms[0]


def mixer_back_body(
    grad_gated_in, head_in, profile_in, out_gate_in, projected_in, cumulative_in, states_in,
    normed_in, tok_in, residual_in, grad_residual_in, out_part_in, hidden_grads, output_parts,
    w_proj_in, w_gate_in, low_rank, halo, taps_in, rank_up, bias, w_rank, before, entering,
    decays, head_gain, mixer_gain, channel_part, lengths,
    output, token_grads, hidden_out, mixer_out, small_local, small_shared,
    grad_gated, head, profile, out_gate, projected, cumulative, states, normed, tok, residual,
    grad_residual, part, w_proj, w_gate,
    hidden_kept, hidden_seq, hidden_dp, output_kept, output_seq, output_mp, output_dp,
    f_via_across, f_via_down, f_across, f_down, g_via_across, g_via_down, g_across, g_down,
    grad_out_gate, grad_head, grad_projected, grad_low_rank, mixer_grad, mixer_seq, mixer_dp,
    state_grad, state_seq, upstream, extended, grad_extended, edge_out, edge_in,
    small, small_low, small_seq, small_dp, small_mp, out_stage,
    load_sem, seq_send, seq_recv, dp_send, dp_recv, mp_send, mp_recv, f_send, f_recv,
    g_send, g_recv, store_sem,
):
    sequences, length, dv = grad_gated.shape
    width = normed.shape[-1]
    rank, dk = rank_up.shape
    c3 = projected.shape[-1]
    halves = 2
    turns = sequences * halves
    MESH = pl.DeviceIdType.MESH
    me, side, place = lax.axis_index("mp"), lax.axis_index("seq"), lax.axis_index("dp")
    sides, places = lax.axis_size("seq"), lax.axis_size("dp")
    across = me + 1 - 2 * (me % 2)
    down = (me + 2) % 4
    far = 3 - me
    share_rows = width // sides
    shard_rows = share_rows // places
    steps = length // STEP
    per_step = STEP // CHUNK
    first, second = pl.ds(0, HALF), pl.ds(HALF, HALF)

    def remote(source, target, send, recv, axis, device):
        return pltpu.make_async_remote_copy(
            src_ref=source,
            dst_ref=target,
            send_sem=send,
            recv_sem=recv,
            device_id={axis: device},
            device_id_type=MESH,
        )


    loads = [
        pltpu.make_async_copy(source, target, load_sem.at[index])
        for index, (source, target) in enumerate(
            [
                (grad_gated_in, grad_gated),
                (head_in, head),
                (profile_in, profile),
                (out_gate_in, out_gate),
                (out_part_in, part),
                (hidden_grads.at[:, pl.ds(side * share_rows, share_rows)], hidden_kept),
                (output_parts.at[:, pl.ds(side * share_rows, share_rows)], output_kept),
                (normed_in, normed),
                (projected_in, projected),
                (cumulative_in, cumulative),
                (states_in, states),
                (residual_in, residual),
                (w_proj_in, w_proj),
                (w_gate_in, w_gate),
                (grad_residual_in, grad_residual),
                (tok_in.at[:, me], tok),
            ]
        )
    ]

    def to_sides(kind, source_of, target):
        copies = []
        for hop in range(1, sides):
            peer = (side + hop) % sides
            copies.append(
                remote(
                    source_of(peer),
                    target.at[hop - 1],
                    seq_send.at[kind, hop - 1],
                    seq_recv.at[kind, hop - 1],
                    "seq",
                    peer,
                )
            )
        return copies

    def to_places(kind, source_of, target):
        copies = []
        for hop in range(1, places):
            peer = (place + hop) % places
            copies.append(
                remote(
                    source_of(peer),
                    target.at[hop - 1],
                    dp_send.at[kind, hop - 1],
                    dp_recv.at[kind, hop - 1],
                    "dp",
                    peer,
                )
            )
        return copies

    def to_heads(kind, source_of, target):
        return [
            remote(
                source_of(slot),
                target.at[slot - 1],
                mp_send.at[kind, slot - 1],
                mp_recv.at[kind, slot - 1],
                "mp",
                (me, across, down, far)[slot],
            )
            for slot in range(1, 4)
        ]

    def share_of(ref):
        return lambda peer: ref.at[:, pl.ds(peer * share_rows, share_rows)]

    def shard_of(ref):
        return lambda peer: ref.at[:, pl.ds(peer * shard_rows, shard_rows)]

    hidden_to_sides = to_sides(0, share_of(hidden_grads), hidden_seq)
    output_to_sides = to_sides(1, share_of(output_parts), output_seq)
    state_to_sides = to_sides(2, lambda peer: state_grad, state_seq)
    mixer_to_sides = to_sides(
        3, lambda peer: mixer_grad.at[pl.ds(peer * share_rows, share_rows)], mixer_seq
    )
    small_to_sides = to_sides(4, lambda peer: small_low.at[0], small_seq)
    edge_copy = remote(
        edge_out,
        edge_in,
        seq_send.at[5, 0],
        seq_recv.at[5, 0],
        "seq",
        (side + sides - 1) % sides,
    )
    hidden_to_places = to_places(0, shard_of(hidden_kept), hidden_dp)

    def own_share(peer):
        return pl.ds(pl.multiple_of(side * share_rows + peer * shard_rows, 16), shard_rows)

    mixer_to_places = to_places(1, lambda peer: mixer_grad.at[own_share(peer)], mixer_dp)
    output_to_places = to_places(
        2, lambda peer: output_kept.at[0, pl.ds(peer * shard_rows, shard_rows)], output_dp
    )
    small_to_places = to_places(3, lambda peer: small_low.at[1], small_dp)
    output_to_heads = to_heads(0, lambda slot: output_kept.at[slot], output_mp)
    small_to_heads = to_heads(1, lambda slot: small_low.at[2], small_mp)

    def scatter(turn, index, forward):
        if forward:
            via_across, via_down, from_across, from_down = (
                f_via_across, f_via_down, f_across, f_down,
            )
            send, recv = f_send, f_recv
        else:
            via_across, via_down, from_across, from_down = (
                g_via_across, g_via_down, g_across, g_down,
            )
            send, recv = g_send, g_recv
        s, h = turn // halves, turn % halves
        low, high = pl.ds(h * PIECE, HALF), pl.ds(h * PIECE + HALF, HALF)
        source, target, device = (
            (part.at[s, far, low], via_across.at[turn], across),
            (part.at[s, far, high], via_down.at[turn], down),
            (part.at[s, across, low], from_across.at[turn, first], across),
            (part.at[s, down, high], from_down.at[turn, second], down),
            (part.at[s, across, high], from_across.at[turn, second], across),
            (part.at[s, down, low], from_down.at[turn, first], down),
        )[index]
        return remote(source, target, send.at[index, turn], recv.at[index, turn], "mp", device)

    def pass_on(turn, forward):
        via_across, via_down = (
            (f_via_across, f_via_down) if forward else (g_via_across, g_via_down)
        )
        s, h = turn // halves, turn % halves
        low = pl.ds(h * PIECE, HALF)
        high = pl.ds(h * PIECE + HALF, HALF)
        scatter(turn, 0, forward).wait_recv()
        part[s, down, low] = part[s, down, low] + via_across[turn]
        scatter(turn, 5, forward).start()
        scatter(turn, 1, forward).wait_recv()
        part[s, across, high] = part[s, across, high] + via_down[turn]
        scatter(turn, 4, forward).start()

    def summed(turn, forward):
        from_across, from_down = (f_across, f_down) if forward else (g_across, g_down)
        for index in range(2, 6):
            scatter(turn, index, forward).wait_recv()
        s, h = turn // halves, turn % halves
        total = part[s, me, h * PIECE : (h + 1) * PIECE].astype(F32)
        return total + from_across[turn].astype(F32) + from_down[turn].astype(F32)

    def store(turn, kind):
        source, target = ((out_stage, output), (grad_residual, token_grads))[kind]
        return pltpu.make_async_copy(source.at[turn], target.at[turn], store_sem.at[kind, turn])


    barrier = pltpu.get_barrier_semaphore()
    for copy in loads:
        copy.start()
    for axis, peers in (
        ("seq", [(side + hop) % sides for hop in range(1, sides)]),
        ("mp", [across, down, far]),
        ("dp", [(place + hop) % places for hop in range(1, places)]),
    ):
        for peer in peers:
            pl.semaphore_signal(barrier, inc=1, device_id={axis: peer}, device_id_type=MESH)
    small[...] = jnp.zeros_like(small)
    state_grad[...] = jnp.zeros_like(state_grad)
    small[33:34, :] = channel_part[...]
    pl.semaphore_wait(barrier, sides - 1 + 3 + places - 1)
    for copy in hidden_to_sides + output_to_sides:
        copy.start()
    loads[4].wait()
    for turn in range(turns):
        for index in range(2):
            scatter(turn, index, True).start()
    for copy in loads[0:4]:
        copy.wait()


    scale = dk ** (-0.5)

    def ungate(index, carry):
        rows = pl.ds(pl.multiple_of(index * STEP, STEP), STEP)
        for s in range(sequences):
            upper = grad_gated[s, rows, :].astype(F32)
            head_rows_here = head[s, rows, :].astype(F32)
            inverse = lax.rsqrt(
                jnp.mean(head_rows_here * head_rows_here, axis=-1, keepdims=True) + EPS_HEAD
            )
            unit = head_rows_here * inverse
            logits = out_gate[s, rows, :].astype(F32)
            share = sigmoid(logits)
            slope = share * (1.0 + logits * (1.0 - share))
            grad_out_gate[s, rows, :] = (upper * unit * head_gain[...] * slope).astype(BF16)
            grad_normed = upper * (logits * share)
            small[34:35, :dv] += jnp.sum(grad_normed * unit, axis=0, keepdims=True)
            scaled = grad_normed * head_gain[...]
            through = inverse * (scaled - unit * jnp.mean(scaled * unit, axis=-1, keepdims=True))
            rounded = (through * scale).astype(BF16)
            grad_head[s, rows, :] = rounded
            state_grad[s] += mm_tn(rounded, profile[s, rows, :])
        return carry

    lax.fori_loop(0, steps, ungate, 0)
    for copy in state_to_sides:
        copy.start()
    for turn in range(turns):
        for index in range(2, 4):
            scatter(turn, index, True).start()
    loads[5].wait()
    for copy in hidden_to_sides:
        copy.wait_recv()
    hidden_sum = hidden_kept[...]
    for hop in range(sides - 1):
        hidden_sum = hidden_sum + hidden_seq[hop]
    hidden_kept[...] = hidden_sum
    for copy in hidden_to_places:
        copy.start()
    loads[6].wait()
    for copy in output_to_sides:
        copy.wait_recv()
    output_sum = output_kept[...]
    for hop in range(sides - 1):
        output_sum = output_sum + output_seq[hop]
    output_kept[...] = output_sum
    for copy in output_to_heads:
        copy.start()
    for copy in loads[7:11]:
        copy.wait()
    for copy in state_to_sides:
        copy.wait_recv()
    total = jnp.zeros_like(upstream)
    for ahead in range(sides - 1, 0, -1):
        source = side + ahead
        decay = decays[source % sides]
        longer = state_seq[sides - ahead - 1] + jnp.exp(decay) * total
        total = jnp.where(source < sides, longer, total)
    upstream[...] = total
    grad_extended[:, STEP : STEP + 8, :] = jnp.zeros_like(grad_extended[:, STEP : STEP + 8, :])


    taps = taps_in[...]
    causal = triangle(True)

    def backward_step(back, carry):
        step = steps - 1 - back
        start = pl.multiple_of(step * STEP, STEP)

        @pl.when(back > 0)
        def _():
            grad_extended[:, STEP : STEP + 8, :] = grad_extended[:, 0:8, :]

        @pl.when(step == 0)
        def _():
            extended[:, 0:8, :] = halo[...]

        @pl.when(step > 0)
        def _():
            earlier = projected[:, pl.ds(pl.multiple_of(jnp.maximum(start - 16, 0), 16), 16), :]
            extended[:, 0:8, :] = earlier.astype(F32)[:, 8:16, :]

        for s in range(sequences):
            here = pl.ds(start, STEP)
            extended[s, 8 : 8 + STEP, :] = projected[s, here, :].astype(F32)
            filtered = filter_rows(extended.at[s], taps, STEP)
            share = sigmoid(filtered)
            convolved = (filtered * share).astype(BF16)
            slope = share * (1.0 + filtered * (1.0 - share))
            low_rows = low_rank[s, here, :]
            logit = mm(low_rows, rank_up[...]) + bias[...]
            logit_grads = [None] * per_step
            for piece in reversed(range(per_step)):
                rows = slice(piece * CHUNK, (piece + 1) * CHUNK)
                there = pl.ds(start + piece * CHUNK, CHUNK)
                queries = convolved[rows, :dk].astype(F32)
                keys = convolved[rows, dk : 2 * dk].astype(F32)
                values = convolved[rows, 2 * dk :]
                grad_rows = grad_head[s, there, :]
                total = cumulative[s, there, :]
                middle, last = total[CHUNK // 2 - 1 : CHUNK // 2], total[CHUNK - 1 : CHUNK]
                lift, lower = jnp.exp(total - middle), jnp.exp(middle - total)
                inner, outer = jnp.exp(total), jnp.exp(last - total)
                whole_decay = jnp.exp(last)
                lifted, lowered = (queries * lift).astype(BF16), (keys * lower).astype(BF16)
                inside, tails = (queries * inner).astype(BF16), (keys * outer).astype(BF16)
                previous = before[s, pl.ds(step * per_step + piece, 1), :]
                state = states[s, step * per_step + piece].astype(F32)
                state = state + entering[s] * jnp.exp(previous)
                scores = jnp.where(causal, mm_nt(lifted, lowered), 0.0).astype(BF16)
                grad_scores = jnp.where(causal, mm_nt(grad_rows, values), 0.0).astype(BF16)
                later = upstream[s]
                later_low = later.astype(BF16)
                grad_values = mm_tn(scores, grad_rows) + mm_nt(tails, later_low)
                grad_lifted = mm(grad_scores, lowered)
                grad_lowered = mm_tn(grad_scores, lifted)
                grad_inside = mm(grad_rows, state.astype(BF16))
                grad_tails = mm(values, later_low)
                upstream[s] = later * whole_decay + mm_tn(grad_rows, inside)
                tail_terms = tails.astype(F32) * grad_tails
                grad_total = (
                    lifted.astype(F32) * grad_lifted
                    - lowered.astype(F32) * grad_lowered
                    + inside.astype(F32) * grad_inside
                    - tail_terms
                )
                grad_last = jnp.sum(tail_terms, axis=0, keepdims=True) + whole_decay * jnp.sum(
                    later * state, axis=0, keepdims=True
                )
                grad_decay = running_sum(grad_total, False) + grad_last
                logit_grads[piece] = grad_decay / GATE_NORMALIZER * sigmoid(-logit[rows])
                grad_extended[s, rows, :dk] = (
                    grad_lifted * lift + grad_inside * inner
                ) * slope[rows, :dk]
                grad_extended[s, rows, dk : 2 * dk] = (
                    grad_lowered * lower + grad_tails * outer
                ) * slope[rows, dk : 2 * dk]
                grad_extended[s, rows, 2 * dk :] = grad_values * slope[rows, 2 * dk :]
            logit_grad = jnp.concatenate(logit_grads, axis=0)
            logit_low = logit_grad.astype(BF16)
            small[35:36, :dk] += jnp.sum(logit_grad, axis=0, keepdims=True)
            small[16 : 16 + rank, :dk] += mm_tn(low_rows, logit_low)
            grad_low_rank[s, here, :] = mm_nt(logit_low, rank_up[...]).astype(BF16)
            total_rows = taps[EDGE : EDGE + 1, :] * grad_extended[s, 0:STEP, :]
            for offset in range(EDGE):
                total_rows = total_rows + taps[offset : offset + 1, :] * grad_extended[
                    s, pl.ds(EDGE - offset, STEP), :
                ]
            grad_projected[s, here, :] = total_rows.astype(BF16)
            grad_filtered = grad_extended[s, 0:STEP, :]
            for offset in range(CONV):
                small[16 + offset : 17 + offset, dk : dk + c3] += jnp.sum(
                    grad_filtered * extended[s, pl.ds(8 - EDGE + offset, STEP), :],
                    axis=0,
                    keepdims=True,
                )
        for turn in range(turns):

            @pl.when(back == turn % steps)
            def _():
                pass_on(turn, True)

        return carry

    lax.fori_loop(0, steps, backward_step, 0)


    edge_out[...] = jnp.zeros_like(edge_out)
    for s in range(sequences):
        rows = grad_extended[s, 0:8, :]
        for i in range(EDGE):
            edge_row = taps[0:1] * rows[i : i + 1]
            for j in range(1, i + 1):
                edge_row = edge_row + taps[j : j + 1] * rows[i - j : i - j + 1]
            edge_out[s, 16 - EDGE + i : 17 - EDGE + i, :] = edge_row
    edge_copy.start()


    loads[11].wait()
    for turn in range(turns):
        s, h = turn // halves, turn % halves
        total = residual[turn] + summed(turn, True)
        position = side * length + me * (length // 4) + h * PIECE
        position = position + lax.broadcasted_iota(jnp.int32, (PIECE, 1), 0)
        out_stage[turn] = jnp.where(position < lengths[s : s + 1, 0:1], total, 0.0).astype(BF16)
        store(turn, 0).start()
    for turn in range(turns):
        for index in range(6):
            scatter(turn, index, True).wait_send()
    edge_copy.wait_recv()
    for s in range(sequences):
        tail = grad_projected[s, length - 16 :, :].astype(F32)
        tail = tail + jnp.where(side < sides - 1, edge_in[s], 0.0)
        grad_projected[s, length - 16 :, :] = tail.astype(BF16)


    loads[12].wait()
    loads[13].wait()

    def input_grad(turn):
        s, h = turn // halves, turn % halves
        quarter = length // 4

        def rows_of_turn(ref):
            blocks = [
                ref[s, q * quarter + h * PIECE : q * quarter + (h + 1) * PIECE, :]
                for q in range(4)
            ]
            return jnp.concatenate(blocks, axis=0)

        total = mm_nt(rows_of_turn(grad_projected), w_proj[...])
        total = total + mm_nt(rows_of_turn(grad_out_gate), w_gate[...])
        total = total + mm_nt(rows_of_turn(grad_low_rank), w_rank[...])
        rounded = total.astype(BF16)
        for q in range(4):
            part[s, q, h * PIECE : (h + 1) * PIECE] = rounded[q * PIECE : (q + 1) * PIECE]
        for index in range(4):
            scatter(turn, index, False).start()
        small[32:33, :] += jnp.sum(
            total * rows_of_turn(normed).astype(F32), axis=0, keepdims=True
        )

    for turn in range(turns):
        input_grad(turn)


    flat = sequences * length
    tile = 256

    def weight_tile(index, carry):
        columns = pl.ds(pl.multiple_of(index * tile, tile), tile)
        left = normed[:, :, columns].reshape(flat, tile)
        mixer_grad[columns, :c3] = mm_tn(left, grad_projected[...].reshape(flat, c3)).astype(BF16)
        mixer_grad[columns, c3:] = mm_tn(left, grad_out_gate[...].reshape(flat, dv)).astype(BF16)
        small[0:rank, columns] = mm_tn(grad_low_rank[...].reshape(flat, rank), left)
        return carry

    lax.fori_loop(0, width // tile, weight_tile, 0)
    small_low[0] = small[...].astype(BF16)
    for copy in small_to_sides + mixer_to_sides:
        copy.start()
    pass_on(0, False)
    for copy in output_to_heads:
        copy.wait_recv()
    output_kept[0] = output_kept[0] + output_mp[0] + output_mp[1] + output_mp[2]
    for copy in output_to_places:
        copy.start()
    for copy in small_to_sides:
        copy.wait_recv()
    small_low[1] = paired_sum(small_low[0], small_seq, range(sides - 1)).astype(BF16)
    for copy in small_to_places:
        copy.start()
    for copy in mixer_to_sides:
        copy.wait_recv()
    own = pl.ds(pl.multiple_of(side * share_rows, 16), share_rows)
    mixer_sum = mixer_grad[own, :]
    for hop in range(sides - 1):
        mixer_sum = mixer_sum + mixer_seq[hop]
    mixer_grad[own, :] = mixer_sum
    for copy in mixer_to_places:
        copy.start()
    pass_on(1, False)
    for copy in small_to_places:
        copy.wait_recv()
    summed_here = paired_sum(small_low[1], small_dp, range(places - 1))
    small_local[...] = summed_here
    small_low[2] = summed_here.astype(BF16)
    for copy in small_to_heads:
        copy.start()
    pass_on(2, False)
    for copy in hidden_to_places:
        copy.wait_recv()
    own_shard = pl.ds(pl.multiple_of(place * shard_rows, 16), shard_rows)
    for kind in range(3):
        total = hidden_kept[kind, own_shard, :].astype(F32)
        for hop in range(places - 1):
            total = total + hidden_dp[hop, kind].astype(F32)
        hidden_out[kind] = total
    pass_on(3, False)


    loads[14].wait()
    loads[15].wait()
    for turn in range(turns):
        s, h = turn // halves, turn % halves
        grad_normed = summed(turn, False)
        rows = tok[s, h * PIECE : (h + 1) * PIECE].astype(F32)
        inverse = lax.rsqrt(jnp.mean(rows * rows, axis=-1, keepdims=True) + EPS_NORM)
        unit = rows * inverse
        scaled = grad_normed * mixer_gain[...]
        through = inverse * (scaled - unit * jnp.mean(scaled * unit, axis=-1, keepdims=True))
        grad_residual[turn] = grad_residual[turn] + through
        store(turn, 1).start()
    for copy in small_to_heads:
        copy.wait_recv()
    small_shared[...] = paired_sum(small_low[2], small_mp, (1, 0, 2))
    for copy in mixer_to_places + output_to_places:
        copy.wait_recv()
    total = mixer_grad[own_share(place), :].astype(F32)
    for hop in range(places - 1):
        total = total + mixer_dp[hop].astype(F32)
    mixer_out[:, : c3 + dv] = total
    total = output_kept[0, own_shard, :].astype(F32)
    for hop in range(places - 1):
        total = total + output_dp[hop].astype(F32)
    mixer_out[:, c3 + dv :] = total


    for copies in (
        hidden_to_sides, output_to_sides, state_to_sides, mixer_to_sides, small_to_sides,
        [edge_copy], hidden_to_places, mixer_to_places, output_to_places, small_to_places,
        output_to_heads, small_to_heads,
    ):
        for copy in copies:
            copy.wait_send()
    for turn in range(turns):
        for index in range(6):
            scatter(turn, index, False).wait_send()
        store(turn, 0).wait()
        store(turn, 1).wait()


def mixer_back(
    grad_gated, head, profile, out_gate, projected, cumulative, states, normed, tok, residual,
    grad_residual, out_part, hidden_grads, output_parts, w_proj, w_gate, low_rank, halo, taps,
    rank_up, bias, w_rank, before, entering, decays, head_gain, mixer_gain, channel_part, lengths,
    seq_count, dp_count,
):
    sequences, length, width = normed.shape
    dv, c3 = grad_gated.shape[-1], projected.shape[-1]
    rank, dk = rank_up.shape
    units = hidden_grads.shape[-1]
    quarter = length // 4
    turns = sequences * quarter // PIECE
    share_rows = width // seq_count
    shard_rows = share_rows // dp_count
    peers, others = seq_count - 1, dp_count - 1
    anywhere = pl.BlockSpec(memory_space=pl.ANY)
    vmem = pl.BlockSpec(memory_space=pltpu.VMEM)
    dma = pltpu.SemaphoreType.DMA

    def low(*shape):
        return pltpu.VMEM(shape, BF16)

    def full(*shape):
        return pltpu.VMEM(shape, F32)

    hops = [
        low(turns, HALF, width),
        low(turns, HALF, width),
        low(turns, PIECE, width),
        low(turns, PIECE, width),
    ]
    return pl.pallas_call(
        mixer_back_body,
        in_specs=[anywhere] * 16 + [vmem] * 13,
        out_specs=[anywhere] * 2 + [vmem] * 4,
        out_shape=[
            shape_of((turns, PIECE, width), BF16),
            shape_of((turns, PIECE, width), F32),
            shape_of((3, shard_rows, units), F32),
            shape_of((shard_rows, c3 + 2 * dv), F32),
            shape_of((SMALL, width), F32),
            shape_of((SMALL, width), F32),
        ],
        scratch_shapes=[
            low(sequences, length, dv),
            low(sequences, length, dv),
            low(sequences, length, dk),
            low(sequences, length, dv),
            low(sequences, length, c3),
            full(sequences, length, dk),
            low(sequences, length // CHUNK, dv, dk),
            low(sequences, length, width),
            low(sequences, quarter, width),
            full(turns, PIECE, width),
            full(turns, PIECE, width),
            low(sequences, 4, quarter, width),
            low(width, c3),
            low(width, dv),
            low(3, share_rows, units),
            low(peers, 3, share_rows, units),
            low(others, 3, shard_rows, units),
            low(4, share_rows, dv),
            low(peers, 4, share_rows, dv),
            low(3, share_rows, dv),
            low(others, shard_rows, dv),
            *hops,
            *hops,
            low(sequences, length, dv),
            low(sequences, length, dv),
            low(sequences, length, c3),
            low(sequences, length, rank),
            low(width, c3 + dv),
            low(peers, share_rows, c3 + dv),
            low(others, shard_rows, c3 + dv),
            full(sequences, dv, dk),
            full(peers, sequences, dv, dk),
            full(sequences, dv, dk),
            full(sequences, STEP + 8, c3),
            full(sequences, STEP + 8, c3),
            full(sequences, 16, c3),
            full(sequences, 16, c3),
            full(SMALL, width),
            low(3, SMALL, width),
            low(peers, SMALL, width),
            low(others, SMALL, width),
            low(3, SMALL, width),
            low(turns, PIECE, width),
            dma((16,)),
            dma((6, peers)),
            dma((6, peers)),
            dma((4, others)),
            dma((4, others)),
            dma((2, 3)),
            dma((2, 3)),
            dma((6, turns)),
            dma((6, turns)),
            dma((6, turns)),
            dma((6, turns)),
            dma((2, turns)),
        ],
        compiler_params=pltpu.CompilerParams(
            collective_id=1, has_side_effects=True, vmem_limit_bytes=64 * 2**20
        ),
        cost_estimate=pl.CostEstimate(
            flops=2 * sequences * length * width * 2 * (c3 + dv) * 2,
            bytes_accessed=sequences * length * width * 16,
            transcendentals=0,
        ),
        name="mixer_back",
    )(
        grad_gated, head, profile, out_gate, projected, cumulative, states, normed, tok, residual,
        grad_residual, out_part, hidden_grads, output_parts, w_proj, w_gate, low_rank, halo, taps,
        rank_up, bias, w_rank, before, entering, decays, head_gain, mixer_gain, channel_part,
        lengths,
    )


ACROSS = [(i, i ^ 1) for i in range(4)]
DOWN = [(i, i ^ 2) for i in range(4)]


def gather_relative(block):
    half = block.shape[0] // 2
    across = lax.ppermute(block, "mp", ACROSS)
    down = lax.ppermute(block, "mp", DOWN)
    first = lax.ppermute(across[:half], "mp", DOWN)
    second = lax.ppermute(down[half:], "mp", ACROSS)
    return [block, across, down, jnp.concatenate([first, second], axis=0)]


def passed_along(block, axis, distance):
    devices = range(lax.axis_size(axis))
    route = [(i - distance, i) for i in devices if i - distance in devices]
    return lax.ppermute(block, axis, route)


def chain_states(decay, state, backward):
    count, mine = lax.axis_size("seq"), lax.axis_index("seq")
    if count == 2:
        return passed_along(state, "seq", -1 if backward else 1)
    decays, states = lax.all_gather(decay, "seq"), lax.all_gather(state, "seq")
    if backward:
        decays, states, mine = decays[::-1], states[::-1], count - 1 - mine

    def hop(position, subtotal):
        longer = subtotal * jnp.exp(decays[position]) + states[position]
        return jnp.where(position < mine, longer, subtotal)

    return lax.fori_loop(0, count - 1, hop, jnp.zeros_like(state))


def on_device(
    tokens, lengths, mixer_gain, project_weight, filter_weight, rank_down, rank_up, decay_bias,
    gate_weight, head_gain, output_weight, channel_gain, hidden_gate, hidden_up, hidden_down,
    cotangent,
):
    length, sequences, width = tokens.shape
    shards = lax.axis_size("seq") * lax.axis_size("dp")
    shard = lax.axis_index("seq") * lax.axis_size("dp") + lax.axis_index("dp")
    me = lax.axis_index("mp")
    own_rows = length // lax.axis_size("mp")
    w_proj = project_weight[:, 0]
    taps = filter_weight[:, 0].astype(F32)
    rank_up_here = rank_up[:, 0]
    bias = decay_bias.astype(F32)
    mixer_gain_f = mixer_gain.astype(F32)[None]
    channel_gain_f = channel_gain.astype(F32)[None]
    head_gain_f = head_gain.astype(F32)[None]
    dv = gate_weight.shape[1]
    places = jnp.concatenate(
        [lengths.astype(jnp.int32), (lax.axis_index("seq") * length).astype(jnp.int32).reshape(1)]
    )

    edge_tokens = passed_along(tokens[length - EDGE :], "seq", 1)
    edge_f = edge_tokens.astype(F32)
    edge_inverse = lax.rsqrt(jnp.mean(edge_f * edge_f, axis=-1, keepdims=True) + EPS_NORM)
    edge_normed = (edge_f * edge_inverse * mixer_gain_f).astype(BF16)
    edge_projected = jnp.einsum(
        "psd,dc->spc", edge_normed, w_proj, preferred_element_type=F32
    ).astype(BF16)
    halo = jnp.pad(edge_projected.astype(F32), ((0, 0), (8 - EDGE, 0), (0, 0)))

    output_weights = gather_relative(output_weight)
    tok, upstream, normed, projected, out_gate, low_rank = project(
        places,
        tokens.reshape(length * sequences, width),
        cotangent.reshape(length * sequences, width),
        sequences,
        mixer_gain_f,
        w_proj,
        gate_weight,
        rank_down,
    )
    head_local, query_profile, cumulative, states, before, end_state, total_decay = forward_mix(
        projected, halo, low_rank, taps, rank_up_here, bias, dv
    )
    entering = chain_states(total_decay, end_state, False)
    gated, head = gate(head_local, query_profile, entering, out_gate, head_gain_f)
    (
        out_part, hidden_grads, output_parts, grad_gated, residual, grad_residual,
        channel_gain_part,
    ) = feed_forward(
        gated, output_weights, tok, channel_gain_f, hidden_gate, hidden_up, hidden_down, upstream
    )
    count = lax.axis_size("seq")
    if count > 2:
        decays = lax.all_gather(total_decay, "seq")
    else:
        decays = jnp.zeros((count, *total_decay.shape), F32)
    outputs, token_grads, hidden_sums, mixer_sums, small, shared = mixer_back(
        grad_gated, head, query_profile, out_gate, projected, cumulative, states, normed,
        tok.reshape(sequences, 4, own_rows, width), residual, grad_residual, out_part,
        hidden_grads, output_parts, w_proj, gate_weight, low_rank, halo, taps, rank_up_here, bias,
        rank_down, before, entering, decays, head_gain_f, mixer_gain_f, channel_gain_part,
        jnp.broadcast_to(lengths.astype(jnp.int32)[:, None], (sequences, 128)),
        count, lax.axis_size("dp"),
    )
    c3, (rank, _, dk) = w_proj.shape[1], rank_up.shape

    def own(values):
        size = values.shape[-1] // shards
        return lax.dynamic_slice_in_dim(values, shard * size, size, values.ndim - 1)

    own_shape = (sequences, own_rows, width)
    return (
        outputs.reshape(own_shape).swapaxes(0, 1),
        token_grads.reshape(own_shape).swapaxes(0, 1),
        shared[32] / mixer_gain_f[0],
        mixer_sums[:, None, :c3],
        own(small[16 : 16 + CONV, dk : dk + c3])[:, None],
        shared[:rank].T,
        own(small[16 : 16 + rank, :dk])[:, None],
        own(small[35:36, :dk]),
        mixer_sums[:, c3 : c3 + dv],
        shared[34, :dv],
        mixer_sums[:, c3 + dv :].T,
        shared[33],
        hidden_sums[0],
        hidden_sums[1],
        hidden_sums[2].T,
    )


def solution(mesh):
    in_specs = (
        P("seq", "dp", None),
        P("dp"),
        P(),
        P(None, "mp", None),
        P(None, "mp", None),
        P(),
        P(None, "mp", None),
        P("mp", None),
        P(None, "mp"),
        P(),
        P("mp", None),
        P(),
        P(None, "mp"),
        P(None, "mp"),
        P("mp", None),
        P("seq", "dp", None),
    )
    out_specs = (
        P(("seq", "mp"), "dp", None),
        P(("seq", "mp"), "dp", None),
        P(),
        P(("seq", "dp"), "mp", None),
        P(None, "mp", ("seq", "dp")),
        P(),
        P(None, "mp", ("seq", "dp")),
        P("mp", ("seq", "dp")),
        P(("seq", "dp"), "mp"),
        P(),
        P("mp", ("seq", "dp")),
        P(),
        P(("seq", "dp"), "mp"),
        P(("seq", "dp"), "mp"),
        P("mp", ("seq", "dp")),
    )
    return jax.shard_map(
        on_device, mesh=mesh, in_specs=in_specs, out_specs=out_specs, check_vma=False
    )
```

```python
import jax
import jax.numpy as jnp
from jax import lax
from jax.experimental import pallas as pl
from jax.experimental.pallas import tpu as pltpu
from jax.sharding import PartitionSpec as P

CONV = 4
EDGE = CONV - 1
CHUNK = 128
STEP = 256
EPS_NORM = 1e-06
EPS_HEAD = 1e-05
GATE_NORMALIZER = 16.0
BF16 = jnp.bfloat16
F32 = jnp.float32
VMEM_LIMIT = 56 * 2**20


def mm(left, right):
    return lax.dot_general(left, right, (((1,), (0,)), ((), ())), preferred_element_type=F32)


def mm_nt(left, right):
    return lax.dot_general(left, right, (((1,), (1,)), ((), ())), preferred_element_type=F32)


def mm_tn(left, right):
    return lax.dot_general(left, right, (((0,), (0,)), ((), ())), preferred_element_type=F32)


def sigmoid(values):
    return 1.0 / (1.0 + jnp.exp(-values))


def whole(shape):
    return pl.BlockSpec(shape, lambda *_: (0,) * len(shape))


def shape_of(shape, dtype):
    return jax.ShapeDtypeStruct(shape, dtype)


MIXER_GAIN, CHANNEL_GAIN, HEAD_GAIN, TAPS, BIAS = 0, 1, 2, 3, 7


def triangle(lower):
    row = lax.broadcasted_iota(jnp.int32, (CHUNK, CHUNK), 0)
    column = lax.broadcasted_iota(jnp.int32, (CHUNK, CHUNK), 1)
    return row >= column if lower else row <= column


def running_sums(blocks, lower):
    ones = jnp.where(triangle(lower), 1.0, 0.0).astype(BF16)
    parts = []
    for block in blocks:
        high = block.astype(BF16)
        parts += [high, (block - high.astype(F32)).astype(BF16)]
    sums = mm(ones, jnp.concatenate(parts, axis=1))
    width = blocks[0].shape[1]
    return [
        sums[:, 2 * i * width : (2 * i + 1) * width]
        + sums[:, (2 * i + 1) * width : (2 * i + 2) * width]
        for i in range(len(blocks))
    ]


def causal_pairs(sequences):
    total = sequences * CHUNK
    row = lax.broadcasted_iota(jnp.int32, (total, total), 0)
    column = lax.broadcasted_iota(jnp.int32, (total, total), 1)
    return jnp.logical_and(row // CHUNK == column // CHUNK, row >= column)


def spread(blocks):
    zeros = jnp.zeros_like(blocks[0])
    count = len(blocks)
    return jnp.concatenate(
        [
            jnp.concatenate([blocks[s] if t == s else zeros for t in range(count)], axis=1)
            for s in range(count)
        ],
        axis=0,
    )


def filter_rows(buffer, taps, count):
    total = taps[0:1, :] * buffer[pl.ds(8 - EDGE, count), :]
    for offset in range(1, CONV):
        total = total + taps[offset : offset + 1, :] * buffer[pl.ds(8 - EDGE + offset, count), :]
    return total


def front_body(
    tokens, params, w_proj, w_gate, w_rank, rank_up, edge_source, w_own,
    tok, normed, projected, low_rank, cumulative, states, before, out_gate, profile, gated, head,
    halo, entering, decays, w_others,
    extended, memory, preceding, head_local, edge_in, state_out, state_seq, w_here,
    edge_sem, seq_send, seq_recv, w_send, w_recv, w_store,
):
    step = pl.program_id(0)
    last_step = pl.num_programs(0) - 1
    sequences, size, width = tok.shape
    rank, dk = rank_up.shape
    c3, dv = w_proj.shape[1], w_gate.shape[1]
    per_step = size // CHUNK
    MESH = pl.DeviceIdType.MESH
    me, side, sides = lax.axis_index("mp"), lax.axis_index("seq"), lax.axis_size("seq")
    across = me + 1 - 2 * (me % 2)
    down = (me + 2) % 4
    peers = [(side + hop) % sides for hop in range(1, sides)]
    half = w_own.shape[0] // 2

    def remote(source, target, send, recv, axis, device):
        return pltpu.make_async_remote_copy(
            src_ref=source,
            dst_ref=target,
            send_sem=send,
            recv_sem=recv,
            device_id={axis: device},
            device_id_type=MESH,
        )

    edge_copy = remote(
        edge_source.at[pl.ds(edge_source.shape[0] - 8, 8)],
        edge_in,
        edge_sem.at[0],
        edge_sem.at[1],
        "seq",
        peers[0],
    )
    state_copies = [
        remote(state_out, state_seq.at[i], seq_send.at[i], seq_recv.at[i], "seq", peers[i])
        for i in range(sides - 1)
    ]
    first, second = pl.ds(0, half), pl.ds(half, half)
    weight_copies = [
        remote(w_own, w_here.at[0], w_send.at[0], w_recv.at[0], "mp", across),
        remote(w_own, w_here.at[1], w_send.at[1], w_recv.at[1], "mp", down),
        remote(
            w_here.at[0, first], w_here.at[2, first], w_send.at[2], w_recv.at[2], "mp", down
        ),
        remote(
            w_here.at[1, second], w_here.at[2, second], w_send.at[3], w_recv.at[3], "mp", across
        ),
    ]
    weights_out = pltpu.make_async_copy(w_here, w_others, w_store.at[0])
    barrier = pltpu.get_barrier_semaphore()

    @pl.when(step == 0)
    def _():
        for peer in peers:
            pl.semaphore_signal(barrier, inc=1, device_id={"seq": peer}, device_id_type=MESH)
        for peer in (across, down):
            pl.semaphore_signal(barrier, inc=1, device_id={"mp": peer}, device_id_type=MESH)
        memory[...] = jnp.zeros_like(memory)
        preceding[...] = jnp.zeros_like(preceding)

    @pl.when(step > 0)
    def _():
        extended[:, 0:8, :] = extended[:, size : size + 8, :]

    def first_norm(rows):
        inverse = lax.rsqrt(jnp.mean(rows * rows, axis=-1, keepdims=True) + EPS_NORM)
        return (rows * inverse * params[MIXER_GAIN : MIXER_GAIN + 1, :]).astype(BF16)

    here = jnp.swapaxes(tokens[...], 0, 1)
    tok[...] = here
    rounded = first_norm(here.reshape(sequences * size, width).astype(F32))
    normed[...] = rounded.reshape(sequences, size, width)
    projected_rows = mm(rounded, w_proj[...]).astype(BF16)
    projected[...] = projected_rows.reshape(sequences, size, c3)
    rows_here = pl.ds(pl.multiple_of(step * size, size), size)
    out_gate[:, rows_here, :] = mm(rounded, w_gate[...]).astype(BF16).reshape(sequences, size, dv)
    low_rows = mm_nt(rounded, w_rank[...]).astype(BF16)
    low_rank[...] = low_rows.reshape(sequences, size, rank)

    @pl.when(step == 0)
    def _():
        pl.semaphore_wait(barrier, sides - 1 + 2)
        edge_copy.start()
        for copy in weight_copies[:2]:
            copy.start()
        edge_copy.wait()
        edge = jnp.swapaxes(edge_in[...].astype(F32), 0, 1).reshape(sequences * 8, width)
        edge_rows = mm(first_norm(edge), w_proj[...]).astype(BF16).astype(F32)
        edge_rows = jnp.where(side > 0, edge_rows, 0.0).reshape(sequences, 8, c3)
        extended[:, 0:8, :] = edge_rows
        halo[...] = edge_rows

    @pl.when(step == 1)
    def _():
        for i in range(2):
            weight_copies[i].wait_recv()
            weight_copies[2 + i].start()

    taps = params[TAPS : TAPS + CONV, :c3]
    logit = mm(low_rows, rank_up[...]) + params[BIAS : BIAS + 1, :dk]
    decay = (jnp.minimum(logit, 0.0) - jnp.log1p(jnp.exp(-jnp.abs(logit)))) / GATE_NORMALIZER
    blocks = [
        decay[s * size + p * CHUNK : s * size + (p + 1) * CHUNK]
        for s in range(sequences)
        for p in range(per_step)
    ]
    totals = running_sums(blocks, True)
    convolved = []
    for s in range(sequences):
        rows = projected_rows[s * size : (s + 1) * size]
        extended[s, 8 : 8 + size, :] = rows.astype(F32)
        filtered = filter_rows(extended.at[s], taps, size)
        convolved.append((filtered * sigmoid(filtered)).astype(BF16))
    visible = causal_pairs(sequences)
    for p in range(per_step):
        rows = slice(p * CHUNK, (p + 1) * CHUNK)
        there = pl.ds(pl.multiple_of(step * size + p * CHUNK, CHUNK), CHUNK)
        lifted, lowered, profiles, tails, lasts = [], [], [], [], []
        for s in range(sequences):
            queries = convolved[s][rows, :dk].astype(F32)
            keys = convolved[s][rows, dk : 2 * dk].astype(F32)
            total = totals[s * per_step + p]
            middle, last = total[CHUNK // 2 - 1 : CHUNK // 2], total[CHUNK - 1 : CHUNK]
            lifted.append((queries * jnp.exp(total - middle)).astype(BF16))
            lowered.append((keys * jnp.exp(middle - total)).astype(BF16))
            inside = queries * jnp.exp(total)
            profiles.append(inside.astype(BF16))
            tails.append((keys * jnp.exp(last - total)).astype(BF16))
            lasts.append(last)
            gone = preceding[:, s * dk : (s + 1) * dk]
            profile[s, there, :] = (inside * jnp.exp(gone)).astype(BF16)
            cumulative[s, rows, :] = total
        values = jnp.concatenate([convolved[s][rows, 2 * dk :] for s in range(sequences)], axis=0)
        scores = mm_nt(jnp.concatenate(lifted, axis=0), jnp.concatenate(lowered, axis=0))
        scores = jnp.where(visible, scores, 0.0).astype(BF16)
        entry = memory[...]
        entry_low = entry.astype(BF16)
        states[p] = entry_low
        mixed = mm(scores, values) + mm_nt(spread(profiles), entry_low)
        for s in range(sequences):
            head_local[s, there, :] = mixed[s * CHUNK : (s + 1) * CHUNK]
        last = jnp.concatenate(lasts, axis=1)
        memory[...] = entry * jnp.exp(last) + mm_tn(values, spread(tails))
        before[step * per_step + p] = preceding[...]
        preceding[...] = preceding[...] + last

    @pl.when(step == last_step)
    def _():
        state_out[0:dv, :] = memory[...]
        state_out[dv : dv + 8, :] = jnp.broadcast_to(preceding[...], (8, sequences * dk))
        for copy in state_copies:
            copy.start()
        for copy in weight_copies[2:]:
            copy.wait_recv()
        weights_out.start()
        decays[...] = jnp.zeros_like(decays)
        for copy in state_copies:
            copy.wait_recv()
        total = jnp.zeros_like(memory)
        for behind in range(sides - 1, 0, -1):
            source = side - behind
            gone = state_seq[behind - 1, dv : dv + 1, :]
            decays[(source + sides) % sides] = gone
            longer = state_seq[behind - 1, 0:dv, :] + jnp.exp(gone) * total
            total = jnp.where(source >= 0, longer, total)
        entering[...] = total
        entry_low = total.astype(BF16)
        scale = dk ** (-0.5)

        def gate(index, carry):
            there = pl.ds(pl.multiple_of(index * size, size), size)
            for s in range(sequences):
                rows = head_local[s, there, :]
                rows = rows + mm_nt(profile[s, there, :], entry_low[:, s * dk : (s + 1) * dk])
                rows = rows * scale
                head[s, there, :] = rows.astype(BF16)
                inverse = lax.rsqrt(jnp.mean(rows * rows, axis=-1, keepdims=True) + EPS_HEAD)
                logits = out_gate[s, there, :].astype(F32)
                rows = rows * inverse * params[HEAD_GAIN : HEAD_GAIN + 1, :dv]
                gated[s, there, :] = (rows * (logits * sigmoid(logits))).astype(BF16)
            return carry

        lax.fori_loop(0, last_step + 1, gate, 0)
        edge_sends = state_copies + weight_copies
        for copy in edge_sends:
            copy.wait_send()
        weights_out.wait()


def front(tokens, params, w_proj, w_gate, w_rank, rank_up, w_own, seq_count):
    length, sequences, width = tokens.shape
    c3, dv = w_proj.shape[1], w_gate.shape[1]
    rank, dk = rank_up.shape
    chunks, per_step = length // CHUNK, STEP // CHUNK
    both = sequences * dk
    anywhere = pl.BlockSpec(memory_space=pl.ANY)
    dma = pltpu.SemaphoreType.DMA
    peers = seq_count - 1

    def steps(columns):
        return pl.BlockSpec((sequences, STEP, columns), lambda i: (0, i, 0))

    return pl.pallas_call(
        front_body,
        grid=(length // STEP,),
        in_specs=[
            pl.BlockSpec((STEP, sequences, width), lambda i: (i, 0, 0)),
            whole(params.shape),
            whole(w_proj.shape),
            whole(w_gate.shape),
            whole(w_rank.shape),
            whole(rank_up.shape),
            anywhere,
            anywhere,
        ],
        out_specs=[
            steps(width),
            steps(width),
            steps(c3),
            steps(rank),
            steps(dk),
            pl.BlockSpec((per_step, dv, both), lambda i: (i, 0, 0)),
            whole((chunks, 1, both)),
            whole((sequences, length, dv)),
            whole((sequences, length, dk)),
            whole((sequences, length, dv)),
            whole((sequences, length, dv)),
            whole((sequences, 8, c3)),
            whole((dv, both)),
            whole((seq_count, 1, both)),
            anywhere,
        ],
        out_shape=[
            shape_of((sequences, length, width), BF16),
            shape_of((sequences, length, width), BF16),
            shape_of((sequences, length, c3), BF16),
            shape_of((sequences, length, rank), BF16),
            shape_of((sequences, length, dk), F32),
            shape_of((chunks, dv, both), BF16),
            shape_of((chunks, 1, both), F32),
            shape_of((sequences, length, dv), BF16),
            shape_of((sequences, length, dk), BF16),
            shape_of((sequences, length, dv), BF16),
            shape_of((sequences, length, dv), BF16),
            shape_of((sequences, 8, c3), F32),
            shape_of((dv, both), F32),
            shape_of((seq_count, 1, both), F32),
            shape_of((3, *w_own.shape), BF16),
        ],
        scratch_shapes=[
            pltpu.VMEM((sequences, STEP + 8, c3), F32),
            pltpu.VMEM((dv, both), F32),
            pltpu.VMEM((1, both), F32),
            pltpu.VMEM((sequences, length, dv), F32),
            pltpu.VMEM((8, sequences, width), BF16),
            pltpu.VMEM((dv + 8, both), F32),
            pltpu.VMEM((peers, dv + 8, both), F32),
            pltpu.VMEM((3, *w_own.shape), BF16),
            dma((2,)),
            dma((peers,)),
            dma((peers,)),
            dma((4,)),
            dma((4,)),
            dma((1,)),
        ],
        compiler_params=pltpu.CompilerParams(
            dimension_semantics=("arbitrary",),
            collective_id=2,
            has_side_effects=True,
            vmem_limit_bytes=VMEM_LIMIT,
        ),
        cost_estimate=pl.CostEstimate(
            flops=2 * sequences * length * width * (c3 + dv + 128),
            bytes_accessed=sequences * length * width * 8,
            transcendentals=0,
        ),
        name="front",
    )(tokens, params, w_proj, w_gate, w_rank, rank_up, tokens, w_own)


PIECE = 128
HALF = PIECE // 2


def ffn_body(
    gated, w_own, w_others, tok, params, w_gate, w_up, w_down, cotangent,
    out_part, weight_grads, output_grads, grad_gated, own_residual, own_grad, gain_grad,
    g_across, g_down, g_far, tok_here, cot_here, up_here, wg, wu, wd, normed, hidden, grad_gate,
    grad_up,
    out_stage, part, via_across, via_down, from_across, from_down, residual_here, grad_here,
    mixer_here, pieces, received, weight_stage, output_stage,
    load_sem, row_sem, cot_sem, ag_send, ag_recv, rs_send, rs_recv, back_send, back_recv,
    store_sem, stage_sem, last_sem,
):
    turns = up_here.shape[0]
    halves = 2
    width = tok_here.shape[-1]
    me = lax.axis_index("mp")
    across = me + 1 - 2 * (me % 2)
    down = (me + 2) % 4
    far = 3 - me
    MESH = pl.DeviceIdType.MESH

    def remote(source, target, send, recv, device):
        return pltpu.make_async_remote_copy(
            src_ref=source,
            dst_ref=target,
            send_sem=send,
            recv_sem=recv,
            device_id={"mp": device},
            device_id_type=MESH,
        )

    def load(index, source, target):
        return pltpu.make_async_copy(source, target, load_sem.at[index])

    def load_tok(turn):
        return pltpu.make_async_copy(
            tok.at[turn // halves, :, turn % halves], tok_here.at[turn % 2], row_sem.at[turn]
        )

    def load_cot(block):
        start = pl.multiple_of(block * PIECE, PIECE)
        return pltpu.make_async_copy(
            cotangent.at[pl.ds(start, PIECE)], cot_here.at[block % 2], cot_sem.at[block % 2]
        )

    def direct(turn, side):
        return remote(
            gated.at[turn // halves, :, turn % halves],
            (g_across, g_down)[side].at[turn],
            ag_send.at[side, turn],
            ag_recv.at[side, turn],
            (across, down)[side],
        )

    def relay(turn, side):
        cut = pl.ds(2 * side, 2)
        return remote(
            (g_across, g_down)[side].at[turn, cut],
            g_far.at[turn, cut],
            ag_send.at[2 + side, turn],
            ag_recv.at[2 + side, turn],
            (down, across)[side],
        )

    first, second = pl.ds(0, HALF), pl.ds(HALF, HALF)

    def scatter(turn, index):
        source, target, device = (
            (part.at[turn, far, first], via_across.at[turn], across),
            (part.at[turn, far, second], via_down.at[turn], down),
            (part.at[turn, across, first], from_across.at[turn, first], across),
            (part.at[turn, down, second], from_down.at[turn, second], down),
            (part.at[turn, across, second], from_across.at[turn, second], across),
            (part.at[turn, down, first], from_down.at[turn, first], down),
        )[index]
        return remote(source, target, rs_send.at[index, turn], rs_recv.at[index, turn], device)

    def give_back(turn, slot):
        return remote(
            pieces.at[turn, slot],
            received.at[turn, slot],
            back_send.at[slot, turn],
            back_recv.at[slot, turn],
            (me, across, down, far)[slot],
        )

    def store_out(turn):
        return pltpu.make_async_copy(
            out_stage.at[turn % 2],
            out_part.at[turn // halves, :, turn % halves],
            store_sem.at[turn],
        )

    barrier = pltpu.get_barrier_semaphore()
    loads = [load(0, w_gate, wg), load(1, w_up, wu), load(2, w_down, wd)]
    for copy in loads:
        copy.start()
    blocks = cotangent.shape[0] // PIECE
    for turn in range(2):
        load_tok(turn).start()
        load_cot(turn).start()
    for device in (across, down, far):
        pl.semaphore_signal(barrier, inc=1, device_id={"mp": device}, device_id_type=MESH)
    pl.semaphore_wait(barrier, 3)
    for side in range(2):
        direct(0, side).start()
    gain_grad[...] = jnp.zeros_like(gain_grad)
    gain = params[CHANNEL_GAIN : CHANNEL_GAIN + 1, :]
    length = cotangent.shape[0]
    first_position = lax.axis_index("seq") * length

    def take_cotangent(block, carry):
        load_cot(block).wait()
        rows = jnp.swapaxes(cot_here[block % 2], 0, 1)
        position = first_position + block * PIECE
        position = (position + lax.broadcasted_iota(jnp.int32, (PIECE, 1), 0)).astype(F32)
        for s in range(turns // halves):
            column = gated.shape[-1] + s
            keep = position < params[HEAD_GAIN : HEAD_GAIN + 1, column : column + 1]
            kept = jnp.where(keep, rows[s].astype(F32), 0.0).astype(BF16)
            up_here[s * halves + block % halves, block // halves] = kept

        @pl.when(block + 2 < blocks)
        def _():
            load_cot(block + 2).start()

        return carry

    lax.fori_loop(0, blocks // 2, take_cotangent, 0)
    for side in range(2):
        direct(0, side).wait_recv()
        relay(0, side).start()
    for side in range(2):
        direct(1, side).start()
    lax.fori_loop(blocks // 2, blocks, take_cotangent, 0)
    for copy in loads:
        copy.wait()

    def forward_and_back(turn):
        load_tok(turn).wait()
        for side in range(2):
            relay(turn, side).wait_recv()
        rows = 4 * PIECE

        def flat(values):
            return values.reshape(rows, values.shape[-1])

        mixed = mm(flat(gated[turn // halves, :, turn % halves]), w_own[...])
        for slot, source in enumerate((g_across, g_down, g_far)):
            mixed = mixed + mm(flat(source[turn]), w_others[slot])
        residual = flat(tok_here[turn % 2]).astype(F32) + mixed
        for quarter in range(4):

            @pl.when(me == quarter)
            def _():
                residual_here[turn] = residual[quarter * PIECE : (quarter + 1) * PIECE]

        inverse = lax.rsqrt(jnp.mean(residual * residual, axis=-1, keepdims=True) + EPS_NORM)
        unit = residual * inverse
        rounded = (unit * gain).astype(BF16)
        normed[turn] = rounded
        gate_rows = mm_nt(rounded, wg[...])
        up_rows = mm_nt(rounded, wu[...])
        share = sigmoid(gate_rows)
        swished = gate_rows * share
        hidden_rows = (swished * up_rows).astype(BF16)
        hidden[turn] = hidden_rows
        grad_hidden = mm_nt(flat(up_here[turn]), wd[...])
        for side in range(2):

            @pl.when(turn + 1 < turns)
            def _():
                direct(turn + 1, side).wait_recv()
                relay(turn + 1, side).start()

        for side in range(2):

            @pl.when(turn + 2 < turns)
            def _():
                direct(turn + 2, side).start()

        slope = share * (1.0 + gate_rows * (1.0 - share))
        grad_gate_rows = (grad_hidden * up_rows * slope).astype(BF16)
        grad_up_rows = (grad_hidden * swished).astype(BF16)
        grad_gate[turn] = grad_gate_rows
        grad_up[turn] = grad_up_rows
        grad_rows = mm(grad_gate_rows, wg[...]) + mm(grad_up_rows, wu[...])
        part[turn] = grad_rows.astype(BF16).reshape(4, PIECE, width)
        for index in range(4):
            scatter(turn, index).start()
        gain_grad[...] += jnp.sum(grad_rows * unit, axis=0, keepdims=True)

        @pl.when(turn >= 2)
        def _():
            store_out(turn - 2).wait()

        out_stage[turn % 2] = mm(hidden_rows, wd[...]).astype(BF16).reshape(4, PIECE, width)
        store_out(turn).start()

        @pl.when(turn + 2 < turns)
        def _():
            load_tok(turn + 2).start()

    def pass_on(turn):
        scatter(turn, 0).wait_recv()
        part[turn, down, 0:HALF] = part[turn, down, 0:HALF] + via_across[turn]
        scatter(turn, 5).start()
        scatter(turn, 1).wait_recv()
        part[turn, across, HALF:PIECE] = part[turn, across, HALF:PIECE] + via_down[turn]
        scatter(turn, 4).start()

    def collect(turn):
        for index in range(2, 6):
            scatter(turn, index).wait_recv()
        grad_normed = part[turn, me].astype(F32) + from_across[turn].astype(F32)
        grad_normed = grad_normed + from_down[turn].astype(F32)
        residual = residual_here[turn]
        inverse = lax.rsqrt(jnp.mean(residual * residual, axis=-1, keepdims=True) + EPS_NORM)
        unit = residual * inverse
        scaled = grad_normed * gain
        through = inverse * (scaled - unit * jnp.mean(scaled * unit, axis=-1, keepdims=True))
        grad_residual = up_here[turn, me].astype(F32) + through
        grad_here[turn] = grad_residual
        grad_mixer = grad_residual.astype(BF16)
        mixer_here[turn] = grad_mixer
        for slot in range(4):
            weight = w_own[...] if slot == 0 else w_others[slot - 1]
            piece = mm_nt(grad_mixer, weight).astype(BF16)
            if slot == 0:
                received[turn, 0] = piece
            else:
                pieces[turn, slot] = piece
                give_back(turn, slot).start()

    tile = weight_stage.shape[2]
    tiles = width // tile

    def store_weight(kind, index, slot):
        return pltpu.make_async_copy(
            weight_stage.at[slot, kind],
            weight_grads.at[kind, pl.ds(index * tile, tile)],
            stage_sem.at[slot, kind],
        )

    all_rows = turns * 4 * PIECE

    def weight_tile(index, carry):
        slot = index % 2
        columns = pl.ds(pl.multiple_of(index * tile, tile), tile)

        @pl.when(index >= 2)
        def _():
            for kind in range(3):
                store_weight(kind, index - 2, slot).wait()

        left = normed[:, :, columns].reshape(all_rows, tile)
        upper = up_here[:, :, :, columns].reshape(all_rows, tile)
        units = hidden.shape[-1]
        for kind, (one, other) in enumerate(
            ((left, grad_gate), (left, grad_up), (upper, hidden))
        ):
            weight_stage[slot, kind] = mm_tn(one, other[...].reshape(all_rows, units)).astype(BF16)
            store_weight(kind, index, slot).start()
        return carry

    def round_of(index, carry):
        @pl.when(index < turns)
        def _():
            forward_and_back(index)

        @pl.when(index >= turns)
        def _():
            first_tile = (index - turns) * (tiles // 2)
            lax.fori_loop(first_tile, first_tile + tiles // 2, weight_tile, 0)

        @pl.when(jnp.logical_and(index >= 1, index <= turns))
        def _():
            pass_on(index - 1)

        @pl.when(index >= 2)
        def _():
            collect(index - 2)

        return carry

    lax.fori_loop(0, turns + 2, round_of, 0)
    mixer_rows = mixer_here[...].reshape(turns * PIECE, width)
    dv = gated.shape[-1]
    for slot in range(4):
        if slot == 0:
            blocks = [gated[t // halves, me, t % halves] for t in range(turns)]
        else:
            source = (None, g_across, g_down, g_far)[slot]
            blocks = [source[t, me] for t in range(turns)]
        rows = jnp.concatenate(blocks, axis=0)
        output_stage[slot] = mm_tn(mixer_rows, rows).astype(BF16)

    last = [
        pltpu.make_async_copy(residual_here, own_residual, last_sem.at[0]),
        pltpu.make_async_copy(grad_here, own_grad, last_sem.at[1]),
        pltpu.make_async_copy(output_stage, output_grads, last_sem.at[2]),
    ]
    for copy in last:
        copy.start()
    for turn in range(turns):
        for slot in range(1, 4):
            give_back(turn, slot).wait_recv()
        for slot in range(4):
            source = (me, across, down, far)[slot]
            pltpu.make_async_copy(
                received.at[turn, slot],
                grad_gated.at[turn // halves, source, turn % halves],
                last_sem.at[3 + turn * 4 + slot],
            ).start()
    for turn in range(turns):
        for slot in range(4):
            source = (me, across, down, far)[slot]
            pltpu.make_async_copy(
                received.at[turn, slot],
                grad_gated.at[turn // halves, source, turn % halves],
                last_sem.at[3 + turn * 4 + slot],
            ).wait()
        if turn >= turns - 2:
            store_out(turn).wait()
        for side in range(2):
            direct(turn, side).wait_send()
            relay(turn, side).wait_send()
        for index in range(6):
            scatter(turn, index).wait_send()
        for slot in range(1, 4):
            give_back(turn, slot).wait_send()
    for index in range(max(tiles - 2, 0), tiles):
        for kind in range(3):
            store_weight(kind, index, index % 2).wait()
    for copy in last:
        copy.wait()


def feed_forward(gated, w_own, w_others, tok, params, w_gate, w_up, w_down, cotangent):
    sequences, length, width = tok.shape
    dv, units = gated.shape[-1], w_gate.shape[0]
    halves = length // 4 // PIECE
    turns = sequences * halves

    def pieces_of(values):
        return values.reshape(sequences, 4, halves, PIECE, values.shape[-1])

    anywhere = pl.BlockSpec(memory_space=pl.ANY)
    vmem = pl.BlockSpec(memory_space=pltpu.VMEM)
    dma = pltpu.SemaphoreType.DMA
    rows = 4 * PIECE
    outs = pl.pallas_call(
        ffn_body,
        in_specs=[vmem] * 3 + [anywhere, vmem] + [anywhere] * 4,
        out_specs=[anywhere] * 6 + [vmem],
        out_shape=[
            shape_of((sequences, 4, halves, PIECE, width), BF16),
            shape_of((3, width, units), BF16),
            shape_of((4, width, dv), BF16),
            shape_of((sequences, 4, halves, PIECE, dv), BF16),
            shape_of((turns, PIECE, width), F32),
            shape_of((turns, PIECE, width), F32),
            shape_of((1, width), F32),
        ],
        scratch_shapes=[
            pltpu.VMEM((turns, 4, PIECE, dv), BF16),
            pltpu.VMEM((turns, 4, PIECE, dv), BF16),
            pltpu.VMEM((turns, 4, PIECE, dv), BF16),
            pltpu.VMEM((2, 4, PIECE, width), BF16),
            pltpu.VMEM((2, PIECE, sequences, width), BF16),
            pltpu.VMEM((turns, 4, PIECE, width), BF16),
            pltpu.VMEM((units, width), BF16),
            pltpu.VMEM((units, width), BF16),
            pltpu.VMEM((units, width), BF16),
            pltpu.VMEM((turns, rows, width), BF16),
            pltpu.VMEM((turns, rows, units), BF16),
            pltpu.VMEM((turns, rows, units), BF16),
            pltpu.VMEM((turns, rows, units), BF16),
            pltpu.VMEM((2, 4, PIECE, width), BF16),
            pltpu.VMEM((turns, 4, PIECE, width), BF16),
            pltpu.VMEM((turns, HALF, width), BF16),
            pltpu.VMEM((turns, HALF, width), BF16),
            pltpu.VMEM((turns, PIECE, width), BF16),
            pltpu.VMEM((turns, PIECE, width), BF16),
            pltpu.VMEM((turns, PIECE, width), F32),
            pltpu.VMEM((turns, PIECE, width), F32),
            pltpu.VMEM((turns, PIECE, width), BF16),
            pltpu.VMEM((turns, 4, PIECE, dv), BF16),
            pltpu.VMEM((turns, 4, PIECE, dv), BF16),
            pltpu.VMEM((2, 3, 256, units), BF16),
            pltpu.VMEM((4, width, dv), BF16),
            dma((3,)),
            dma((turns,)),
            dma((2,)),
            dma((4, turns)),
            dma((4, turns)),
            dma((6, turns)),
            dma((6, turns)),
            dma((4, turns)),
            dma((4, turns)),
            dma((turns,)),
            dma((2, 3)),
            dma((3 + 4 * turns,)),
        ],
        compiler_params=pltpu.CompilerParams(
            collective_id=0, has_side_effects=True, vmem_limit_bytes=64 * 2**20
        ),
        cost_estimate=pl.CostEstimate(
            flops=2 * sequences * length * width * (4 * dv + 9 * units),
            bytes_accessed=sequences * length * width * 8,
            transcendentals=0,
        ),
        name="feed_forward",
    )(
        pieces_of(gated), w_own, w_others, pieces_of(tok), params, w_gate, w_up, w_down, cotangent
    )
    out_part, weight_grads, output_grads, grad_gated, own_residual, own_grad, gain_grad = outs
    return (
        out_part.reshape(sequences, 4, length // 4, width),
        weight_grads,
        output_grads,
        grad_gated.reshape(sequences, length, dv),
        own_residual,
        own_grad,
        gain_grad,
    )


SMALL = 48


def paired_sum(own, received, order):
    terms = [own.astype(F32)] + [received[index].astype(F32) for index in order]
    while len(terms) > 1:
        half = len(terms) // 2
        terms = [terms[index] + terms[index + half] for index in range(half)]
    return terms[0]


def mixer_back_body(
    grad_gated_in, head_in, profile_in, out_gate_in, projected_in, cumulative_in, states_in,
    normed_in, tok_in, residual_in, grad_residual_in, out_part_in, hidden_grads, output_parts,
    w_proj_in, w_gate_in, low_rank, halo, params, rank_up, w_rank, before, entering,
    decays, channel_part,
    output, token_grads, hidden_out, mixer_out, small_local, small_shared,
    grad_gated, head, profile, out_gate, projected, cumulative, states, normed, tok, residual,
    grad_residual, part, w_proj, w_gate,
    hidden_kept, hidden_seq, hidden_dp, output_kept, output_seq, output_mp, output_dp,
    f_via_across, f_via_down, f_across, f_down, g_via_across, g_via_down, g_across, g_down,
    grad_out_gate, grad_head, grad_projected, grad_low_rank, mixer_grad, mixer_seq, mixer_dp,
    state_grad, state_seq, upstream, extended, grad_extended, edge_out, edge_in,
    small, small_low, small_seq, small_dp, small_mp, out_stage,
    load_sem, seq_send, seq_recv, dp_send, dp_recv, mp_send, mp_recv, f_send, f_recv,
    g_send, g_recv, store_sem,
):
    sequences, length, dv = grad_gated.shape
    width = normed.shape[-1]
    rank, dk = rank_up.shape
    c3 = projected.shape[-1]
    halves = 2
    turns = sequences * halves
    MESH = pl.DeviceIdType.MESH
    me, side, place = lax.axis_index("mp"), lax.axis_index("seq"), lax.axis_index("dp")
    sides, places = lax.axis_size("seq"), lax.axis_size("dp")
    across = me + 1 - 2 * (me % 2)
    down = (me + 2) % 4
    far = 3 - me
    share_rows = width // sides
    shard_rows = share_rows // places
    steps = length // STEP
    per_step = STEP // CHUNK
    first, second = pl.ds(0, HALF), pl.ds(HALF, HALF)

    def remote(source, target, send, recv, axis, device):
        return pltpu.make_async_remote_copy(
            src_ref=source,
            dst_ref=target,
            send_sem=send,
            recv_sem=recv,
            device_id={axis: device},
            device_id_type=MESH,
        )


    loads = [
        pltpu.make_async_copy(source, target, load_sem.at[index])
        for index, (source, target) in enumerate(
            [
                (grad_gated_in, grad_gated),
                (head_in, head),
                (profile_in, profile),
                (out_gate_in, out_gate),
                (out_part_in, part),
                (hidden_grads.at[:, pl.ds(side * share_rows, share_rows)], hidden_kept),
                (output_parts.at[:, pl.ds(side * share_rows, share_rows)], output_kept),
                (normed_in, normed),
                (projected_in, projected),
                (cumulative_in, cumulative),
                (states_in, states),
                (residual_in, residual),
                (w_proj_in, w_proj),
                (w_gate_in, w_gate),
                (grad_residual_in, grad_residual),
                (tok_in.at[:, me], tok),
            ]
        )
    ]

    def to_sides(kind, source_of, target):
        copies = []
        for hop in range(1, sides):
            peer = (side + hop) % sides
            copies.append(
                remote(
                    source_of(peer),
                    target.at[hop - 1],
                    seq_send.at[kind, hop - 1],
                    seq_recv.at[kind, hop - 1],
                    "seq",
                    peer,
                )
            )
        return copies

    def to_places(kind, source_of, target):
        copies = []
        for hop in range(1, places):
            peer = (place + hop) % places
            copies.append(
                remote(
                    source_of(peer),
                    target.at[hop - 1],
                    dp_send.at[kind, hop - 1],
                    dp_recv.at[kind, hop - 1],
                    "dp",
                    peer,
                )
            )
        return copies

    def to_heads(kind, source_of, target):
        return [
            remote(
                source_of(slot),
                target.at[slot - 1],
                mp_send.at[kind, slot - 1],
                mp_recv.at[kind, slot - 1],
                "mp",
                (me, across, down, far)[slot],
            )
            for slot in range(1, 4)
        ]

    def share_of(ref):
        return lambda peer: ref.at[:, pl.ds(peer * share_rows, share_rows)]

    def shard_of(ref):
        return lambda peer: ref.at[:, pl.ds(peer * shard_rows, shard_rows)]

    hidden_to_sides = to_sides(0, share_of(hidden_grads), hidden_seq)
    output_to_sides = to_sides(1, share_of(output_parts), output_seq)
    state_to_sides = to_sides(2, lambda peer: state_grad, state_seq)
    mixer_to_sides = to_sides(
        3, lambda peer: mixer_grad.at[pl.ds(peer * share_rows, share_rows)], mixer_seq
    )
    small_to_sides = to_sides(4, lambda peer: small_low.at[0], small_seq)
    edge_copy = remote(
        edge_out,
        edge_in,
        seq_send.at[5, 0],
        seq_recv.at[5, 0],
        "seq",
        (side + sides - 1) % sides,
    )
    hidden_to_places = to_places(0, shard_of(hidden_kept), hidden_dp)

    def own_share(peer):
        return pl.ds(pl.multiple_of(side * share_rows + peer * shard_rows, 16), shard_rows)

    mixer_to_places = to_places(1, lambda peer: mixer_grad.at[own_share(peer)], mixer_dp)
    output_to_places = to_places(
        2, lambda peer: output_kept.at[0, pl.ds(peer * shard_rows, shard_rows)], output_dp
    )
    small_to_places = to_places(3, lambda peer: small_low.at[1], small_dp)
    output_to_heads = to_heads(0, lambda slot: output_kept.at[slot], output_mp)
    small_to_heads = to_heads(1, lambda slot: small_low.at[2], small_mp)

    def scatter(turn, index, forward):
        if forward:
            via_across, via_down, from_across, from_down = (
                f_via_across, f_via_down, f_across, f_down,
            )
            send, recv = f_send, f_recv
        else:
            via_across, via_down, from_across, from_down = (
                g_via_across, g_via_down, g_across, g_down,
            )
            send, recv = g_send, g_recv
        s, h = turn // halves, turn % halves
        low, high = pl.ds(h * PIECE, HALF), pl.ds(h * PIECE + HALF, HALF)
        source, target, device = (
            (part.at[s, far, low], via_across.at[turn], across),
            (part.at[s, far, high], via_down.at[turn], down),
            (part.at[s, across, low], from_across.at[turn, first], across),
            (part.at[s, down, high], from_down.at[turn, second], down),
            (part.at[s, across, high], from_across.at[turn, second], across),
            (part.at[s, down, low], from_down.at[turn, first], down),
        )[index]
        return remote(source, target, send.at[index, turn], recv.at[index, turn], "mp", device)

    def pass_on(turn, forward):
        via_across, via_down = (
            (f_via_across, f_via_down) if forward else (g_via_across, g_via_down)
        )
        s, h = turn // halves, turn % halves
        low = pl.ds(h * PIECE, HALF)
        high = pl.ds(h * PIECE + HALF, HALF)
        scatter(turn, 0, forward).wait_recv()
        part[s, down, low] = part[s, down, low] + via_across[turn]
        scatter(turn, 5, forward).start()
        scatter(turn, 1, forward).wait_recv()
        part[s, across, high] = part[s, across, high] + via_down[turn]
        scatter(turn, 4, forward).start()

    def summed(turn, forward):
        from_across, from_down = (f_across, f_down) if forward else (g_across, g_down)
        for index in range(2, 6):
            scatter(turn, index, forward).wait_recv()
        s, h = turn // halves, turn % halves
        total = part[s, me, h * PIECE : (h + 1) * PIECE].astype(F32)
        return total + from_across[turn].astype(F32) + from_down[turn].astype(F32)

    def store(turn, kind):
        source, target = ((out_stage, output), (grad_residual, token_grads))[kind]
        return pltpu.make_async_copy(source.at[turn], target.at[turn], store_sem.at[kind, turn])


    barrier = pltpu.get_barrier_semaphore()
    for copy in loads:
        copy.start()
    for axis, peers in (
        ("seq", [(side + hop) % sides for hop in range(1, sides)]),
        ("mp", [across, down, far]),
        ("dp", [(place + hop) % places for hop in range(1, places)]),
    ):
        for peer in peers:
            pl.semaphore_signal(barrier, inc=1, device_id={axis: peer}, device_id_type=MESH)
    small[...] = jnp.zeros_like(small)
    state_grad[...] = jnp.zeros_like(state_grad)
    small[33:34, :] = channel_part[...]
    pl.semaphore_wait(barrier, sides - 1 + 3 + places - 1)
    for copy in hidden_to_sides + output_to_sides:
        copy.start()
    loads[4].wait()
    for turn in range(turns):
        for index in range(2):
            scatter(turn, index, True).start()
    for copy in loads[0:4]:
        copy.wait()


    scale = dk ** (-0.5)
    head_gain = params[HEAD_GAIN : HEAD_GAIN + 1, :dv]
    mixer_gain = params[MIXER_GAIN : MIXER_GAIN + 1, :]

    def ungate(index, carry):
        rows = pl.ds(pl.multiple_of(index * STEP, STEP), STEP)
        for s in range(sequences):
            upper = grad_gated[s, rows, :].astype(F32)
            head_rows_here = head[s, rows, :].astype(F32)
            inverse = lax.rsqrt(
                jnp.mean(head_rows_here * head_rows_here, axis=-1, keepdims=True) + EPS_HEAD
            )
            unit = head_rows_here * inverse
            logits = out_gate[s, rows, :].astype(F32)
            share = sigmoid(logits)
            slope = share * (1.0 + logits * (1.0 - share))
            grad_out_gate[s, rows, :] = (upper * unit * head_gain * slope).astype(BF16)
            grad_normed = upper * (logits * share)
            small[34:35, :dv] += jnp.sum(grad_normed * unit, axis=0, keepdims=True)
            scaled = grad_normed * head_gain
            through = inverse * (scaled - unit * jnp.mean(scaled * unit, axis=-1, keepdims=True))
            rounded = (through * scale).astype(BF16)
            grad_head[s, rows, :] = rounded
            state_grad[:, s * dk : (s + 1) * dk] += mm_tn(rounded, profile[s, rows, :])
        return carry

    lax.fori_loop(0, steps, ungate, 0)
    for copy in state_to_sides:
        copy.start()
    for turn in range(turns):
        for index in range(2, 4):
            scatter(turn, index, True).start()
    loads[5].wait()
    for copy in hidden_to_sides:
        copy.wait_recv()
    hidden_sum = hidden_kept[...]
    for hop in range(sides - 1):
        hidden_sum = hidden_sum + hidden_seq[hop]
    hidden_kept[...] = hidden_sum
    for copy in hidden_to_places:
        copy.start()
    loads[6].wait()
    for copy in output_to_sides:
        copy.wait_recv()
    output_sum = output_kept[...]
    for hop in range(sides - 1):
        output_sum = output_sum + output_seq[hop]
    output_kept[...] = output_sum
    for copy in output_to_heads:
        copy.start()
    for copy in loads[7:11]:
        copy.wait()
    for copy in state_to_sides:
        copy.wait_recv()
    total = jnp.zeros_like(upstream)
    for ahead in range(sides - 1, 0, -1):
        source = side + ahead
        decay = decays[source % sides]
        longer = state_seq[sides - ahead - 1] + jnp.exp(decay) * total
        total = jnp.where(source < sides, longer, total)
    upstream[...] = total
    grad_extended[:, STEP : STEP + 8, :] = jnp.zeros_like(grad_extended[:, STEP : STEP + 8, :])


    taps = params[TAPS : TAPS + CONV, :c3]
    causal = triangle(True)

    def backward_step(back, carry):
        step = steps - 1 - back
        start = pl.multiple_of(step * STEP, STEP)

        @pl.when(back > 0)
        def _():
            grad_extended[:, STEP : STEP + 8, :] = grad_extended[:, 0:8, :]

        @pl.when(step == 0)
        def _():
            extended[:, 0:8, :] = halo[...]

        @pl.when(step > 0)
        def _():
            earlier = projected[:, pl.ds(pl.multiple_of(jnp.maximum(start - 16, 0), 16), 16), :]
            extended[:, 0:8, :] = earlier.astype(F32)[:, 8:16, :]

        for s in range(sequences):
            here = pl.ds(start, STEP)
            extended[s, 8 : 8 + STEP, :] = projected[s, here, :].astype(F32)
            filtered = filter_rows(extended.at[s], taps, STEP)
            share = sigmoid(filtered)
            convolved = (filtered * share).astype(BF16)
            slope = share * (1.0 + filtered * (1.0 - share))
            low_rows = low_rank[s, here, :]
            logit = mm(low_rows, rank_up[...]) + params[BIAS : BIAS + 1, :dk]
            logit_grads = [None] * per_step
            for piece in reversed(range(per_step)):
                rows = slice(piece * CHUNK, (piece + 1) * CHUNK)
                there = pl.ds(start + piece * CHUNK, CHUNK)
                queries = convolved[rows, :dk].astype(F32)
                keys = convolved[rows, dk : 2 * dk].astype(F32)
                values = convolved[rows, 2 * dk :]
                grad_rows = grad_head[s, there, :]
                total = cumulative[s, there, :]
                middle, last = total[CHUNK // 2 - 1 : CHUNK // 2], total[CHUNK - 1 : CHUNK]
                lift, lower = jnp.exp(total - middle), jnp.exp(middle - total)
                inner, outer = jnp.exp(total), jnp.exp(last - total)
                whole_decay = jnp.exp(last)
                lifted, lowered = (queries * lift).astype(BF16), (keys * lower).astype(BF16)
                inside, tails = (queries * inner).astype(BF16), (keys * outer).astype(BF16)
                own = slice(s * dk, (s + 1) * dk)
                previous = before[step * per_step + piece, :, own]
                state = states[step * per_step + piece, :, own].astype(F32)
                state = state + entering[:, own] * jnp.exp(previous)
                scores = jnp.where(causal, mm_nt(lifted, lowered), 0.0).astype(BF16)
                grad_scores = jnp.where(causal, mm_nt(grad_rows, values), 0.0).astype(BF16)
                later = upstream[:, own]
                later_low = later.astype(BF16)
                grad_values = mm_tn(scores, grad_rows) + mm_nt(tails, later_low)
                grad_lifted = mm(grad_scores, lowered)
                grad_lowered = mm_tn(grad_scores, lifted)
                grad_inside = mm(grad_rows, state.astype(BF16))
                grad_tails = mm(values, later_low)
                upstream[:, own] = later * whole_decay + mm_tn(grad_rows, inside)
                tail_terms = tails.astype(F32) * grad_tails
                grad_total = (
                    lifted.astype(F32) * grad_lifted
                    - lowered.astype(F32) * grad_lowered
                    + inside.astype(F32) * grad_inside
                    - tail_terms
                )
                grad_last = jnp.sum(tail_terms, axis=0, keepdims=True) + whole_decay * jnp.sum(
                    later * state, axis=0, keepdims=True
                )
                grad_decay = running_sums([grad_total], False)[0] + grad_last
                logit_grads[piece] = grad_decay / GATE_NORMALIZER * sigmoid(-logit[rows])
                grad_extended[s, rows, :dk] = (
                    grad_lifted * lift + grad_inside * inner
                ) * slope[rows, :dk]
                grad_extended[s, rows, dk : 2 * dk] = (
                    grad_lowered * lower + grad_tails * outer
                ) * slope[rows, dk : 2 * dk]
                grad_extended[s, rows, 2 * dk :] = grad_values * slope[rows, 2 * dk :]
            logit_grad = jnp.concatenate(logit_grads, axis=0)
            logit_low = logit_grad.astype(BF16)
            small[35:36, :dk] += jnp.sum(logit_grad, axis=0, keepdims=True)
            small[16 : 16 + rank, :dk] += mm_tn(low_rows, logit_low)
            grad_low_rank[s, here, :] = mm_nt(logit_low, rank_up[...]).astype(BF16)
            total_rows = taps[EDGE : EDGE + 1, :] * grad_extended[s, 0:STEP, :]
            for offset in range(EDGE):
                total_rows = total_rows + taps[offset : offset + 1, :] * grad_extended[
                    s, pl.ds(EDGE - offset, STEP), :
                ]
            grad_projected[s, here, :] = total_rows.astype(BF16)
            grad_filtered = grad_extended[s, 0:STEP, :]
            for offset in range(CONV):
                small[16 + offset : 17 + offset, dk : dk + c3] += jnp.sum(
                    grad_filtered * extended[s, pl.ds(8 - EDGE + offset, STEP), :],
                    axis=0,
                    keepdims=True,
                )
        for turn in range(turns):

            @pl.when(back == turn % steps)
            def _():
                pass_on(turn, True)

        return carry

    lax.fori_loop(0, steps, backward_step, 0)


    edge_out[...] = jnp.zeros_like(edge_out)
    for s in range(sequences):
        rows = grad_extended[s, 0:8, :]
        for i in range(EDGE):
            edge_row = taps[0:1] * rows[i : i + 1]
            for j in range(1, i + 1):
                edge_row = edge_row + taps[j : j + 1] * rows[i - j : i - j + 1]
            edge_out[s, 16 - EDGE + i : 17 - EDGE + i, :] = edge_row
    edge_copy.start()


    loads[11].wait()
    for turn in range(turns):
        s, h = turn // halves, turn % halves
        total = residual[turn] + summed(turn, True)
        position = side * length + me * (length // 4) + h * PIECE
        position = position + lax.broadcasted_iota(jnp.int32, (PIECE, 1), 0)
        limit = params[HEAD_GAIN : HEAD_GAIN + 1, dv + s : dv + s + 1]
        out_stage[turn] = jnp.where(position.astype(F32) < limit, total, 0.0).astype(BF16)
        store(turn, 0).start()
    for turn in range(turns):
        for index in range(6):
            scatter(turn, index, True).wait_send()
    edge_copy.wait_recv()
    for s in range(sequences):
        tail = grad_projected[s, length - 16 :, :].astype(F32)
        tail = tail + jnp.where(side < sides - 1, edge_in[s], 0.0)
        grad_projected[s, length - 16 :, :] = tail.astype(BF16)


    loads[12].wait()
    loads[13].wait()

    def input_grad(turn):
        s, h = turn // halves, turn % halves
        quarter = length // 4

        def rows_of_turn(ref):
            blocks = [
                ref[s, q * quarter + h * PIECE : q * quarter + (h + 1) * PIECE, :]
                for q in range(4)
            ]
            return jnp.concatenate(blocks, axis=0)

        total = mm_nt(rows_of_turn(grad_projected), w_proj[...])
        total = total + mm_nt(rows_of_turn(grad_out_gate), w_gate[...])
        total = total + mm(rows_of_turn(grad_low_rank), w_rank[...])
        rounded = total.astype(BF16)
        for q in range(4):
            part[s, q, h * PIECE : (h + 1) * PIECE] = rounded[q * PIECE : (q + 1) * PIECE]
        for index in range(4):
            scatter(turn, index, False).start()
        small[32:33, :] += jnp.sum(
            total * rows_of_turn(normed).astype(F32), axis=0, keepdims=True
        )

    for turn in range(turns):
        input_grad(turn)


    flat = sequences * length
    tile = 256

    def weight_tile(index, carry):
        columns = pl.ds(pl.multiple_of(index * tile, tile), tile)
        left = normed[:, :, columns].reshape(flat, tile)
        mixer_grad[columns, :c3] = mm_tn(left, grad_projected[...].reshape(flat, c3)).astype(BF16)
        mixer_grad[columns, c3:] = mm_tn(left, grad_out_gate[...].reshape(flat, dv)).astype(BF16)
        small[0:rank, columns] = mm_tn(grad_low_rank[...].reshape(flat, rank), left)
        return carry

    lax.fori_loop(0, width // tile, weight_tile, 0)
    small_low[0] = small[...].astype(BF16)
    for copy in small_to_sides + mixer_to_sides:
        copy.start()
    pass_on(0, False)
    for copy in output_to_heads:
        copy.wait_recv()
    output_kept[0] = output_kept[0] + output_mp[0] + output_mp[1] + output_mp[2]
    for copy in output_to_places:
        copy.start()
    for copy in small_to_sides:
        copy.wait_recv()
    small_low[1] = paired_sum(small_low[0], small_seq, range(sides - 1)).astype(BF16)
    for copy in small_to_places:
        copy.start()
    for copy in mixer_to_sides:
        copy.wait_recv()
    own = pl.ds(pl.multiple_of(side * share_rows, 16), share_rows)
    mixer_sum = mixer_grad[own, :]
    for hop in range(sides - 1):
        mixer_sum = mixer_sum + mixer_seq[hop]
    mixer_grad[own, :] = mixer_sum
    for copy in mixer_to_places:
        copy.start()
    pass_on(1, False)
    for copy in small_to_places:
        copy.wait_recv()
    summed_here = paired_sum(small_low[1], small_dp, range(places - 1))
    small_local[...] = summed_here
    small_low[2] = summed_here.astype(BF16)
    for copy in small_to_heads:
        copy.start()
    pass_on(2, False)
    for copy in hidden_to_places:
        copy.wait_recv()
    own_shard = pl.ds(pl.multiple_of(place * shard_rows, 16), shard_rows)
    for kind in range(3):
        total = hidden_kept[kind, own_shard, :].astype(F32)
        for hop in range(places - 1):
            total = total + hidden_dp[hop, kind].astype(F32)
        hidden_out[kind] = total
    pass_on(3, False)


    loads[14].wait()
    loads[15].wait()
    for turn in range(turns):
        s, h = turn // halves, turn % halves
        grad_normed = summed(turn, False)
        rows = tok[s, h * PIECE : (h + 1) * PIECE].astype(F32)
        inverse = lax.rsqrt(jnp.mean(rows * rows, axis=-1, keepdims=True) + EPS_NORM)
        unit = rows * inverse
        scaled = grad_normed * mixer_gain
        through = inverse * (scaled - unit * jnp.mean(scaled * unit, axis=-1, keepdims=True))
        grad_residual[turn] = grad_residual[turn] + through
        store(turn, 1).start()
    for copy in small_to_heads:
        copy.wait_recv()
    small_shared[...] = paired_sum(small_low[2], small_mp, (1, 0, 2))
    for copy in mixer_to_places + output_to_places:
        copy.wait_recv()
    total = mixer_grad[own_share(place), :].astype(F32)
    for hop in range(places - 1):
        total = total + mixer_dp[hop].astype(F32)
    mixer_out[:, : c3 + dv] = total
    total = output_kept[0, own_shard, :].astype(F32)
    for hop in range(places - 1):
        total = total + output_dp[hop].astype(F32)
    mixer_out[:, c3 + dv :] = total


    for copies in (
        hidden_to_sides, output_to_sides, state_to_sides, mixer_to_sides, small_to_sides,
        [edge_copy], hidden_to_places, mixer_to_places, output_to_places, small_to_places,
        output_to_heads, small_to_heads,
    ):
        for copy in copies:
            copy.wait_send()
    for turn in range(turns):
        for index in range(6):
            scatter(turn, index, False).wait_send()
        store(turn, 0).wait()
        store(turn, 1).wait()


def mixer_back(
    grad_gated, head, profile, out_gate, projected, cumulative, states, normed, tok, residual,
    grad_residual, out_part, hidden_grads, output_parts, w_proj, w_gate, low_rank, halo, params,
    rank_up, w_rank, before, entering, decays, channel_part, seq_count, dp_count,
):
    sequences, length, width = normed.shape
    dv, c3 = grad_gated.shape[-1], projected.shape[-1]
    rank, dk = rank_up.shape
    units = hidden_grads.shape[-1]
    quarter = length // 4
    turns = sequences * quarter // PIECE
    share_rows = width // seq_count
    shard_rows = share_rows // dp_count
    peers, others = seq_count - 1, dp_count - 1
    anywhere = pl.BlockSpec(memory_space=pl.ANY)
    vmem = pl.BlockSpec(memory_space=pltpu.VMEM)
    dma = pltpu.SemaphoreType.DMA

    def low(*shape):
        return pltpu.VMEM(shape, BF16)

    def full(*shape):
        return pltpu.VMEM(shape, F32)

    hops = [
        low(turns, HALF, width),
        low(turns, HALF, width),
        low(turns, PIECE, width),
        low(turns, PIECE, width),
    ]
    return pl.pallas_call(
        mixer_back_body,
        in_specs=[anywhere] * 16 + [vmem] * 9,
        out_specs=[anywhere] * 2 + [vmem] * 4,
        out_shape=[
            shape_of((turns, PIECE, width), BF16),
            shape_of((turns, PIECE, width), F32),
            shape_of((3, shard_rows, units), F32),
            shape_of((shard_rows, c3 + 2 * dv), F32),
            shape_of((SMALL, width), F32),
            shape_of((SMALL, width), F32),
        ],
        scratch_shapes=[
            low(sequences, length, dv),
            low(sequences, length, dv),
            low(sequences, length, dk),
            low(sequences, length, dv),
            low(sequences, length, c3),
            full(sequences, length, dk),
            low(length // CHUNK, dv, sequences * dk),
            low(sequences, length, width),
            low(sequences, quarter, width),
            full(turns, PIECE, width),
            full(turns, PIECE, width),
            low(sequences, 4, quarter, width),
            low(width, c3),
            low(width, dv),
            low(3, share_rows, units),
            low(peers, 3, share_rows, units),
            low(others, 3, shard_rows, units),
            low(4, share_rows, dv),
            low(peers, 4, share_rows, dv),
            low(3, share_rows, dv),
            low(others, shard_rows, dv),
            *hops,
            *hops,
            low(sequences, length, dv),
            low(sequences, length, dv),
            low(sequences, length, c3),
            low(sequences, length, rank),
            low(width, c3 + dv),
            low(peers, share_rows, c3 + dv),
            low(others, shard_rows, c3 + dv),
            full(dv, sequences * dk),
            full(peers, dv, sequences * dk),
            full(dv, sequences * dk),
            full(sequences, STEP + 8, c3),
            full(sequences, STEP + 8, c3),
            full(sequences, 16, c3),
            full(sequences, 16, c3),
            full(SMALL, width),
            low(3, SMALL, width),
            low(peers, SMALL, width),
            low(others, SMALL, width),
            low(3, SMALL, width),
            low(turns, PIECE, width),
            dma((16,)),
            dma((6, peers)),
            dma((6, peers)),
            dma((4, others)),
            dma((4, others)),
            dma((2, 3)),
            dma((2, 3)),
            dma((6, turns)),
            dma((6, turns)),
            dma((6, turns)),
            dma((6, turns)),
            dma((2, turns)),
        ],
        compiler_params=pltpu.CompilerParams(
            collective_id=1, has_side_effects=True, vmem_limit_bytes=64 * 2**20
        ),
        cost_estimate=pl.CostEstimate(
            flops=2 * sequences * length * width * 2 * (c3 + dv) * 2,
            bytes_accessed=sequences * length * width * 16,
            transcendentals=0,
        ),
        name="mixer_back",
    )(
        grad_gated, head, profile, out_gate, projected, cumulative, states, normed, tok, residual,
        grad_residual, out_part, hidden_grads, output_parts, w_proj, w_gate, low_rank, halo,
        params, rank_up, w_rank, before, entering, decays, channel_part,
    )


def on_device(
    tokens, lengths, mixer_gain, project_weight, filter_weight, rank_down, rank_up, decay_bias,
    gate_weight, head_gain, output_weight, channel_gain, hidden_gate, hidden_up, hidden_down,
    cotangent,
):
    length, sequences, width = tokens.shape
    seq_count, dp_count = lax.axis_size("seq"), lax.axis_size("dp")
    shards = seq_count * dp_count
    shard = lax.axis_index("seq") * dp_count + lax.axis_index("dp")
    own_rows = length // lax.axis_size("mp")
    w_proj, rank_up_here = project_weight[:, 0], rank_up[:, 0]
    c3, dv = w_proj.shape[1], gate_weight.shape[1]
    rank, dk = rank_up_here.shape
    w_rank = rank_down.T

    def row(values):
        values = values.astype(F32).reshape(-1, values.shape[-1])
        return jnp.pad(values, ((0, 0), (0, width - values.shape[1])))

    params = jnp.concatenate(
        [
            row(mixer_gain),
            row(channel_gain),
            row(jnp.concatenate([head_gain.astype(F32), lengths.astype(F32)])),
            row(filter_weight[:, 0]),
            row(decay_bias),
        ],
        axis=0,
    )
    (
        tok, normed, projected, low_rank, cumulative, states, before, out_gate, profile, gated,
        head, halo, entering, decays, w_others,
    ) = front(
        tokens, params, w_proj, gate_weight, w_rank, rank_up_here, output_weight, seq_count
    )
    (
        out_part, hidden_grads, output_parts, grad_gated, residual, grad_residual, channel_part,
    ) = feed_forward(
        gated, output_weight, w_others, tok, params, hidden_gate.T, hidden_up.T, hidden_down,
        cotangent,
    )
    outputs, token_grads, hidden_sums, mixer_sums, small, shared = mixer_back(
        grad_gated, head, profile, out_gate, projected, cumulative, states, normed,
        tok.reshape(sequences, 4, own_rows, width), residual, grad_residual, out_part,
        hidden_grads, output_parts, w_proj, gate_weight, low_rank, halo, params, rank_up_here,
        w_rank, before, entering, decays, channel_part, seq_count, dp_count,
    )

    def own(values):
        size = values.shape[-1] // shards
        return lax.dynamic_slice_in_dim(values, shard * size, size, values.ndim - 1)

    own_shape = (sequences, own_rows, width)
    return (
        outputs.reshape(own_shape).swapaxes(0, 1),
        token_grads.reshape(own_shape).swapaxes(0, 1),
        shared[32] / mixer_gain.astype(F32),
        mixer_sums[:, None, :c3],
        own(small[16 : 16 + CONV, dk : dk + c3])[:, None],
        shared[:rank].T,
        own(small[16 : 16 + rank, :dk])[:, None],
        own(small[35:36, :dk]),
        mixer_sums[:, c3 : c3 + dv],
        shared[34, :dv],
        mixer_sums[:, c3 + dv :].T,
        shared[33],
        hidden_sums[0],
        hidden_sums[1],
        hidden_sums[2].T,
    )


def solution(mesh):
    in_specs = (
        P("seq", "dp", None),
        P("dp"),
        P(),
        P(None, "mp", None),
        P(None, "mp", None),
        P(),
        P(None, "mp", None),
        P("mp", None),
        P(None, "mp"),
        P(),
        P("mp", None),
        P(),
        P(None, "mp"),
        P(None, "mp"),
        P("mp", None),
        P("seq", "dp", None),
    )
    out_specs = (
        P(("seq", "mp"), "dp", None),
        P(("seq", "mp"), "dp", None),
        P(),
        P(("seq", "dp"), "mp", None),
        P(None, "mp", ("seq", "dp")),
        P(),
        P(None, "mp", ("seq", "dp")),
        P("mp", ("seq", "dp")),
        P(("seq", "dp"), "mp"),
        P(),
        P("mp", ("seq", "dp")),
        P(),
        P(("seq", "dp"), "mp"),
        P(("seq", "dp"), "mp"),
        P("mp", ("seq", "dp")),
    )
    return jax.shard_map(
        on_device, mesh=mesh, in_specs=in_specs, out_specs=out_specs, check_vma=False
    )
```

```python
import jax
import jax.numpy as jnp
from jax import lax
from jax.experimental import pallas as pl
from jax.experimental.pallas import tpu as pltpu
from jax.sharding import PartitionSpec as P

CONV = 4
EDGE = CONV - 1
CHUNK = 128
STEP = 256
EPS_NORM = 1e-06
EPS_HEAD = 1e-05
GATE_NORMALIZER = 16.0
BF16 = jnp.bfloat16
F32 = jnp.float32
VMEM_LIMIT = 56 * 2**20


def mm(left, right):
    return lax.dot_general(left, right, (((1,), (0,)), ((), ())), preferred_element_type=F32)


def mm_nt(left, right):
    return lax.dot_general(left, right, (((1,), (1,)), ((), ())), preferred_element_type=F32)


def mm_tn(left, right):
    return lax.dot_general(left, right, (((0,), (0,)), ((), ())), preferred_element_type=F32)


def sigmoid(values):
    return 1.0 / (1.0 + jnp.exp(-values))


def whole(shape):
    return pl.BlockSpec(shape, lambda *_: (0,) * len(shape))


def shape_of(shape, dtype):
    return jax.ShapeDtypeStruct(shape, dtype)


MIXER_GAIN, CHANNEL_GAIN, HEAD_GAIN, TAPS, BIAS = 0, 1, 2, 3, 7


def triangle(lower):
    row = lax.broadcasted_iota(jnp.int32, (CHUNK, CHUNK), 0)
    column = lax.broadcasted_iota(jnp.int32, (CHUNK, CHUNK), 1)
    return row >= column if lower else row <= column


def running_sums(blocks, lower):
    ones = jnp.where(triangle(lower), 1.0, 0.0).astype(BF16)
    parts = []
    for block in blocks:
        high = block.astype(BF16)
        parts += [high, (block - high.astype(F32)).astype(BF16)]
    sums = mm(ones, jnp.concatenate(parts, axis=1))
    width = blocks[0].shape[1]
    return [
        sums[:, 2 * i * width : (2 * i + 1) * width]
        + sums[:, (2 * i + 1) * width : (2 * i + 2) * width]
        for i in range(len(blocks))
    ]


def causal_pairs(sequences):
    total = sequences * CHUNK
    row = lax.broadcasted_iota(jnp.int32, (total, total), 0)
    column = lax.broadcasted_iota(jnp.int32, (total, total), 1)
    return jnp.logical_and(row // CHUNK == column // CHUNK, row >= column)


def spread(blocks):
    zeros = jnp.zeros_like(blocks[0])
    count = len(blocks)
    return jnp.concatenate(
        [
            jnp.concatenate([blocks[s] if t == s else zeros for t in range(count)], axis=1)
            for s in range(count)
        ],
        axis=0,
    )


def filter_rows(buffer, taps, count):
    total = taps[0:1, :] * buffer[pl.ds(8 - EDGE, count), :]
    for offset in range(1, CONV):
        total = total + taps[offset : offset + 1, :] * buffer[pl.ds(8 - EDGE + offset, count), :]
    return total


def front_body(
    tokens, mixer_gain, channel_gain, head_gain, filter_weight, decay_bias, lengths, w_proj,
    w_gate, w_rank, rank_up, edge_source, w_own,
    params, tok, normed, projected, low_rank, cumulative, states, before, out_gate, profile, gated, head,
    halo, entering, decays, w_others,
    extended, memory, preceding, head_local, edge_in, state_out, state_seq, w_here,
    edge_sem, seq_send, seq_recv, w_send, w_recv, w_store,
):
    step = pl.program_id(0)
    last_step = pl.num_programs(0) - 1
    sequences, size, width = tok.shape
    rank, dk = rank_up.shape
    c3, dv = w_proj.shape[1], w_gate.shape[1]
    per_step = size // CHUNK
    MESH = pl.DeviceIdType.MESH
    me, side, sides = lax.axis_index("mp"), lax.axis_index("seq"), lax.axis_size("seq")
    across = me + 1 - 2 * (me % 2)
    down = (me + 2) % 4
    peers = [(side + hop) % sides for hop in range(1, sides)]
    half = w_own.shape[0] // 2

    def remote(source, target, send, recv, axis, device):
        return pltpu.make_async_remote_copy(
            src_ref=source,
            dst_ref=target,
            send_sem=send,
            recv_sem=recv,
            device_id={axis: device},
            device_id_type=MESH,
        )

    edge_copy = remote(
        edge_source.at[pl.ds(edge_source.shape[0] - 8, 8)],
        edge_in,
        edge_sem.at[0],
        edge_sem.at[1],
        "seq",
        peers[0],
    )
    state_copies = [
        remote(state_out, state_seq.at[i], seq_send.at[i], seq_recv.at[i], "seq", peers[i])
        for i in range(sides - 1)
    ]
    first, second = pl.ds(0, half), pl.ds(half, half)
    weight_copies = [
        remote(w_own, w_here.at[0], w_send.at[0], w_recv.at[0], "mp", across),
        remote(w_own, w_here.at[1], w_send.at[1], w_recv.at[1], "mp", down),
        remote(
            w_here.at[0, first], w_here.at[2, first], w_send.at[2], w_recv.at[2], "mp", down
        ),
        remote(
            w_here.at[1, second], w_here.at[2, second], w_send.at[3], w_recv.at[3], "mp", across
        ),
    ]
    weights_out = pltpu.make_async_copy(w_here, w_others, w_store.at[0])
    barrier = pltpu.get_barrier_semaphore()

    @pl.when(step == 0)
    def _():
        for peer in peers:
            pl.semaphore_signal(barrier, inc=1, device_id={"seq": peer}, device_id_type=MESH)
        for peer in (across, down):
            pl.semaphore_signal(barrier, inc=1, device_id={"mp": peer}, device_id_type=MESH)
        memory[...] = jnp.zeros_like(memory)
        preceding[...] = jnp.zeros_like(preceding)
        params[...] = jnp.zeros_like(params)
        params[MIXER_GAIN : MIXER_GAIN + 1, :] = mixer_gain[...].astype(F32).reshape(1, width)
        params[CHANNEL_GAIN : CHANNEL_GAIN + 1, :] = channel_gain[...].astype(F32).reshape(1, width)
        params[HEAD_GAIN : HEAD_GAIN + 1, :dv] = head_gain[...].astype(F32).reshape(1, dv)
        column = lax.broadcasted_iota(jnp.int32, (1, 128), 1)
        limits = jnp.zeros((1, 128), F32)
        for s in range(sequences):
            limits = jnp.where(column == s, lengths[s].astype(F32), limits)
        params[HEAD_GAIN : HEAD_GAIN + 1, dv : dv + 128] = limits
        params[TAPS : TAPS + CONV, :c3] = filter_weight[...].astype(F32)
        params[BIAS : BIAS + 1, :dk] = decay_bias[...]

    @pl.when(step > 0)
    def _():
        extended[:, 0:8, :] = extended[:, size : size + 8, :]

    def first_norm(rows):
        inverse = lax.rsqrt(jnp.mean(rows * rows, axis=-1, keepdims=True) + EPS_NORM)
        return (rows * inverse * params[MIXER_GAIN : MIXER_GAIN + 1, :]).astype(BF16)

    here = jnp.swapaxes(tokens[...], 0, 1)
    tok[...] = here
    rounded = first_norm(here.reshape(sequences * size, width).astype(F32))
    normed[...] = rounded.reshape(sequences, size, width)
    projected_rows = mm(rounded, w_proj[...]).astype(BF16)
    projected[...] = projected_rows.reshape(sequences, size, c3)
    rows_here = pl.ds(pl.multiple_of(step * size, size), size)
    out_gate[:, rows_here, :] = mm(rounded, w_gate[...]).astype(BF16).reshape(sequences, size, dv)
    low_rows = mm_nt(rounded, w_rank[...]).astype(BF16)
    low_rank[...] = low_rows.reshape(sequences, size, rank)

    @pl.when(step == 0)
    def _():
        pl.semaphore_wait(barrier, sides - 1 + 2)
        edge_copy.start()
        for copy in weight_copies[:2]:
            copy.start()
        edge_copy.wait()
        edge = jnp.swapaxes(edge_in[...].astype(F32), 0, 1).reshape(sequences * 8, width)
        edge_rows = mm(first_norm(edge), w_proj[...]).astype(BF16).astype(F32)
        edge_rows = jnp.where(side > 0, edge_rows, 0.0).reshape(sequences, 8, c3)
        extended[:, 0:8, :] = edge_rows
        halo[...] = edge_rows

    @pl.when(step == 1)
    def _():
        for i in range(2):
            weight_copies[i].wait_recv()
            weight_copies[2 + i].start()

    taps = params[TAPS : TAPS + CONV, :c3]
    logit = mm(low_rows, rank_up[...]) + params[BIAS : BIAS + 1, :dk]
    decay = (jnp.minimum(logit, 0.0) - jnp.log1p(jnp.exp(-jnp.abs(logit)))) / GATE_NORMALIZER
    blocks = [
        decay[s * size + p * CHUNK : s * size + (p + 1) * CHUNK]
        for s in range(sequences)
        for p in range(per_step)
    ]
    totals = running_sums(blocks, True)
    convolved = []
    for s in range(sequences):
        rows = projected_rows[s * size : (s + 1) * size]
        extended[s, 8 : 8 + size, :] = rows.astype(F32)
        filtered = filter_rows(extended.at[s], taps, size)
        convolved.append((filtered * sigmoid(filtered)).astype(BF16))
    visible = causal_pairs(sequences)
    for p in range(per_step):
        rows = slice(p * CHUNK, (p + 1) * CHUNK)
        there = pl.ds(pl.multiple_of(step * size + p * CHUNK, CHUNK), CHUNK)
        lifted, lowered, profiles, tails, lasts = [], [], [], [], []
        for s in range(sequences):
            queries = convolved[s][rows, :dk].astype(F32)
            keys = convolved[s][rows, dk : 2 * dk].astype(F32)
            total = totals[s * per_step + p]
            middle, last = total[CHUNK // 2 - 1 : CHUNK // 2], total[CHUNK - 1 : CHUNK]
            lifted.append((queries * jnp.exp(total - middle)).astype(BF16))
            lowered.append((keys * jnp.exp(middle - total)).astype(BF16))
            inside = queries * jnp.exp(total)
            profiles.append(inside.astype(BF16))
            tails.append((keys * jnp.exp(last - total)).astype(BF16))
            lasts.append(last)
            gone = preceding[:, s * dk : (s + 1) * dk]
            profile[s, there, :] = (inside * jnp.exp(gone)).astype(BF16)
            cumulative[s, rows, :] = total
        values = jnp.concatenate([convolved[s][rows, 2 * dk :] for s in range(sequences)], axis=0)
        scores = mm_nt(jnp.concatenate(lifted, axis=0), jnp.concatenate(lowered, axis=0))
        scores = jnp.where(visible, scores, 0.0).astype(BF16)
        entry = memory[...]
        entry_low = entry.astype(BF16)
        states[p] = entry_low
        mixed = mm(scores, values) + mm_nt(spread(profiles), entry_low)
        for s in range(sequences):
            head_local[s, there, :] = mixed[s * CHUNK : (s + 1) * CHUNK]
        last = jnp.concatenate(lasts, axis=1)
        memory[...] = entry * jnp.exp(last) + mm_tn(values, spread(tails))
        before[step * per_step + p] = preceding[...]
        preceding[...] = preceding[...] + last

    @pl.when(step == last_step)
    def _():
        state_out[0:dv, :] = memory[...]
        state_out[dv : dv + 8, :] = jnp.broadcast_to(preceding[...], (8, sequences * dk))
        for copy in state_copies:
            copy.start()
        for copy in weight_copies[2:]:
            copy.wait_recv()
        weights_out.start()
        decays[...] = jnp.zeros_like(decays)
        for copy in state_copies:
            copy.wait_recv()
        total = jnp.zeros_like(memory)
        for behind in range(sides - 1, 0, -1):
            source = side - behind
            gone = state_seq[behind - 1, dv : dv + 1, :]
            decays[(source + sides) % sides] = gone
            longer = state_seq[behind - 1, 0:dv, :] + jnp.exp(gone) * total
            total = jnp.where(source >= 0, longer, total)
        entering[...] = total
        entry_low = total.astype(BF16)
        scale = dk ** (-0.5)

        def gate(index, carry):
            there = pl.ds(pl.multiple_of(index * size, size), size)
            for s in range(sequences):
                rows = head_local[s, there, :]
                rows = rows + mm_nt(profile[s, there, :], entry_low[:, s * dk : (s + 1) * dk])
                rows = rows * scale
                head[s, there, :] = rows.astype(BF16)
                inverse = lax.rsqrt(jnp.mean(rows * rows, axis=-1, keepdims=True) + EPS_HEAD)
                logits = out_gate[s, there, :].astype(F32)
                rows = rows * inverse * params[HEAD_GAIN : HEAD_GAIN + 1, :dv]
                gated[s, there, :] = (rows * (logits * sigmoid(logits))).astype(BF16)
            return carry

        lax.fori_loop(0, last_step + 1, gate, 0)
        edge_sends = state_copies + weight_copies
        for copy in edge_sends:
            copy.wait_send()
        weights_out.wait()


def front(
    tokens, mixer_gain, channel_gain, head_gain, filter_weight, decay_bias, lengths, w_proj,
    w_gate, w_rank, rank_up, w_own, seq_count,
):
    length, sequences, width = tokens.shape
    c3, dv = w_proj.shape[1], w_gate.shape[1]
    rank, dk = rank_up.shape
    chunks, per_step = length // CHUNK, STEP // CHUNK
    both = sequences * dk
    anywhere = pl.BlockSpec(memory_space=pl.ANY)
    dma = pltpu.SemaphoreType.DMA
    peers = seq_count - 1

    def steps(columns):
        return pl.BlockSpec((sequences, STEP, columns), lambda i: (0, i, 0))

    return pl.pallas_call(
        front_body,
        grid=(length // STEP,),
        in_specs=[
            pl.BlockSpec((STEP, sequences, width), lambda i: (i, 0, 0)),
            whole(mixer_gain.shape),
            whole(channel_gain.shape),
            whole(head_gain.shape),
            whole(filter_weight.shape),
            whole(decay_bias.shape),
            pl.BlockSpec(memory_space=pltpu.SMEM),
            whole(w_proj.shape),
            whole(w_gate.shape),
            whole(w_rank.shape),
            whole(rank_up.shape),
            anywhere,
            anywhere,
        ],
        out_specs=[
            whole((8, width)),
            steps(width),
            steps(width),
            steps(c3),
            steps(rank),
            steps(dk),
            pl.BlockSpec((per_step, dv, both), lambda i: (i, 0, 0)),
            whole((chunks, 1, both)),
            whole((sequences, length, dv)),
            whole((sequences, length, dk)),
            whole((sequences, length, dv)),
            whole((sequences, length, dv)),
            whole((sequences, 8, c3)),
            whole((dv, both)),
            whole((seq_count, 1, both)),
            anywhere,
        ],
        out_shape=[
            shape_of((8, width), F32),
            shape_of((sequences, length, width), BF16),
            shape_of((sequences, length, width), BF16),
            shape_of((sequences, length, c3), BF16),
            shape_of((sequences, length, rank), BF16),
            shape_of((sequences, length, dk), F32),
            shape_of((chunks, dv, both), BF16),
            shape_of((chunks, 1, both), F32),
            shape_of((sequences, length, dv), BF16),
            shape_of((sequences, length, dk), BF16),
            shape_of((sequences, length, dv), BF16),
            shape_of((sequences, length, dv), BF16),
            shape_of((sequences, 8, c3), F32),
            shape_of((dv, both), F32),
            shape_of((seq_count, 1, both), F32),
            shape_of((3, *w_own.shape), BF16),
        ],
        scratch_shapes=[
            pltpu.VMEM((sequences, STEP + 8, c3), F32),
            pltpu.VMEM((dv, both), F32),
            pltpu.VMEM((1, both), F32),
            pltpu.VMEM((sequences, length, dv), F32),
            pltpu.VMEM((8, sequences, width), BF16),
            pltpu.VMEM((dv + 8, both), F32),
            pltpu.VMEM((peers, dv + 8, both), F32),
            pltpu.VMEM((3, *w_own.shape), BF16),
            dma((2,)),
            dma((peers,)),
            dma((peers,)),
            dma((4,)),
            dma((4,)),
            dma((1,)),
        ],
        compiler_params=pltpu.CompilerParams(
            dimension_semantics=("arbitrary",),
            collective_id=2,
            has_side_effects=True,
            vmem_limit_bytes=VMEM_LIMIT,
        ),
        cost_estimate=pl.CostEstimate(
            flops=2 * sequences * length * width * (c3 + dv + 128),
            bytes_accessed=sequences * length * width * 8,
            transcendentals=0,
        ),
        name="front",
    )(
        tokens, mixer_gain, channel_gain, head_gain, filter_weight, decay_bias, lengths, w_proj,
        w_gate, w_rank, rank_up, tokens, w_own,
    )


PIECE = 128
HALF = PIECE // 2


def ffn_body(
    gated, w_own, w_others, tok, params, w_gate, w_up, w_down, cotangent,
    out_part, weight_grads, output_grads, grad_gated, own_residual, own_grad, gain_grad,
    g_across, g_down, g_far, tok_here, cot_here, up_here, wg, wu, wd, normed, hidden, grad_gate,
    grad_up,
    out_stage, part, via_across, via_down, from_across, from_down, residual_here, grad_here,
    mixer_here, pieces, received, weight_stage, output_stage,
    load_sem, row_sem, cot_sem, ag_send, ag_recv, rs_send, rs_recv, back_send, back_recv,
    store_sem, stage_sem, last_sem,
):
    turns = up_here.shape[0]
    halves = 2
    width = tok_here.shape[-1]
    me = lax.axis_index("mp")
    across = me + 1 - 2 * (me % 2)
    down = (me + 2) % 4
    far = 3 - me
    MESH = pl.DeviceIdType.MESH

    def remote(source, target, send, recv, device):
        return pltpu.make_async_remote_copy(
            src_ref=source,
            dst_ref=target,
            send_sem=send,
            recv_sem=recv,
            device_id={"mp": device},
            device_id_type=MESH,
        )

    def load(index, source, target):
        return pltpu.make_async_copy(source, target, load_sem.at[index])

    def load_tok(turn):
        return pltpu.make_async_copy(
            tok.at[turn // halves, :, turn % halves], tok_here.at[turn % 2], row_sem.at[turn]
        )

    def load_cot(block):
        start = pl.multiple_of(block * PIECE, PIECE)
        return pltpu.make_async_copy(
            cotangent.at[pl.ds(start, PIECE)], cot_here.at[block % 2], cot_sem.at[block % 2]
        )

    def direct(turn, side):
        return remote(
            gated.at[turn // halves, :, turn % halves],
            (g_across, g_down)[side].at[turn],
            ag_send.at[side, turn],
            ag_recv.at[side, turn],
            (across, down)[side],
        )

    def relay(turn, side):
        cut = pl.ds(2 * side, 2)
        return remote(
            (g_across, g_down)[side].at[turn, cut],
            g_far.at[turn, cut],
            ag_send.at[2 + side, turn],
            ag_recv.at[2 + side, turn],
            (down, across)[side],
        )

    first, second = pl.ds(0, HALF), pl.ds(HALF, HALF)

    def scatter(turn, index):
        source, target, device = (
            (part.at[turn, far, first], via_across.at[turn], across),
            (part.at[turn, far, second], via_down.at[turn], down),
            (part.at[turn, across, first], from_across.at[turn, first], across),
            (part.at[turn, down, second], from_down.at[turn, second], down),
            (part.at[turn, across, second], from_across.at[turn, second], across),
            (part.at[turn, down, first], from_down.at[turn, first], down),
        )[index]
        return remote(source, target, rs_send.at[index, turn], rs_recv.at[index, turn], device)

    def give_back(turn, slot):
        return remote(
            pieces.at[turn, slot],
            received.at[turn, slot],
            back_send.at[slot, turn],
            back_recv.at[slot, turn],
            (me, across, down, far)[slot],
        )

    def store_out(turn):
        return pltpu.make_async_copy(
            out_stage.at[turn % 2],
            out_part.at[turn // halves, :, turn % halves],
            store_sem.at[turn],
        )

    barrier = pltpu.get_barrier_semaphore()
    loads = [load(0, w_gate, wg), load(1, w_up, wu), load(2, w_down, wd)]
    for copy in loads:
        copy.start()
    blocks = cotangent.shape[0] // PIECE
    for turn in range(2):
        load_tok(turn).start()
        load_cot(turn).start()
    for device in (across, down, far):
        pl.semaphore_signal(barrier, inc=1, device_id={"mp": device}, device_id_type=MESH)
    pl.semaphore_wait(barrier, 3)
    for side in range(2):
        direct(0, side).start()
    gain_grad[...] = jnp.zeros_like(gain_grad)
    gain = params[CHANNEL_GAIN : CHANNEL_GAIN + 1, :]
    length = cotangent.shape[0]
    first_position = lax.axis_index("seq") * length

    def take_cotangent(block, carry):
        load_cot(block).wait()
        rows = jnp.swapaxes(cot_here[block % 2], 0, 1)
        position = first_position + block * PIECE
        position = (position + lax.broadcasted_iota(jnp.int32, (PIECE, 1), 0)).astype(F32)
        for s in range(turns // halves):
            column = gated.shape[-1] + s
            keep = position < params[HEAD_GAIN : HEAD_GAIN + 1, column : column + 1]
            kept = jnp.where(keep, rows[s].astype(F32), 0.0).astype(BF16)
            up_here[s * halves + block % halves, block // halves] = kept

        @pl.when(block + 2 < blocks)
        def _():
            load_cot(block + 2).start()

        return carry

    lax.fori_loop(0, blocks // 2, take_cotangent, 0)
    for side in range(2):
        direct(0, side).wait_recv()
        relay(0, side).start()
    for side in range(2):
        direct(1, side).start()
    lax.fori_loop(blocks // 2, blocks, take_cotangent, 0)
    for copy in loads:
        copy.wait()

    def forward_and_back(turn):
        load_tok(turn).wait()
        for side in range(2):
            relay(turn, side).wait_recv()
        rows = 4 * PIECE

        def flat(values):
            return values.reshape(rows, values.shape[-1])

        mixed = mm(flat(gated[turn // halves, :, turn % halves]), w_own[...])
        for slot, source in enumerate((g_across, g_down, g_far)):
            mixed = mixed + mm(flat(source[turn]), w_others[slot])
        residual = flat(tok_here[turn % 2]).astype(F32) + mixed
        for quarter in range(4):

            @pl.when(me == quarter)
            def _():
                residual_here[turn] = residual[quarter * PIECE : (quarter + 1) * PIECE]

        inverse = lax.rsqrt(jnp.mean(residual * residual, axis=-1, keepdims=True) + EPS_NORM)
        unit = residual * inverse
        rounded = (unit * gain).astype(BF16)
        normed[turn] = rounded
        gate_rows = mm_nt(rounded, wg[...])
        up_rows = mm_nt(rounded, wu[...])
        share = sigmoid(gate_rows)
        swished = gate_rows * share
        hidden_rows = (swished * up_rows).astype(BF16)
        hidden[turn] = hidden_rows
        grad_hidden = mm_nt(flat(up_here[turn]), wd[...])
        for side in range(2):

            @pl.when(turn + 1 < turns)
            def _():
                direct(turn + 1, side).wait_recv()
                relay(turn + 1, side).start()

        for side in range(2):

            @pl.when(turn + 2 < turns)
            def _():
                direct(turn + 2, side).start()

        slope = share * (1.0 + gate_rows * (1.0 - share))
        grad_gate_rows = (grad_hidden * up_rows * slope).astype(BF16)
        grad_up_rows = (grad_hidden * swished).astype(BF16)
        grad_gate[turn] = grad_gate_rows
        grad_up[turn] = grad_up_rows
        grad_rows = mm(grad_gate_rows, wg[...]) + mm(grad_up_rows, wu[...])
        part[turn] = grad_rows.astype(BF16).reshape(4, PIECE, width)
        for index in range(4):
            scatter(turn, index).start()
        gain_grad[...] += jnp.sum(grad_rows * unit, axis=0, keepdims=True)

        @pl.when(turn >= 2)
        def _():
            store_out(turn - 2).wait()

        out_stage[turn % 2] = mm(hidden_rows, wd[...]).astype(BF16).reshape(4, PIECE, width)
        store_out(turn).start()

        @pl.when(turn + 2 < turns)
        def _():
            load_tok(turn + 2).start()

    def pass_on(turn):
        scatter(turn, 0).wait_recv()
        part[turn, down, 0:HALF] = part[turn, down, 0:HALF] + via_across[turn]
        scatter(turn, 5).start()
        scatter(turn, 1).wait_recv()
        part[turn, across, HALF:PIECE] = part[turn, across, HALF:PIECE] + via_down[turn]
        scatter(turn, 4).start()

    def collect(turn):
        for index in range(2, 6):
            scatter(turn, index).wait_recv()
        grad_normed = part[turn, me].astype(F32) + from_across[turn].astype(F32)
        grad_normed = grad_normed + from_down[turn].astype(F32)
        residual = residual_here[turn]
        inverse = lax.rsqrt(jnp.mean(residual * residual, axis=-1, keepdims=True) + EPS_NORM)
        unit = residual * inverse
        scaled = grad_normed * gain
        through = inverse * (scaled - unit * jnp.mean(scaled * unit, axis=-1, keepdims=True))
        grad_residual = up_here[turn, me].astype(F32) + through
        grad_here[turn] = grad_residual
        grad_mixer = grad_residual.astype(BF16)
        mixer_here[turn] = grad_mixer
        for slot in range(4):
            weight = w_own[...] if slot == 0 else w_others[slot - 1]
            piece = mm_nt(grad_mixer, weight).astype(BF16)
            if slot == 0:
                received[turn, 0] = piece
            else:
                pieces[turn, slot] = piece
                give_back(turn, slot).start()

    tile = weight_stage.shape[2]
    tiles = width // tile

    def store_weight(kind, index, slot):
        return pltpu.make_async_copy(
            weight_stage.at[slot, kind],
            weight_grads.at[kind, pl.ds(index * tile, tile)],
            stage_sem.at[slot, kind],
        )

    all_rows = turns * 4 * PIECE

    def weight_tile(index, carry):
        slot = index % 2
        columns = pl.ds(pl.multiple_of(index * tile, tile), tile)

        @pl.when(index >= 2)
        def _():
            for kind in range(3):
                store_weight(kind, index - 2, slot).wait()

        left = normed[:, :, columns].reshape(all_rows, tile)
        upper = up_here[:, :, :, columns].reshape(all_rows, tile)
        units = hidden.shape[-1]
        for kind, (one, other) in enumerate(
            ((left, grad_gate), (left, grad_up), (upper, hidden))
        ):
            weight_stage[slot, kind] = mm_tn(one, other[...].reshape(all_rows, units)).astype(BF16)
            store_weight(kind, index, slot).start()
        return carry

    def round_of(index, carry):
        @pl.when(index < turns)
        def _():
            forward_and_back(index)

        @pl.when(index >= turns)
        def _():
            first_tile = (index - turns) * (tiles // 2)
            lax.fori_loop(first_tile, first_tile + tiles // 2, weight_tile, 0)

        @pl.when(jnp.logical_and(index >= 1, index <= turns))
        def _():
            pass_on(index - 1)

        @pl.when(index >= 2)
        def _():
            collect(index - 2)

        return carry

    lax.fori_loop(0, turns + 2, round_of, 0)
    mixer_rows = mixer_here[...].reshape(turns * PIECE, width)
    dv = gated.shape[-1]
    for slot in range(4):
        if slot == 0:
            blocks = [gated[t // halves, me, t % halves] for t in range(turns)]
        else:
            source = (None, g_across, g_down, g_far)[slot]
            blocks = [source[t, me] for t in range(turns)]
        rows = jnp.concatenate(blocks, axis=0)
        output_stage[slot] = mm_tn(mixer_rows, rows).astype(BF16)

    last = [
        pltpu.make_async_copy(residual_here, own_residual, last_sem.at[0]),
        pltpu.make_async_copy(grad_here, own_grad, last_sem.at[1]),
        pltpu.make_async_copy(output_stage, output_grads, last_sem.at[2]),
    ]
    for copy in last:
        copy.start()
    for turn in range(turns):
        for slot in range(1, 4):
            give_back(turn, slot).wait_recv()
        for slot in range(4):
            source = (me, across, down, far)[slot]
            pltpu.make_async_copy(
                received.at[turn, slot],
                grad_gated.at[turn // halves, source, turn % halves],
                last_sem.at[3 + turn * 4 + slot],
            ).start()
    for turn in range(turns):
        for slot in range(4):
            source = (me, across, down, far)[slot]
            pltpu.make_async_copy(
                received.at[turn, slot],
                grad_gated.at[turn // halves, source, turn % halves],
                last_sem.at[3 + turn * 4 + slot],
            ).wait()
        if turn >= turns - 2:
            store_out(turn).wait()
        for side in range(2):
            direct(turn, side).wait_send()
            relay(turn, side).wait_send()
        for index in range(6):
            scatter(turn, index).wait_send()
        for slot in range(1, 4):
            give_back(turn, slot).wait_send()
    for index in range(max(tiles - 2, 0), tiles):
        for kind in range(3):
            store_weight(kind, index, index % 2).wait()
    for copy in last:
        copy.wait()


def feed_forward(gated, w_own, w_others, tok, params, w_gate, w_up, w_down, cotangent):
    sequences, length, width = tok.shape
    dv, units = gated.shape[-1], w_gate.shape[0]
    halves = length // 4 // PIECE
    turns = sequences * halves

    def pieces_of(values):
        return values.reshape(sequences, 4, halves, PIECE, values.shape[-1])

    anywhere = pl.BlockSpec(memory_space=pl.ANY)
    vmem = pl.BlockSpec(memory_space=pltpu.VMEM)
    dma = pltpu.SemaphoreType.DMA
    rows = 4 * PIECE
    outs = pl.pallas_call(
        ffn_body,
        in_specs=[vmem] * 3 + [anywhere, vmem] + [anywhere] * 4,
        out_specs=[anywhere] * 6 + [vmem],
        out_shape=[
            shape_of((sequences, 4, halves, PIECE, width), BF16),
            shape_of((3, width, units), BF16),
            shape_of((4, width, dv), BF16),
            shape_of((sequences, 4, halves, PIECE, dv), BF16),
            shape_of((turns, PIECE, width), F32),
            shape_of((turns, PIECE, width), F32),
            shape_of((1, width), F32),
        ],
        scratch_shapes=[
            pltpu.VMEM((turns, 4, PIECE, dv), BF16),
            pltpu.VMEM((turns, 4, PIECE, dv), BF16),
            pltpu.VMEM((turns, 4, PIECE, dv), BF16),
            pltpu.VMEM((2, 4, PIECE, width), BF16),
            pltpu.VMEM((2, PIECE, sequences, width), BF16),
            pltpu.VMEM((turns, 4, PIECE, width), BF16),
            pltpu.VMEM((units, width), BF16),
            pltpu.VMEM((units, width), BF16),
            pltpu.VMEM((units, width), BF16),
            pltpu.VMEM((turns, rows, width), BF16),
            pltpu.VMEM((turns, rows, units), BF16),
            pltpu.VMEM((turns, rows, units), BF16),
            pltpu.VMEM((turns, rows, units), BF16),
            pltpu.VMEM((2, 4, PIECE, width), BF16),
            pltpu.VMEM((turns, 4, PIECE, width), BF16),
            pltpu.VMEM((turns, HALF, width), BF16),
            pltpu.VMEM((turns, HALF, width), BF16),
            pltpu.VMEM((turns, PIECE, width), BF16),
            pltpu.VMEM((turns, PIECE, width), BF16),
            pltpu.VMEM((turns, PIECE, width), F32),
            pltpu.VMEM((turns, PIECE, width), F32),
            pltpu.VMEM((turns, PIECE, width), BF16),
            pltpu.VMEM((turns, 4, PIECE, dv), BF16),
            pltpu.VMEM((turns, 4, PIECE, dv), BF16),
            pltpu.VMEM((2, 3, 256, units), BF16),
            pltpu.VMEM((4, width, dv), BF16),
            dma((3,)),
            dma((turns,)),
            dma((2,)),
            dma((4, turns)),
            dma((4, turns)),
            dma((6, turns)),
            dma((6, turns)),
            dma((4, turns)),
            dma((4, turns)),
            dma((turns,)),
            dma((2, 3)),
            dma((3 + 4 * turns,)),
        ],
        compiler_params=pltpu.CompilerParams(
            collective_id=0, has_side_effects=True, vmem_limit_bytes=64 * 2**20
        ),
        cost_estimate=pl.CostEstimate(
            flops=2 * sequences * length * width * (4 * dv + 9 * units),
            bytes_accessed=sequences * length * width * 8,
            transcendentals=0,
        ),
        name="feed_forward",
    )(
        pieces_of(gated), w_own, w_others, pieces_of(tok), params, w_gate, w_up, w_down, cotangent
    )
    out_part, weight_grads, output_grads, grad_gated, own_residual, own_grad, gain_grad = outs
    return (
        out_part.reshape(sequences, 4, length // 4, width),
        weight_grads,
        output_grads,
        grad_gated.reshape(sequences, length, dv),
        own_residual,
        own_grad,
        gain_grad,
    )


SMALL = 48


def paired_sum(own, received, order):
    terms = [own.astype(F32)] + [received[index].astype(F32) for index in order]
    while len(terms) > 1:
        half = len(terms) // 2
        terms = [terms[index] + terms[index + half] for index in range(half)]
    return terms[0]


def mixer_back_body(
    grad_gated_in, head_in, profile_in, out_gate_in, projected_in, cumulative_in, states_in,
    normed_in, tok_in, residual_in, grad_residual_in, out_part_in, hidden_grads, output_parts,
    w_proj_in, w_gate_in, low_rank, halo, params, rank_up, w_rank, before, entering,
    decays, channel_part,
    output, token_grads, hidden_out, mixer_out, small_out, shared_out,
    grad_gated, head, profile, out_gate, projected, cumulative, states, normed, tok, residual,
    grad_residual, part, w_proj, w_gate,
    hidden_kept, hidden_seq, hidden_dp, output_kept, output_seq, output_mp, output_dp,
    f_via_across, f_via_down, f_across, f_down, g_via_across, g_via_down, g_across, g_down,
    grad_out_gate, grad_head, grad_projected, grad_low_rank, mixer_grad, mixer_seq, mixer_dp,
    state_grad, state_seq, upstream, extended, grad_extended, edge_out, edge_in,
    small, small_low, small_seq, small_dp, small_mp, out_stage,
    load_sem, seq_send, seq_recv, dp_send, dp_recv, mp_send, mp_recv, f_send, f_recv,
    g_send, g_recv, store_sem,
):
    sequences, length, dv = grad_gated.shape
    width = normed.shape[-1]
    rank, dk = rank_up.shape
    c3 = projected.shape[-1]
    halves = 2
    turns = sequences * halves
    MESH = pl.DeviceIdType.MESH
    me, side, place = lax.axis_index("mp"), lax.axis_index("seq"), lax.axis_index("dp")
    sides, places = lax.axis_size("seq"), lax.axis_size("dp")
    across = me + 1 - 2 * (me % 2)
    down = (me + 2) % 4
    far = 3 - me
    share_rows = width // sides
    shard_rows = share_rows // places
    steps = length // STEP
    per_step = STEP // CHUNK
    first, second = pl.ds(0, HALF), pl.ds(HALF, HALF)

    def remote(source, target, send, recv, axis, device):
        return pltpu.make_async_remote_copy(
            src_ref=source,
            dst_ref=target,
            send_sem=send,
            recv_sem=recv,
            device_id={axis: device},
            device_id_type=MESH,
        )


    loads = [
        pltpu.make_async_copy(source, target, load_sem.at[index])
        for index, (source, target) in enumerate(
            [
                (grad_gated_in, grad_gated),
                (head_in, head),
                (profile_in, profile),
                (out_gate_in, out_gate),
                (out_part_in, part),
                (hidden_grads.at[:, pl.ds(side * share_rows, share_rows)], hidden_kept),
                (output_parts.at[:, pl.ds(side * share_rows, share_rows)], output_kept),
                (normed_in, normed),
                (projected_in, projected),
                (cumulative_in, cumulative),
                (states_in, states),
                (residual_in, residual),
                (w_proj_in, w_proj),
                (w_gate_in, w_gate),
                (grad_residual_in, grad_residual),
                (tok_in.at[:, me], tok),
            ]
        )
    ]

    def to_sides(kind, source_of, target):
        copies = []
        for hop in range(1, sides):
            peer = (side + hop) % sides
            copies.append(
                remote(
                    source_of(peer),
                    target.at[hop - 1],
                    seq_send.at[kind, hop - 1],
                    seq_recv.at[kind, hop - 1],
                    "seq",
                    peer,
                )
            )
        return copies

    def to_places(kind, source_of, target):
        copies = []
        for hop in range(1, places):
            peer = (place + hop) % places
            copies.append(
                remote(
                    source_of(peer),
                    target.at[hop - 1],
                    dp_send.at[kind, hop - 1],
                    dp_recv.at[kind, hop - 1],
                    "dp",
                    peer,
                )
            )
        return copies

    def to_heads(kind, source_of, target):
        return [
            remote(
                source_of(slot),
                target.at[slot - 1],
                mp_send.at[kind, slot - 1],
                mp_recv.at[kind, slot - 1],
                "mp",
                (me, across, down, far)[slot],
            )
            for slot in range(1, 4)
        ]

    def share_of(ref):
        return lambda peer: ref.at[:, pl.ds(peer * share_rows, share_rows)]

    def shard_of(ref):
        return lambda peer: ref.at[:, pl.ds(peer * shard_rows, shard_rows)]

    hidden_to_sides = to_sides(0, share_of(hidden_grads), hidden_seq)
    output_to_sides = to_sides(1, share_of(output_parts), output_seq)
    state_to_sides = to_sides(2, lambda peer: state_grad, state_seq)
    mixer_to_sides = to_sides(
        3, lambda peer: mixer_grad.at[pl.ds(peer * share_rows, share_rows)], mixer_seq
    )
    small_to_sides = to_sides(4, lambda peer: small_low.at[0], small_seq)
    edge_copy = remote(
        edge_out,
        edge_in,
        seq_send.at[5, 0],
        seq_recv.at[5, 0],
        "seq",
        (side + sides - 1) % sides,
    )
    hidden_to_places = to_places(0, shard_of(hidden_kept), hidden_dp)

    def own_share(peer):
        return pl.ds(pl.multiple_of(side * share_rows + peer * shard_rows, 16), shard_rows)

    mixer_to_places = to_places(1, lambda peer: mixer_grad.at[own_share(peer)], mixer_dp)
    output_to_places = to_places(
        2, lambda peer: output_kept.at[0, pl.ds(peer * shard_rows, shard_rows)], output_dp
    )
    small_to_places = to_places(3, lambda peer: small_low.at[1], small_dp)
    output_to_heads = to_heads(0, lambda slot: output_kept.at[slot], output_mp)
    small_to_heads = to_heads(1, lambda slot: small_low.at[2], small_mp)

    def scatter(turn, index, forward):
        if forward:
            via_across, via_down, from_across, from_down = (
                f_via_across, f_via_down, f_across, f_down,
            )
            send, recv = f_send, f_recv
        else:
            via_across, via_down, from_across, from_down = (
                g_via_across, g_via_down, g_across, g_down,
            )
            send, recv = g_send, g_recv
        s, h = turn // halves, turn % halves
        low, high = pl.ds(h * PIECE, HALF), pl.ds(h * PIECE + HALF, HALF)
        source, target, device = (
            (part.at[s, far, low], via_across.at[turn], across),
            (part.at[s, far, high], via_down.at[turn], down),
            (part.at[s, across, low], from_across.at[turn, first], across),
            (part.at[s, down, high], from_down.at[turn, second], down),
            (part.at[s, across, high], from_across.at[turn, second], across),
            (part.at[s, down, low], from_down.at[turn, first], down),
        )[index]
        return remote(source, target, send.at[index, turn], recv.at[index, turn], "mp", device)

    def pass_on(turn, forward):
        via_across, via_down = (
            (f_via_across, f_via_down) if forward else (g_via_across, g_via_down)
        )
        s, h = turn // halves, turn % halves
        low = pl.ds(h * PIECE, HALF)
        high = pl.ds(h * PIECE + HALF, HALF)
        scatter(turn, 0, forward).wait_recv()
        part[s, down, low] = part[s, down, low] + via_across[turn]
        scatter(turn, 5, forward).start()
        scatter(turn, 1, forward).wait_recv()
        part[s, across, high] = part[s, across, high] + via_down[turn]
        scatter(turn, 4, forward).start()

    def summed(turn, forward):
        from_across, from_down = (f_across, f_down) if forward else (g_across, g_down)
        for index in range(2, 6):
            scatter(turn, index, forward).wait_recv()
        s, h = turn // halves, turn % halves
        total = part[s, me, h * PIECE : (h + 1) * PIECE].astype(F32)
        return total + from_across[turn].astype(F32) + from_down[turn].astype(F32)

    def store(turn, kind):
        source, target = ((out_stage, output), (grad_residual, token_grads))[kind]
        return pltpu.make_async_copy(source.at[turn], target.at[turn], store_sem.at[kind, turn])


    barrier = pltpu.get_barrier_semaphore()
    for copy in loads:
        copy.start()
    for axis, peers in (
        ("seq", [(side + hop) % sides for hop in range(1, sides)]),
        ("mp", [across, down, far]),
        ("dp", [(place + hop) % places for hop in range(1, places)]),
    ):
        for peer in peers:
            pl.semaphore_signal(barrier, inc=1, device_id={axis: peer}, device_id_type=MESH)
    small[...] = jnp.zeros_like(small)
    state_grad[...] = jnp.zeros_like(state_grad)
    small[33:34, :] = channel_part[...]
    pl.semaphore_wait(barrier, sides - 1 + 3 + places - 1)
    for copy in hidden_to_sides + output_to_sides:
        copy.start()
    loads[4].wait()
    for turn in range(turns):
        for index in range(2):
            scatter(turn, index, True).start()
    for copy in loads[0:4]:
        copy.wait()


    scale = dk ** (-0.5)
    head_gain = params[HEAD_GAIN : HEAD_GAIN + 1, :dv]
    mixer_gain = params[MIXER_GAIN : MIXER_GAIN + 1, :]

    def ungate(index, carry):
        rows = pl.ds(pl.multiple_of(index * STEP, STEP), STEP)
        for s in range(sequences):
            upper = grad_gated[s, rows, :].astype(F32)
            head_rows_here = head[s, rows, :].astype(F32)
            inverse = lax.rsqrt(
                jnp.mean(head_rows_here * head_rows_here, axis=-1, keepdims=True) + EPS_HEAD
            )
            unit = head_rows_here * inverse
            logits = out_gate[s, rows, :].astype(F32)
            share = sigmoid(logits)
            slope = share * (1.0 + logits * (1.0 - share))
            grad_out_gate[s, rows, :] = (upper * unit * head_gain * slope).astype(BF16)
            grad_normed = upper * (logits * share)
            small[34:35, :dv] += jnp.sum(grad_normed * unit, axis=0, keepdims=True)
            scaled = grad_normed * head_gain
            through = inverse * (scaled - unit * jnp.mean(scaled * unit, axis=-1, keepdims=True))
            rounded = (through * scale).astype(BF16)
            grad_head[s, rows, :] = rounded
            state_grad[:, s * dk : (s + 1) * dk] += mm_tn(rounded, profile[s, rows, :])
        return carry

    lax.fori_loop(0, steps, ungate, 0)
    for copy in state_to_sides:
        copy.start()
    for turn in range(turns):
        for index in range(2, 4):
            scatter(turn, index, True).start()
    loads[5].wait()
    for copy in hidden_to_sides:
        copy.wait_recv()
    hidden_sum = hidden_kept[...]
    for hop in range(sides - 1):
        hidden_sum = hidden_sum + hidden_seq[hop]
    hidden_kept[...] = hidden_sum
    for copy in hidden_to_places:
        copy.start()
    loads[6].wait()
    for copy in output_to_sides:
        copy.wait_recv()
    output_sum = output_kept[...]
    for hop in range(sides - 1):
        output_sum = output_sum + output_seq[hop]
    output_kept[...] = output_sum
    for copy in output_to_heads:
        copy.start()
    for copy in loads[7:11]:
        copy.wait()
    for copy in state_to_sides:
        copy.wait_recv()
    total = jnp.zeros_like(upstream)
    for ahead in range(sides - 1, 0, -1):
        source = side + ahead
        decay = decays[source % sides]
        longer = state_seq[sides - ahead - 1] + jnp.exp(decay) * total
        total = jnp.where(source < sides, longer, total)
    upstream[...] = total
    grad_extended[:, STEP : STEP + 8, :] = jnp.zeros_like(grad_extended[:, STEP : STEP + 8, :])


    taps = params[TAPS : TAPS + CONV, :c3]
    causal = triangle(True)

    def backward_step(back, carry):
        step = steps - 1 - back
        start = pl.multiple_of(step * STEP, STEP)

        @pl.when(back > 0)
        def _():
            grad_extended[:, STEP : STEP + 8, :] = grad_extended[:, 0:8, :]

        @pl.when(step == 0)
        def _():
            extended[:, 0:8, :] = halo[...]

        @pl.when(step > 0)
        def _():
            earlier = projected[:, pl.ds(pl.multiple_of(jnp.maximum(start - 16, 0), 16), 16), :]
            extended[:, 0:8, :] = earlier.astype(F32)[:, 8:16, :]

        for s in range(sequences):
            here = pl.ds(start, STEP)
            extended[s, 8 : 8 + STEP, :] = projected[s, here, :].astype(F32)
            filtered = filter_rows(extended.at[s], taps, STEP)
            share = sigmoid(filtered)
            convolved = (filtered * share).astype(BF16)
            slope = share * (1.0 + filtered * (1.0 - share))
            low_rows = low_rank[s, here, :]
            logit = mm(low_rows, rank_up[...]) + params[BIAS : BIAS + 1, :dk]
            logit_grads = [None] * per_step
            for piece in reversed(range(per_step)):
                rows = slice(piece * CHUNK, (piece + 1) * CHUNK)
                there = pl.ds(start + piece * CHUNK, CHUNK)
                queries = convolved[rows, :dk].astype(F32)
                keys = convolved[rows, dk : 2 * dk].astype(F32)
                values = convolved[rows, 2 * dk :]
                grad_rows = grad_head[s, there, :]
                total = cumulative[s, there, :]
                middle, last = total[CHUNK // 2 - 1 : CHUNK // 2], total[CHUNK - 1 : CHUNK]
                lift, lower = jnp.exp(total - middle), jnp.exp(middle - total)
                inner, outer = jnp.exp(total), jnp.exp(last - total)
                whole_decay = jnp.exp(last)
                lifted, lowered = (queries * lift).astype(BF16), (keys * lower).astype(BF16)
                inside, tails = (queries * inner).astype(BF16), (keys * outer).astype(BF16)
                own = slice(s * dk, (s + 1) * dk)
                previous = before[step * per_step + piece, :, own]
                state = states[step * per_step + piece, :, own].astype(F32)
                state = state + entering[:, own] * jnp.exp(previous)
                scores = jnp.where(causal, mm_nt(lifted, lowered), 0.0).astype(BF16)
                grad_scores = jnp.where(causal, mm_nt(grad_rows, values), 0.0).astype(BF16)
                later = upstream[:, own]
                later_low = later.astype(BF16)
                grad_values = mm_tn(scores, grad_rows) + mm_nt(tails, later_low)
                grad_lifted = mm(grad_scores, lowered)
                grad_lowered = mm_tn(grad_scores, lifted)
                grad_inside = mm(grad_rows, state.astype(BF16))
                grad_tails = mm(values, later_low)
                upstream[:, own] = later * whole_decay + mm_tn(grad_rows, inside)
                tail_terms = tails.astype(F32) * grad_tails
                grad_total = (
                    lifted.astype(F32) * grad_lifted
                    - lowered.astype(F32) * grad_lowered
                    + inside.astype(F32) * grad_inside
                    - tail_terms
                )
                grad_last = jnp.sum(tail_terms, axis=0, keepdims=True) + whole_decay * jnp.sum(
                    later * state, axis=0, keepdims=True
                )
                grad_decay = running_sums([grad_total], False)[0] + grad_last
                logit_grads[piece] = grad_decay / GATE_NORMALIZER * sigmoid(-logit[rows])
                grad_extended[s, rows, :dk] = (
                    grad_lifted * lift + grad_inside * inner
                ) * slope[rows, :dk]
                grad_extended[s, rows, dk : 2 * dk] = (
                    grad_lowered * lower + grad_tails * outer
                ) * slope[rows, dk : 2 * dk]
                grad_extended[s, rows, 2 * dk :] = grad_values * slope[rows, 2 * dk :]
            logit_grad = jnp.concatenate(logit_grads, axis=0)
            logit_low = logit_grad.astype(BF16)
            small[35:36, :dk] += jnp.sum(logit_grad, axis=0, keepdims=True)
            small[16 : 16 + rank, :dk] += mm_tn(low_rows, logit_low)
            grad_low_rank[s, here, :] = mm_nt(logit_low, rank_up[...]).astype(BF16)
            total_rows = taps[EDGE : EDGE + 1, :] * grad_extended[s, 0:STEP, :]
            for offset in range(EDGE):
                total_rows = total_rows + taps[offset : offset + 1, :] * grad_extended[
                    s, pl.ds(EDGE - offset, STEP), :
                ]
            grad_projected[s, here, :] = total_rows.astype(BF16)
            grad_filtered = grad_extended[s, 0:STEP, :]
            for offset in range(CONV):
                small[16 + offset : 17 + offset, dk : dk + c3] += jnp.sum(
                    grad_filtered * extended[s, pl.ds(8 - EDGE + offset, STEP), :],
                    axis=0,
                    keepdims=True,
                )
        for turn in range(turns):

            @pl.when(back == turn % steps)
            def _():
                pass_on(turn, True)

        return carry

    lax.fori_loop(0, steps, backward_step, 0)


    edge_out[...] = jnp.zeros_like(edge_out)
    for s in range(sequences):
        rows = grad_extended[s, 0:8, :]
        for i in range(EDGE):
            edge_row = taps[0:1] * rows[i : i + 1]
            for j in range(1, i + 1):
                edge_row = edge_row + taps[j : j + 1] * rows[i - j : i - j + 1]
            edge_out[s, 16 - EDGE + i : 17 - EDGE + i, :] = edge_row
    edge_copy.start()


    loads[11].wait()
    for turn in range(turns):
        s, h = turn // halves, turn % halves
        total = residual[turn] + summed(turn, True)
        position = side * length + me * (length // 4) + h * PIECE
        position = position + lax.broadcasted_iota(jnp.int32, (PIECE, 1), 0)
        limit = params[HEAD_GAIN : HEAD_GAIN + 1, dv + s : dv + s + 1]
        out_stage[turn] = jnp.where(position.astype(F32) < limit, total, 0.0).astype(BF16)
        store(turn, 0).start()
    for turn in range(turns):
        for index in range(6):
            scatter(turn, index, True).wait_send()
    edge_copy.wait_recv()
    for s in range(sequences):
        tail = grad_projected[s, length - 16 :, :].astype(F32)
        tail = tail + jnp.where(side < sides - 1, edge_in[s], 0.0)
        grad_projected[s, length - 16 :, :] = tail.astype(BF16)


    loads[12].wait()
    loads[13].wait()

    def input_grad(turn):
        s, h = turn // halves, turn % halves
        quarter = length // 4

        def rows_of_turn(ref):
            blocks = [
                ref[s, q * quarter + h * PIECE : q * quarter + (h + 1) * PIECE, :]
                for q in range(4)
            ]
            return jnp.concatenate(blocks, axis=0)

        total = mm_nt(rows_of_turn(grad_projected), w_proj[...])
        total = total + mm_nt(rows_of_turn(grad_out_gate), w_gate[...])
        total = total + mm(rows_of_turn(grad_low_rank), w_rank[...])
        rounded = total.astype(BF16)
        for q in range(4):
            part[s, q, h * PIECE : (h + 1) * PIECE] = rounded[q * PIECE : (q + 1) * PIECE]
        for index in range(4):
            scatter(turn, index, False).start()
        small[32:33, :] += jnp.sum(
            total * rows_of_turn(normed).astype(F32), axis=0, keepdims=True
        )

    for turn in range(turns):
        input_grad(turn)


    flat = sequences * length
    tile = 256

    def weight_tile(index, carry):
        columns = pl.ds(pl.multiple_of(index * tile, tile), tile)
        left = normed[:, :, columns].reshape(flat, tile)
        mixer_grad[columns, :c3] = mm_tn(left, grad_projected[...].reshape(flat, c3)).astype(BF16)
        mixer_grad[columns, c3:] = mm_tn(left, grad_out_gate[...].reshape(flat, dv)).astype(BF16)
        small[0:rank, columns] = mm_tn(grad_low_rank[...].reshape(flat, rank), left)
        return carry

    lax.fori_loop(0, width // tile, weight_tile, 0)
    small_low[0] = small[...].astype(BF16)
    for copy in small_to_sides + mixer_to_sides:
        copy.start()
    pass_on(0, False)
    for copy in output_to_heads:
        copy.wait_recv()
    output_kept[0] = output_kept[0] + output_mp[0] + output_mp[1] + output_mp[2]
    for copy in output_to_places:
        copy.start()
    for copy in small_to_sides:
        copy.wait_recv()
    small_low[1] = paired_sum(small_low[0], small_seq, range(sides - 1)).astype(BF16)
    for copy in small_to_places:
        copy.start()
    for copy in mixer_to_sides:
        copy.wait_recv()
    own = pl.ds(pl.multiple_of(side * share_rows, 16), share_rows)
    mixer_sum = mixer_grad[own, :]
    for hop in range(sides - 1):
        mixer_sum = mixer_sum + mixer_seq[hop]
    mixer_grad[own, :] = mixer_sum
    for copy in mixer_to_places:
        copy.start()
    pass_on(1, False)
    for copy in small_to_places:
        copy.wait_recv()
    summed_here = paired_sum(small_low[1], small_dp, range(places - 1))
    small_low[2] = summed_here.astype(BF16)
    shard, shards = side * places + place, sides * places

    def own_columns(values):
        size = values.shape[1] // shards
        total = values[:, 0:size]
        for index in range(1, shards):
            total = jnp.where(shard == index, values[:, index * size : (index + 1) * size], total)
        return total

    small_out[0:CONV, : c3 // shards] = own_columns(summed_here[16 : 16 + CONV, dk : dk + c3])
    small_out[8 : 8 + rank, : dk // shards] = own_columns(summed_here[16 : 16 + rank, :dk])
    small_out[24:25, : dk // shards] = own_columns(summed_here[35:36, :dk])
    for copy in small_to_heads:
        copy.start()
    pass_on(2, False)
    for copy in hidden_to_places:
        copy.wait_recv()
    own_shard = pl.ds(pl.multiple_of(place * shard_rows, 16), shard_rows)
    for kind in range(3):
        total = hidden_kept[kind, own_shard, :].astype(F32)
        for hop in range(places - 1):
            total = total + hidden_dp[hop, kind].astype(F32)
        hidden_out[kind] = total
    pass_on(3, False)


    loads[14].wait()
    loads[15].wait()
    for turn in range(turns):
        s, h = turn // halves, turn % halves
        grad_normed = summed(turn, False)
        rows = tok[s, h * PIECE : (h + 1) * PIECE].astype(F32)
        inverse = lax.rsqrt(jnp.mean(rows * rows, axis=-1, keepdims=True) + EPS_NORM)
        unit = rows * inverse
        scaled = grad_normed * mixer_gain
        through = inverse * (scaled - unit * jnp.mean(scaled * unit, axis=-1, keepdims=True))
        grad_residual[turn] = grad_residual[turn] + through
        store(turn, 1).start()
    for copy in small_to_heads:
        copy.wait_recv()
    shared = paired_sum(small_low[2], small_mp, (1, 0, 2))
    shared_out[...] = shared
    shared_out[32:33, :] = shared[32:33, :] / mixer_gain
    for copy in mixer_to_places + output_to_places:
        copy.wait_recv()
    total = mixer_grad[own_share(place), :].astype(F32)
    for hop in range(places - 1):
        total = total + mixer_dp[hop].astype(F32)
    mixer_out[:, : c3 + dv] = total
    total = output_kept[0, own_shard, :].astype(F32)
    for hop in range(places - 1):
        total = total + output_dp[hop].astype(F32)
    mixer_out[:, c3 + dv :] = total


    for copies in (
        hidden_to_sides, output_to_sides, state_to_sides, mixer_to_sides, small_to_sides,
        [edge_copy], hidden_to_places, mixer_to_places, output_to_places, small_to_places,
        output_to_heads, small_to_heads,
    ):
        for copy in copies:
            copy.wait_send()
    for turn in range(turns):
        for index in range(6):
            scatter(turn, index, False).wait_send()
        store(turn, 0).wait()
        store(turn, 1).wait()


def mixer_back(
    grad_gated, head, profile, out_gate, projected, cumulative, states, normed, tok, residual,
    grad_residual, out_part, hidden_grads, output_parts, w_proj, w_gate, low_rank, halo, params,
    rank_up, w_rank, before, entering, decays, channel_part, seq_count, dp_count,
):
    sequences, length, width = normed.shape
    dv, c3 = grad_gated.shape[-1], projected.shape[-1]
    rank, dk = rank_up.shape
    units = hidden_grads.shape[-1]
    quarter = length // 4
    turns = sequences * quarter // PIECE
    share_rows = width // seq_count
    shard_rows = share_rows // dp_count
    peers, others = seq_count - 1, dp_count - 1
    anywhere = pl.BlockSpec(memory_space=pl.ANY)
    vmem = pl.BlockSpec(memory_space=pltpu.VMEM)
    dma = pltpu.SemaphoreType.DMA

    def low(*shape):
        return pltpu.VMEM(shape, BF16)

    def full(*shape):
        return pltpu.VMEM(shape, F32)

    hops = [
        low(turns, HALF, width),
        low(turns, HALF, width),
        low(turns, PIECE, width),
        low(turns, PIECE, width),
    ]
    return pl.pallas_call(
        mixer_back_body,
        in_specs=[anywhere] * 16 + [vmem] * 9,
        out_specs=[anywhere] * 2 + [vmem] * 4,
        out_shape=[
            shape_of((turns, PIECE, width), BF16),
            shape_of((turns, PIECE, width), F32),
            shape_of((3, shard_rows, units), F32),
            shape_of((shard_rows, c3 + 2 * dv), F32),
            shape_of((32, 128), F32),
            shape_of((SMALL, width), F32),
        ],
        scratch_shapes=[
            low(sequences, length, dv),
            low(sequences, length, dv),
            low(sequences, length, dk),
            low(sequences, length, dv),
            low(sequences, length, c3),
            full(sequences, length, dk),
            low(length // CHUNK, dv, sequences * dk),
            low(sequences, length, width),
            low(sequences, quarter, width),
            full(turns, PIECE, width),
            full(turns, PIECE, width),
            low(sequences, 4, quarter, width),
            low(width, c3),
            low(width, dv),
            low(3, share_rows, units),
            low(peers, 3, share_rows, units),
            low(others, 3, shard_rows, units),
            low(4, share_rows, dv),
            low(peers, 4, share_rows, dv),
            low(3, share_rows, dv),
            low(others, shard_rows, dv),
            *hops,
            *hops,
            low(sequences, length, dv),
            low(sequences, length, dv),
            low(sequences, length, c3),
            low(sequences, length, rank),
            low(width, c3 + dv),
            low(peers, share_rows, c3 + dv),
            low(others, shard_rows, c3 + dv),
            full(dv, sequences * dk),
            full(peers, dv, sequences * dk),
            full(dv, sequences * dk),
            full(sequences, STEP + 8, c3),
            full(sequences, STEP + 8, c3),
            full(sequences, 16, c3),
            full(sequences, 16, c3),
            full(SMALL, width),
            low(3, SMALL, width),
            low(peers, SMALL, width),
            low(others, SMALL, width),
            low(3, SMALL, width),
            low(turns, PIECE, width),
            dma((16,)),
            dma((6, peers)),
            dma((6, peers)),
            dma((4, others)),
            dma((4, others)),
            dma((2, 3)),
            dma((2, 3)),
            dma((6, turns)),
            dma((6, turns)),
            dma((6, turns)),
            dma((6, turns)),
            dma((2, turns)),
        ],
        compiler_params=pltpu.CompilerParams(
            collective_id=1, has_side_effects=True, vmem_limit_bytes=64 * 2**20
        ),
        cost_estimate=pl.CostEstimate(
            flops=2 * sequences * length * width * 2 * (c3 + dv) * 2,
            bytes_accessed=sequences * length * width * 16,
            transcendentals=0,
        ),
        name="mixer_back",
    )(
        grad_gated, head, profile, out_gate, projected, cumulative, states, normed, tok, residual,
        grad_residual, out_part, hidden_grads, output_parts, w_proj, w_gate, low_rank, halo,
        params, rank_up, w_rank, before, entering, decays, channel_part,
    )


def finish_body(
    outputs, token_grads, hidden, mixer, small, shared,
    output, tokens_grad, mixer_gain, project, filters, rank_down, rank_up, bias, w_gate,
    head_gain, w_out, channel_gain, hidden_gate, hidden_up, hidden_down,
):
    output[...] = jnp.swapaxes(outputs[:, 0], 0, 1)
    tokens_grad[...] = jnp.swapaxes(token_grads[:, 0], 0, 1)

    @pl.when(pl.program_id(0) == 0)
    def _():
        c3, dv = project.shape[-1], w_gate.shape[-1]
        project[:, 0, :] = mixer[:, :c3]
        w_gate[...] = mixer[:, c3 : c3 + dv]
        w_out[...] = mixer[:, c3 + dv :].T
        for s in range(filters.shape[0]):
            filters[s] = small[s : s + 1, : filters.shape[-1]]
        for s in range(rank_up.shape[0]):
            rank_up[s] = small[8 + s : 9 + s, : rank_up.shape[-1]]
        bias[...] = small[24:25, : bias.shape[-1]]
        rank_down[...] = shared[: rank_down.shape[0], :]
        mixer_gain[...] = shared[32:33, :]
        channel_gain[...] = shared[33:34, :]
        head_gain[...] = shared[34:35, :dv]
        for target, kind in ((hidden_gate, 0), (hidden_up, 1), (hidden_down, 2)):
            target[...] = hidden[kind].T


def finish(outputs, token_grads, hidden, mixer, small, shared, sequences, c3, dv, dk, rank, shards):
    turns, piece, width = outputs.shape
    halves = turns // sequences
    rows, units = hidden.shape[1:]

    def by_half(values):
        return values.reshape(sequences, halves, piece, width)

    half = pl.BlockSpec((sequences, 1, piece, width), lambda i: (0, i, 0, 0))
    placed = pl.BlockSpec((piece, sequences, width), lambda i: (i, 0, 0))
    shapes = [
        (1, width),
        (rows, 1, c3),
        (CONV, 1, c3 // shards),
        (rank, width),
        (rank, 1, dk // shards),
        (1, dk // shards),
        (rows, dv),
        (1, dv),
        (dv, rows),
        (1, width),
        (units, rows),
        (units, rows),
        (units, rows),
    ]
    return pl.pallas_call(
        finish_body,
        grid=(halves,),
        in_specs=[half, half] + [whole(v.shape) for v in (hidden, mixer, small, shared)],
        out_specs=[placed, placed] + [whole(shape) for shape in shapes],
        out_shape=[
            shape_of((halves * piece, sequences, width), BF16),
            shape_of((halves * piece, sequences, width), F32),
        ]
        + [shape_of(shape, F32) for shape in shapes],
        compiler_params=pltpu.CompilerParams(
            dimension_semantics=("arbitrary",), vmem_limit_bytes=VMEM_LIMIT
        ),
        name="finish",
    )(by_half(outputs), by_half(token_grads), hidden, mixer, small, shared)


def on_device(
    tokens, lengths, mixer_gain, project_weight, filter_weight, rank_down, rank_up, decay_bias,
    gate_weight, head_gain, output_weight, channel_gain, hidden_gate, hidden_up, hidden_down,
    cotangent,
):
    length, sequences, width = tokens.shape
    seq_count, dp_count = lax.axis_size("seq"), lax.axis_size("dp")
    shards = seq_count * dp_count
    own_rows = length // lax.axis_size("mp")
    w_proj, rank_up_here = project_weight[:, 0], rank_up[:, 0]
    c3, dv = w_proj.shape[1], gate_weight.shape[1]
    rank, dk = rank_up_here.shape
    w_rank = rank_down.T
    (
        params, tok, normed, projected, low_rank, cumulative, states, before, out_gate, profile,
        gated, head, halo, entering, decays, w_others,
    ) = front(
        tokens, mixer_gain, channel_gain, head_gain, filter_weight[:, 0], decay_bias, lengths,
        w_proj, gate_weight, w_rank, rank_up_here, output_weight, seq_count,
    )
    (
        out_part, hidden_grads, output_parts, grad_gated, residual, grad_residual, channel_part,
    ) = feed_forward(
        gated, output_weight, w_others, tok, params, hidden_gate.T, hidden_up.T, hidden_down,
        cotangent,
    )
    results = mixer_back(
        grad_gated, head, profile, out_gate, projected, cumulative, states, normed,
        tok.reshape(sequences, 4, own_rows, width), residual, grad_residual, out_part,
        hidden_grads, output_parts, w_proj, gate_weight, low_rank, halo, params, rank_up_here,
        w_rank, before, entering, decays, channel_part, seq_count, dp_count,
    )
    (
        output, tokens_grad, mixer_gain_grad, project_grad, filter_grad, rank_down_grad,
        rank_up_grad, decay_bias_grad, gate_grad, head_gain_grad, output_weight_grad,
        channel_gain_grad, hidden_gate_grad, hidden_up_grad, hidden_down_grad,
    ) = finish(*results, sequences, c3, dv, dk, rank, shards)
    return (
        output,
        tokens_grad,
        mixer_gain_grad[0],
        project_grad,
        filter_grad,
        rank_down_grad.T,
        rank_up_grad,
        decay_bias_grad,
        gate_grad,
        head_gain_grad[0],
        output_weight_grad,
        channel_gain_grad[0],
        hidden_gate_grad.T,
        hidden_up_grad.T,
        hidden_down_grad,
    )


def solution(mesh):
    in_specs = (
        P("seq", "dp", None),
        P("dp"),
        P(),
        P(None, "mp", None),
        P(None, "mp", None),
        P(),
        P(None, "mp", None),
        P("mp", None),
        P(None, "mp"),
        P(),
        P("mp", None),
        P(),
        P(None, "mp"),
        P(None, "mp"),
        P("mp", None),
        P("seq", "dp", None),
    )
    out_specs = (
        P(("seq", "mp"), "dp", None),
        P(("seq", "mp"), "dp", None),
        P(),
        P(("seq", "dp"), "mp", None),
        P(None, "mp", ("seq", "dp")),
        P(),
        P(None, "mp", ("seq", "dp")),
        P("mp", ("seq", "dp")),
        P(("seq", "dp"), "mp"),
        P(),
        P("mp", ("seq", "dp")),
        P(),
        P(("seq", "dp"), "mp"),
        P(("seq", "dp"), "mp"),
        P("mp", ("seq", "dp")),
    )
    return jax.shard_map(
        on_device, mesh=mesh, in_specs=in_specs, out_specs=out_specs, check_vma=False
    )
```

```python
import jax
import jax.numpy as jnp
from jax import lax
from jax.experimental import pallas as pl
from jax.experimental.pallas import tpu as pltpu
from jax.sharding import PartitionSpec as P

CONV = 4
EDGE = CONV - 1
CHUNK = 128
STEP = 256
EPS_NORM = 1e-06
EPS_HEAD = 1e-05
GATE_NORMALIZER = 16.0
BF16 = jnp.bfloat16
F32 = jnp.float32
VMEM_LIMIT = 56 * 2**20


def mm(left, right):
    return lax.dot_general(left, right, (((1,), (0,)), ((), ())), preferred_element_type=F32)


def mm_nt(left, right):
    return lax.dot_general(left, right, (((1,), (1,)), ((), ())), preferred_element_type=F32)


def mm_tn(left, right):
    return lax.dot_general(left, right, (((0,), (0,)), ((), ())), preferred_element_type=F32)


def sigmoid(values):
    return 1.0 / (1.0 + jnp.exp(-values))


def whole(shape):
    return pl.BlockSpec(shape, lambda *_: (0,) * len(shape))


def shape_of(shape, dtype):
    return jax.ShapeDtypeStruct(shape, dtype)


MIXER_GAIN, CHANNEL_GAIN, HEAD_GAIN, TAPS, BIAS = 0, 1, 2, 3, 7


def triangle(lower):
    row = lax.broadcasted_iota(jnp.int32, (CHUNK, CHUNK), 0)
    column = lax.broadcasted_iota(jnp.int32, (CHUNK, CHUNK), 1)
    return row >= column if lower else row <= column


def running_sums(blocks, lower):
    ones = jnp.where(triangle(lower), 1.0, 0.0).astype(BF16)
    parts = []
    for block in blocks:
        high = block.astype(BF16)
        parts += [high, (block - high.astype(F32)).astype(BF16)]
    sums = mm(ones, jnp.concatenate(parts, axis=1))
    width = blocks[0].shape[1]
    return [
        sums[:, 2 * i * width : (2 * i + 1) * width]
        + sums[:, (2 * i + 1) * width : (2 * i + 2) * width]
        for i in range(len(blocks))
    ]


def causal_pairs(sequences):
    total = sequences * CHUNK
    row = lax.broadcasted_iota(jnp.int32, (total, total), 0)
    column = lax.broadcasted_iota(jnp.int32, (total, total), 1)
    return jnp.logical_and(row // CHUNK == column // CHUNK, row >= column)


def spread(blocks):
    zeros = jnp.zeros_like(blocks[0])
    count = len(blocks)
    return jnp.concatenate(
        [
            jnp.concatenate([blocks[s] if t == s else zeros for t in range(count)], axis=1)
            for s in range(count)
        ],
        axis=0,
    )


def filter_rows(buffer, taps, count):
    total = taps[0:1, :] * buffer[pl.ds(8 - EDGE, count), :]
    for offset in range(1, CONV):
        total = total + taps[offset : offset + 1, :] * buffer[pl.ds(8 - EDGE + offset, count), :]
    return total


def front_body(
    tokens, mixer_gain, channel_gain, head_gain, filter_weight, decay_bias, lengths, w_proj,
    w_gate, w_rank, rank_up, edge_source, w_own,
    params, tok, normed, projected, low_rank, cumulative, states, before, out_gate, profile, gated, head,
    halo, entering, decays, w_others,
    extended, memory, preceding, head_local, edge_in, state_out, state_seq, w_here,
    edge_sem, seq_send, seq_recv, w_send, w_recv, w_store,
):
    step = pl.program_id(0)
    last_step = pl.num_programs(0) - 1
    sequences, size, width = tok.shape
    rank, dk = rank_up.shape
    c3, dv = w_proj.shape[1], w_gate.shape[1]
    per_step = size // CHUNK
    MESH = pl.DeviceIdType.MESH
    me, side, sides = lax.axis_index("mp"), lax.axis_index("seq"), lax.axis_size("seq")
    across = me + 1 - 2 * (me % 2)
    down = (me + 2) % 4
    peers = [(side + hop) % sides for hop in range(1, sides)]
    half = w_own.shape[0] // 2

    def remote(source, target, send, recv, axis, device):
        return pltpu.make_async_remote_copy(
            src_ref=source,
            dst_ref=target,
            send_sem=send,
            recv_sem=recv,
            device_id={axis: device},
            device_id_type=MESH,
        )

    edge_copy = remote(
        edge_source.at[pl.ds(edge_source.shape[0] - 8, 8)],
        edge_in,
        edge_sem.at[0],
        edge_sem.at[1],
        "seq",
        peers[0],
    )
    state_copies = [
        remote(state_out, state_seq.at[i], seq_send.at[i], seq_recv.at[i], "seq", peers[i])
        for i in range(sides - 1)
    ]
    first, second = pl.ds(0, half), pl.ds(half, half)
    weight_copies = [
        remote(w_own, w_here.at[0], w_send.at[0], w_recv.at[0], "mp", across),
        remote(w_own, w_here.at[1], w_send.at[1], w_recv.at[1], "mp", down),
        remote(
            w_here.at[0, first], w_here.at[2, first], w_send.at[2], w_recv.at[2], "mp", down
        ),
        remote(
            w_here.at[1, second], w_here.at[2, second], w_send.at[3], w_recv.at[3], "mp", across
        ),
    ]
    weights_out = pltpu.make_async_copy(w_here, w_others, w_store.at[0])
    barrier = pltpu.get_barrier_semaphore()

    @pl.when(step == 0)
    def _():
        for peer in peers:
            pl.semaphore_signal(barrier, inc=1, device_id={"seq": peer}, device_id_type=MESH)
        for peer in (across, down):
            pl.semaphore_signal(barrier, inc=1, device_id={"mp": peer}, device_id_type=MESH)
        memory[...] = jnp.zeros_like(memory)
        preceding[...] = jnp.zeros_like(preceding)
        params[...] = jnp.zeros_like(params)
        params[MIXER_GAIN : MIXER_GAIN + 1, :] = mixer_gain[...].astype(F32).reshape(1, width)
        params[CHANNEL_GAIN : CHANNEL_GAIN + 1, :] = channel_gain[...].astype(F32).reshape(1, width)
        params[HEAD_GAIN : HEAD_GAIN + 1, :dv] = head_gain[...].astype(F32).reshape(1, dv)
        column = lax.broadcasted_iota(jnp.int32, (1, 128), 1)
        limits = jnp.zeros((1, 128), F32)
        for s in range(sequences):
            limits = jnp.where(column == s, lengths[s].astype(F32), limits)
        params[HEAD_GAIN : HEAD_GAIN + 1, dv : dv + 128] = limits
        params[TAPS : TAPS + CONV, :c3] = filter_weight[...].astype(F32)
        params[BIAS : BIAS + 1, :dk] = decay_bias[...]

    @pl.when(step > 0)
    def _():
        extended[:, 0:8, :] = extended[:, size : size + 8, :]

    def first_norm(rows):
        inverse = lax.rsqrt(jnp.mean(rows * rows, axis=-1, keepdims=True) + EPS_NORM)
        return (rows * inverse * params[MIXER_GAIN : MIXER_GAIN + 1, :]).astype(BF16)

    here = jnp.swapaxes(tokens[...], 0, 1)
    tok[...] = here
    rounded = first_norm(here.reshape(sequences * size, width).astype(F32))
    normed[...] = rounded.reshape(sequences, size, width)

    @pl.when(step == 0)
    def _():
        pl.semaphore_wait(barrier, sides - 1 + 2)
        edge_copy.start()
        for copy in weight_copies[:2]:
            copy.start()

    projected_rows = mm(rounded, w_proj[...]).astype(BF16)
    projected[...] = projected_rows.reshape(sequences, size, c3)
    rows_here = pl.ds(pl.multiple_of(step * size, size), size)
    out_gate[:, rows_here, :] = mm(rounded, w_gate[...]).astype(BF16).reshape(sequences, size, dv)
    low_rows = mm_nt(rounded, w_rank[...]).astype(BF16)
    low_rank[...] = low_rows.reshape(sequences, size, rank)

    logit = mm(low_rows, rank_up[...]) + params[BIAS : BIAS + 1, :dk]
    decay = (jnp.minimum(logit, 0.0) - jnp.log1p(jnp.exp(-jnp.abs(logit)))) / GATE_NORMALIZER
    blocks = [
        decay[s * size + p * CHUNK : s * size + (p + 1) * CHUNK]
        for s in range(sequences)
        for p in range(per_step)
    ]
    totals = running_sums(blocks, True)

    @pl.when(step == 0)
    def _():
        edge_copy.wait()
        edge = jnp.swapaxes(edge_in[...].astype(F32), 0, 1).reshape(sequences * 8, width)
        edge_rows = mm(first_norm(edge), w_proj[...]).astype(BF16).astype(F32)
        edge_rows = jnp.where(side > 0, edge_rows, 0.0).reshape(sequences, 8, c3)
        extended[:, 0:8, :] = edge_rows
        halo[...] = edge_rows

    taps = params[TAPS : TAPS + CONV, :c3]
    convolved = []
    for s in range(sequences):
        rows = projected_rows[s * size : (s + 1) * size]
        extended[s, 8 : 8 + size, :] = rows.astype(F32)
        filtered = filter_rows(extended.at[s], taps, size)
        convolved.append((filtered * sigmoid(filtered)).astype(BF16))
    visible = causal_pairs(sequences)
    for p in range(per_step):
        rows = slice(p * CHUNK, (p + 1) * CHUNK)
        there = pl.ds(pl.multiple_of(step * size + p * CHUNK, CHUNK), CHUNK)
        lifted, lowered, profiles, tails, lasts = [], [], [], [], []
        for s in range(sequences):
            queries = convolved[s][rows, :dk].astype(F32)
            keys = convolved[s][rows, dk : 2 * dk].astype(F32)
            total = totals[s * per_step + p]
            middle, last = total[CHUNK // 2 - 1 : CHUNK // 2], total[CHUNK - 1 : CHUNK]
            lifted.append((queries * jnp.exp(total - middle)).astype(BF16))
            lowered.append((keys * jnp.exp(middle - total)).astype(BF16))
            inside = queries * jnp.exp(total)
            profiles.append(inside.astype(BF16))
            tails.append((keys * jnp.exp(last - total)).astype(BF16))
            lasts.append(last)
            gone = preceding[:, s * dk : (s + 1) * dk]
            profile[s, there, :] = (inside * jnp.exp(gone)).astype(BF16)
            cumulative[s, rows, :] = total
        values = jnp.concatenate([convolved[s][rows, 2 * dk :] for s in range(sequences)], axis=0)
        scores = mm_nt(jnp.concatenate(lifted, axis=0), jnp.concatenate(lowered, axis=0))
        scores = jnp.where(visible, scores, 0.0).astype(BF16)
        entry = memory[...]
        entry_low = entry.astype(BF16)
        states[p] = entry_low
        mixed = mm(scores, values) + mm_nt(spread(profiles), entry_low)
        for s in range(sequences):
            head_local[s, there, :] = mixed[s * CHUNK : (s + 1) * CHUNK]
        last = jnp.concatenate(lasts, axis=1)
        memory[...] = entry * jnp.exp(last) + mm_tn(values, spread(tails))
        before[step * per_step + p] = preceding[...]
        preceding[...] = preceding[...] + last

    @pl.when(step == last_step - 1)
    def _():
        for i in range(2):
            weight_copies[i].wait_recv()
            weight_copies[2 + i].start()

    @pl.when(step == last_step)
    def _():
        state_out[0:dv, :] = memory[...]
        state_out[dv : dv + 8, :] = jnp.broadcast_to(preceding[...], (8, sequences * dk))
        for copy in state_copies:
            copy.start()
        for copy in weight_copies[2:]:
            copy.wait_recv()
        weights_out.start()
        decays[...] = jnp.zeros_like(decays)
        for copy in state_copies:
            copy.wait_recv()
        total = jnp.zeros_like(memory)
        for behind in range(sides - 1, 0, -1):
            source = side - behind
            gone = state_seq[behind - 1, dv : dv + 1, :]
            decays[(source + sides) % sides] = gone
            longer = state_seq[behind - 1, 0:dv, :] + jnp.exp(gone) * total
            total = jnp.where(source >= 0, longer, total)
        entering[...] = total
        entry_low = total.astype(BF16)
        scale = dk ** (-0.5)

        def gate(index, carry):
            there = pl.ds(pl.multiple_of(index * size, size), size)
            for s in range(sequences):
                rows = head_local[s, there, :]
                rows = rows + mm_nt(profile[s, there, :], entry_low[:, s * dk : (s + 1) * dk])
                rows = rows * scale
                head[s, there, :] = rows.astype(BF16)
                inverse = lax.rsqrt(jnp.mean(rows * rows, axis=-1, keepdims=True) + EPS_HEAD)
                logits = out_gate[s, there, :].astype(F32)
                rows = rows * inverse * params[HEAD_GAIN : HEAD_GAIN + 1, :dv]
                gated[s, there, :] = (rows * (logits * sigmoid(logits))).astype(BF16)
            return carry

        lax.fori_loop(0, last_step + 1, gate, 0)
        edge_sends = state_copies + weight_copies
        for copy in edge_sends:
            copy.wait_send()
        weights_out.wait()


def front(
    tokens, mixer_gain, channel_gain, head_gain, filter_weight, decay_bias, lengths, w_proj,
    w_gate, w_rank, rank_up, w_own, seq_count,
):
    length, sequences, width = tokens.shape
    c3, dv = w_proj.shape[1], w_gate.shape[1]
    rank, dk = rank_up.shape
    chunks, per_step = length // CHUNK, STEP // CHUNK
    both = sequences * dk
    anywhere = pl.BlockSpec(memory_space=pl.ANY)
    dma = pltpu.SemaphoreType.DMA
    peers = seq_count - 1

    def steps(columns):
        return pl.BlockSpec((sequences, STEP, columns), lambda i: (0, i, 0))

    return pl.pallas_call(
        front_body,
        grid=(length // STEP,),
        in_specs=[
            pl.BlockSpec((STEP, sequences, width), lambda i: (i, 0, 0)),
            whole(mixer_gain.shape),
            whole(channel_gain.shape),
            whole(head_gain.shape),
            whole(filter_weight.shape),
            whole(decay_bias.shape),
            pl.BlockSpec(memory_space=pltpu.SMEM),
            whole(w_proj.shape),
            whole(w_gate.shape),
            whole(w_rank.shape),
            whole(rank_up.shape),
            anywhere,
            anywhere,
        ],
        out_specs=[
            whole((8, width)),
            steps(width),
            steps(width),
            steps(c3),
            steps(rank),
            steps(dk),
            pl.BlockSpec((per_step, dv, both), lambda i: (i, 0, 0)),
            whole((chunks, 1, both)),
            whole((sequences, length, dv)),
            whole((sequences, length, dk)),
            whole((sequences, length, dv)),
            whole((sequences, length, dv)),
            whole((sequences, 8, c3)),
            whole((dv, both)),
            whole((seq_count, 1, both)),
            anywhere,
        ],
        out_shape=[
            shape_of((8, width), F32),
            shape_of((sequences, length, width), BF16),
            shape_of((sequences, length, width), BF16),
            shape_of((sequences, length, c3), BF16),
            shape_of((sequences, length, rank), BF16),
            shape_of((sequences, length, dk), F32),
            shape_of((chunks, dv, both), BF16),
            shape_of((chunks, 1, both), F32),
            shape_of((sequences, length, dv), BF16),
            shape_of((sequences, length, dk), BF16),
            shape_of((sequences, length, dv), BF16),
            shape_of((sequences, length, dv), BF16),
            shape_of((sequences, 8, c3), F32),
            shape_of((dv, both), F32),
            shape_of((seq_count, 1, both), F32),
            shape_of((3, *w_own.shape), BF16),
        ],
        scratch_shapes=[
            pltpu.VMEM((sequences, STEP + 8, c3), F32),
            pltpu.VMEM((dv, both), F32),
            pltpu.VMEM((1, both), F32),
            pltpu.VMEM((sequences, length, dv), F32),
            pltpu.VMEM((8, sequences, width), BF16),
            pltpu.VMEM((dv + 8, both), F32),
            pltpu.VMEM((peers, dv + 8, both), F32),
            pltpu.VMEM((3, *w_own.shape), BF16),
            dma((2,)),
            dma((peers,)),
            dma((peers,)),
            dma((4,)),
            dma((4,)),
            dma((1,)),
        ],
        compiler_params=pltpu.CompilerParams(
            dimension_semantics=("arbitrary",),
            collective_id=2,
            has_side_effects=True,
            vmem_limit_bytes=VMEM_LIMIT,
        ),
        cost_estimate=pl.CostEstimate(
            flops=2 * sequences * length * width * (c3 + dv + 128),
            bytes_accessed=sequences * length * width * 8,
            transcendentals=0,
        ),
        name="front",
    )(
        tokens, mixer_gain, channel_gain, head_gain, filter_weight, decay_bias, lengths, w_proj,
        w_gate, w_rank, rank_up, tokens, w_own,
    )


PIECE = 128
HALF = PIECE // 2


def ffn_body(
    gated, w_own, w_others, tok, params, w_gate, w_up, w_down, cotangent,
    out_part, weight_grads, output_grads, grad_gated, own_residual, own_grad, gain_grad,
    g_across, g_down, g_far, tok_here, cot_here, up_here, wg, wu, wd, normed, hidden, grad_gate,
    grad_up,
    out_stage, part, via_across, via_down, from_across, from_down, residual_here, grad_here,
    mixer_here, pieces, received, weight_stage, output_stage,
    load_sem, row_sem, cot_sem, ag_send, ag_recv, rs_send, rs_recv, back_send, back_recv,
    store_sem, stage_sem, last_sem,
):
    turns = up_here.shape[0]
    halves = 2
    width = tok_here.shape[-1]
    me = lax.axis_index("mp")
    across = me + 1 - 2 * (me % 2)
    down = (me + 2) % 4
    far = 3 - me
    MESH = pl.DeviceIdType.MESH

    def remote(source, target, send, recv, device):
        return pltpu.make_async_remote_copy(
            src_ref=source,
            dst_ref=target,
            send_sem=send,
            recv_sem=recv,
            device_id={"mp": device},
            device_id_type=MESH,
        )

    def load(index, source, target):
        return pltpu.make_async_copy(source, target, load_sem.at[index])

    def load_tok(turn):
        return pltpu.make_async_copy(
            tok.at[turn // halves, :, turn % halves], tok_here.at[turn % 2], row_sem.at[turn]
        )

    def load_cot(block):
        start = pl.multiple_of(block * PIECE, PIECE)
        return pltpu.make_async_copy(
            cotangent.at[pl.ds(start, PIECE)], cot_here.at[block % 2], cot_sem.at[block % 2]
        )

    def direct(turn, side):
        return remote(
            gated.at[turn // halves, :, turn % halves],
            (g_across, g_down)[side].at[turn],
            ag_send.at[side, turn],
            ag_recv.at[side, turn],
            (across, down)[side],
        )

    def relay(turn, side):
        cut = pl.ds(2 * side, 2)
        return remote(
            (g_across, g_down)[side].at[turn, cut],
            g_far.at[turn, cut],
            ag_send.at[2 + side, turn],
            ag_recv.at[2 + side, turn],
            (down, across)[side],
        )

    first, second = pl.ds(0, HALF), pl.ds(HALF, HALF)

    def scatter(turn, index):
        source, target, device = (
            (part.at[turn, far, first], via_across.at[turn], across),
            (part.at[turn, far, second], via_down.at[turn], down),
            (part.at[turn, across, first], from_across.at[turn, first], across),
            (part.at[turn, down, second], from_down.at[turn, second], down),
            (part.at[turn, across, second], from_across.at[turn, second], across),
            (part.at[turn, down, first], from_down.at[turn, first], down),
        )[index]
        return remote(source, target, rs_send.at[index, turn], rs_recv.at[index, turn], device)

    def give_back(turn, slot):
        return remote(
            pieces.at[turn, slot],
            received.at[turn, slot],
            back_send.at[slot, turn],
            back_recv.at[slot, turn],
            (me, across, down, far)[slot],
        )

    def store_out(turn):
        return pltpu.make_async_copy(
            out_stage.at[turn % 2],
            out_part.at[turn // halves, :, turn % halves],
            store_sem.at[turn],
        )

    barrier = pltpu.get_barrier_semaphore()
    loads = [load(0, w_gate, wg), load(1, w_up, wu), load(2, w_down, wd)]
    for copy in loads:
        copy.start()
    blocks = cotangent.shape[0] // PIECE
    for turn in range(2):
        load_tok(turn).start()
        load_cot(turn).start()
    for device in (across, down, far):
        pl.semaphore_signal(barrier, inc=1, device_id={"mp": device}, device_id_type=MESH)
    pl.semaphore_wait(barrier, 3)
    for side in range(2):
        direct(0, side).start()
    gain_grad[...] = jnp.zeros_like(gain_grad)
    gain = params[CHANNEL_GAIN : CHANNEL_GAIN + 1, :]
    length = cotangent.shape[0]
    first_position = lax.axis_index("seq") * length

    def take_cotangent(block, carry):
        load_cot(block).wait()
        rows = jnp.swapaxes(cot_here[block % 2], 0, 1)
        position = first_position + block * PIECE
        position = (position + lax.broadcasted_iota(jnp.int32, (PIECE, 1), 0)).astype(F32)
        for s in range(turns // halves):
            column = gated.shape[-1] + s
            keep = position < params[HEAD_GAIN : HEAD_GAIN + 1, column : column + 1]
            kept = jnp.where(keep, rows[s].astype(F32), 0.0).astype(BF16)
            up_here[s * halves + block % halves, block // halves] = kept

        @pl.when(block + 2 < blocks)
        def _():
            load_cot(block + 2).start()

        return carry

    lax.fori_loop(0, blocks // 2, take_cotangent, 0)
    for side in range(2):
        direct(0, side).wait_recv()
        relay(0, side).start()
    for side in range(2):
        direct(1, side).start()
    lax.fori_loop(blocks // 2, blocks, take_cotangent, 0)
    for copy in loads:
        copy.wait()

    def forward_and_back(turn):
        load_tok(turn).wait()
        for side in range(2):
            relay(turn, side).wait_recv()
        rows = 4 * PIECE

        def flat(values):
            return values.reshape(rows, values.shape[-1])

        mixed = mm(flat(gated[turn // halves, :, turn % halves]), w_own[...])
        for slot, source in enumerate((g_across, g_down, g_far)):
            mixed = mixed + mm(flat(source[turn]), w_others[slot])
        residual = flat(tok_here[turn % 2]).astype(F32) + mixed
        for quarter in range(4):

            @pl.when(me == quarter)
            def _():
                residual_here[turn] = residual[quarter * PIECE : (quarter + 1) * PIECE]

        inverse = lax.rsqrt(jnp.mean(residual * residual, axis=-1, keepdims=True) + EPS_NORM)
        unit = residual * inverse
        rounded = (unit * gain).astype(BF16)
        normed[turn] = rounded
        gate_rows = mm_nt(rounded, wg[...])
        up_rows = mm_nt(rounded, wu[...])
        share = sigmoid(gate_rows)
        swished = gate_rows * share
        hidden_rows = (swished * up_rows).astype(BF16)
        hidden[turn] = hidden_rows
        grad_hidden = mm_nt(flat(up_here[turn]), wd[...])
        for side in range(2):

            @pl.when(turn + 1 < turns)
            def _():
                direct(turn + 1, side).wait_recv()
                relay(turn + 1, side).start()

        for side in range(2):

            @pl.when(turn + 2 < turns)
            def _():
                direct(turn + 2, side).start()

        slope = share * (1.0 + gate_rows * (1.0 - share))
        grad_gate_rows = (grad_hidden * up_rows * slope).astype(BF16)
        grad_up_rows = (grad_hidden * swished).astype(BF16)
        grad_gate[turn] = grad_gate_rows
        grad_up[turn] = grad_up_rows
        grad_rows = mm(grad_gate_rows, wg[...]) + mm(grad_up_rows, wu[...])
        part[turn] = grad_rows.astype(BF16).reshape(4, PIECE, width)
        for index in range(4):
            scatter(turn, index).start()
        gain_grad[...] += jnp.sum(grad_rows * unit, axis=0, keepdims=True)

        @pl.when(turn >= 2)
        def _():
            store_out(turn - 2).wait()

        out_stage[turn % 2] = mm(hidden_rows, wd[...]).astype(BF16).reshape(4, PIECE, width)
        store_out(turn).start()

        @pl.when(turn + 2 < turns)
        def _():
            load_tok(turn + 2).start()

    def pass_on(turn):
        scatter(turn, 0).wait_recv()
        part[turn, down, 0:HALF] = part[turn, down, 0:HALF] + via_across[turn]
        scatter(turn, 5).start()
        scatter(turn, 1).wait_recv()
        part[turn, across, HALF:PIECE] = part[turn, across, HALF:PIECE] + via_down[turn]
        scatter(turn, 4).start()

    def collect(turn):
        for index in range(2, 6):
            scatter(turn, index).wait_recv()
        grad_normed = part[turn, me].astype(F32) + from_across[turn].astype(F32)
        grad_normed = grad_normed + from_down[turn].astype(F32)
        residual = residual_here[turn]
        inverse = lax.rsqrt(jnp.mean(residual * residual, axis=-1, keepdims=True) + EPS_NORM)
        unit = residual * inverse
        scaled = grad_normed * gain
        through = inverse * (scaled - unit * jnp.mean(scaled * unit, axis=-1, keepdims=True))
        grad_residual = up_here[turn, me].astype(F32) + through
        grad_here[turn] = grad_residual
        grad_mixer = grad_residual.astype(BF16)
        mixer_here[turn] = grad_mixer
        for slot in range(4):
            weight = w_own[...] if slot == 0 else w_others[slot - 1]
            piece = mm_nt(grad_mixer, weight).astype(BF16)
            if slot == 0:
                received[turn, 0] = piece
            else:
                pieces[turn, slot] = piece
                give_back(turn, slot).start()

    tile = weight_stage.shape[2]
    tiles = width // tile

    def store_weight(kind, index, slot):
        return pltpu.make_async_copy(
            weight_stage.at[slot, kind],
            weight_grads.at[kind, pl.ds(index * tile, tile)],
            stage_sem.at[slot, kind],
        )

    all_rows = turns * 4 * PIECE

    def weight_tile(index, carry):
        slot = index % 2
        columns = pl.ds(pl.multiple_of(index * tile, tile), tile)

        @pl.when(index >= 2)
        def _():
            for kind in range(3):
                store_weight(kind, index - 2, slot).wait()

        left = normed[:, :, columns].reshape(all_rows, tile)
        upper = up_here[:, :, :, columns].reshape(all_rows, tile)
        units = hidden.shape[-1]
        for kind, (one, other) in enumerate(
            ((left, grad_gate), (left, grad_up), (upper, hidden))
        ):
            weight_stage[slot, kind] = mm_tn(one, other[...].reshape(all_rows, units)).astype(BF16)
            store_weight(kind, index, slot).start()
        return carry

    def round_of(index, carry):
        @pl.when(index < turns)
        def _():
            forward_and_back(index)

        @pl.when(index >= turns)
        def _():
            first_tile = (index - turns) * (tiles // 2)
            lax.fori_loop(first_tile, first_tile + tiles // 2, weight_tile, 0)

        @pl.when(jnp.logical_and(index >= 1, index <= turns))
        def _():
            pass_on(index - 1)

        @pl.when(index >= 2)
        def _():
            collect(index - 2)

        return carry

    lax.fori_loop(0, turns + 2, round_of, 0)
    mixer_rows = mixer_here[...].reshape(turns * PIECE, width)
    dv = gated.shape[-1]
    for slot in range(4):
        if slot == 0:
            blocks = [gated[t // halves, me, t % halves] for t in range(turns)]
        else:
            source = (None, g_across, g_down, g_far)[slot]
            blocks = [source[t, me] for t in range(turns)]
        rows = jnp.concatenate(blocks, axis=0)
        output_stage[slot] = mm_tn(mixer_rows, rows).astype(BF16)

    last = [
        pltpu.make_async_copy(residual_here, own_residual, last_sem.at[0]),
        pltpu.make_async_copy(grad_here, own_grad, last_sem.at[1]),
        pltpu.make_async_copy(output_stage, output_grads, last_sem.at[2]),
    ]
    for copy in last:
        copy.start()
    for turn in range(turns):
        for slot in range(1, 4):
            give_back(turn, slot).wait_recv()
        for slot in range(4):
            source = (me, across, down, far)[slot]
            pltpu.make_async_copy(
                received.at[turn, slot],
                grad_gated.at[turn // halves, source, turn % halves],
                last_sem.at[3 + turn * 4 + slot],
            ).start()
    for turn in range(turns):
        for slot in range(4):
            source = (me, across, down, far)[slot]
            pltpu.make_async_copy(
                received.at[turn, slot],
                grad_gated.at[turn // halves, source, turn % halves],
                last_sem.at[3 + turn * 4 + slot],
            ).wait()
        if turn >= turns - 2:
            store_out(turn).wait()
        for side in range(2):
            direct(turn, side).wait_send()
            relay(turn, side).wait_send()
        for index in range(6):
            scatter(turn, index).wait_send()
        for slot in range(1, 4):
            give_back(turn, slot).wait_send()
    for index in range(max(tiles - 2, 0), tiles):
        for kind in range(3):
            store_weight(kind, index, index % 2).wait()
    for copy in last:
        copy.wait()


def feed_forward(gated, w_own, w_others, tok, params, w_gate, w_up, w_down, cotangent):
    sequences, length, width = tok.shape
    dv, units = gated.shape[-1], w_gate.shape[0]
    halves = length // 4 // PIECE
    turns = sequences * halves

    def pieces_of(values):
        return values.reshape(sequences, 4, halves, PIECE, values.shape[-1])

    anywhere = pl.BlockSpec(memory_space=pl.ANY)
    vmem = pl.BlockSpec(memory_space=pltpu.VMEM)
    dma = pltpu.SemaphoreType.DMA
    rows = 4 * PIECE
    outs = pl.pallas_call(
        ffn_body,
        in_specs=[vmem] * 3 + [anywhere, vmem] + [anywhere] * 4,
        out_specs=[anywhere] * 6 + [vmem],
        out_shape=[
            shape_of((sequences, 4, halves, PIECE, width), BF16),
            shape_of((3, width, units), BF16),
            shape_of((4, width, dv), BF16),
            shape_of((sequences, 4, halves, PIECE, dv), BF16),
            shape_of((turns, PIECE, width), F32),
            shape_of((turns, PIECE, width), F32),
            shape_of((1, width), F32),
        ],
        scratch_shapes=[
            pltpu.VMEM((turns, 4, PIECE, dv), BF16),
            pltpu.VMEM((turns, 4, PIECE, dv), BF16),
            pltpu.VMEM((turns, 4, PIECE, dv), BF16),
            pltpu.VMEM((2, 4, PIECE, width), BF16),
            pltpu.VMEM((2, PIECE, sequences, width), BF16),
            pltpu.VMEM((turns, 4, PIECE, width), BF16),
            pltpu.VMEM((units, width), BF16),
            pltpu.VMEM((units, width), BF16),
            pltpu.VMEM((units, width), BF16),
            pltpu.VMEM((turns, rows, width), BF16),
            pltpu.VMEM((turns, rows, units), BF16),
            pltpu.VMEM((turns, rows, units), BF16),
            pltpu.VMEM((turns, rows, units), BF16),
            pltpu.VMEM((2, 4, PIECE, width), BF16),
            pltpu.VMEM((turns, 4, PIECE, width), BF16),
            pltpu.VMEM((turns, HALF, width), BF16),
            pltpu.VMEM((turns, HALF, width), BF16),
            pltpu.VMEM((turns, PIECE, width), BF16),
            pltpu.VMEM((turns, PIECE, width), BF16),
            pltpu.VMEM((turns, PIECE, width), F32),
            pltpu.VMEM((turns, PIECE, width), F32),
            pltpu.VMEM((turns, PIECE, width), BF16),
            pltpu.VMEM((turns, 4, PIECE, dv), BF16),
            pltpu.VMEM((turns, 4, PIECE, dv), BF16),
            pltpu.VMEM((2, 3, 256, units), BF16),
            pltpu.VMEM((4, width, dv), BF16),
            dma((3,)),
            dma((turns,)),
            dma((2,)),
            dma((4, turns)),
            dma((4, turns)),
            dma((6, turns)),
            dma((6, turns)),
            dma((4, turns)),
            dma((4, turns)),
            dma((turns,)),
            dma((2, 3)),
            dma((3 + 4 * turns,)),
        ],
        compiler_params=pltpu.CompilerParams(
            collective_id=0, has_side_effects=True, vmem_limit_bytes=64 * 2**20
        ),
        cost_estimate=pl.CostEstimate(
            flops=2 * sequences * length * width * (4 * dv + 9 * units),
            bytes_accessed=sequences * length * width * 8,
            transcendentals=0,
        ),
        name="feed_forward",
    )(
        pieces_of(gated), w_own, w_others, pieces_of(tok), params, w_gate, w_up, w_down, cotangent
    )
    out_part, weight_grads, output_grads, grad_gated, own_residual, own_grad, gain_grad = outs
    return (
        out_part.reshape(sequences, 4, length // 4, width),
        weight_grads,
        output_grads,
        grad_gated.reshape(sequences, length, dv),
        own_residual,
        own_grad,
        gain_grad,
    )


SMALL, PACKED = 48, 32


def paired_sum(own, received, order):
    terms = [own.astype(F32)] + [received[index].astype(F32) for index in order]
    while len(terms) > 1:
        half = len(terms) // 2
        terms = [terms[index] + terms[index + half] for index in range(half)]
    return terms[0]


def mixer_back_body(
    grad_gated_in, head_in, profile_in, out_gate_in, projected_in, cumulative_in, states_in,
    normed_in, tok_in, residual_in, grad_residual_in, out_part_in, hidden_grads, output_parts,
    w_proj_in, w_gate_in, low_rank, halo, params, rank_up, w_rank, before, entering,
    decays, channel_part,
    output, token_grads, hidden_out, mixer_out, small_out, shared_out,
    grad_gated, head, profile, out_gate, projected, cumulative, states, normed, tok, residual,
    grad_residual, part_f, part_g, w_proj, w_gate,
    hidden_kept, hidden_seq, hidden_dp, output_kept, output_seq, output_mp, output_dp,
    f_via_across, f_via_down, f_across, f_down, g_via_across, g_via_down, g_across, g_down,
    grad_out_gate, grad_head, grad_projected, grad_low_rank, mixer_grad, mixer_seq, mixer_dp,
    state_grad, state_seq, upstream, extended, grad_extended, edge_out, edge_in,
    small, packed, small_low, small_seq, small_dp, small_mp, out_stage,
    load_sem, seq_send, seq_recv, dp_send, dp_recv, mp_send, mp_recv, f_send, f_recv,
    g_send, g_recv, store_sem,
):
    sequences, length, dv = grad_gated.shape
    width = normed.shape[-1]
    rank, dk = rank_up.shape
    c3 = projected.shape[-1]
    halves = 2
    turns = sequences * halves
    MESH = pl.DeviceIdType.MESH
    me, side, place = lax.axis_index("mp"), lax.axis_index("seq"), lax.axis_index("dp")
    sides, places = lax.axis_size("seq"), lax.axis_size("dp")
    across = me + 1 - 2 * (me % 2)
    down = (me + 2) % 4
    far = 3 - me
    share_rows = width // sides
    shard_rows = share_rows // places
    steps = length // STEP
    per_step = STEP // CHUNK
    first, second = pl.ds(0, HALF), pl.ds(HALF, HALF)

    def remote(source, target, send, recv, axis, device):
        return pltpu.make_async_remote_copy(
            src_ref=source,
            dst_ref=target,
            send_sem=send,
            recv_sem=recv,
            device_id={axis: device},
            device_id_type=MESH,
        )


    loads = [
        pltpu.make_async_copy(source, target, load_sem.at[index])
        for index, (source, target) in enumerate(
            [
                (grad_gated_in, grad_gated),
                (head_in, head),
                (profile_in, profile),
                (out_gate_in, out_gate),
                (out_part_in, part_f),
                (hidden_grads.at[:, pl.ds(side * share_rows, share_rows)], hidden_kept),
                (output_parts.at[:, pl.ds(side * share_rows, share_rows)], output_kept),
                (normed_in, normed),
                (projected_in, projected),
                (cumulative_in, cumulative),
                (states_in, states),
                (residual_in, residual),
                (w_proj_in, w_proj),
                (w_gate_in, w_gate),
                (grad_residual_in, grad_residual),
                (tok_in.at[:, me], tok),
            ]
        )
    ]

    def to_sides(kind, source_of, target):
        copies = []
        for hop in range(1, sides):
            peer = (side + hop) % sides
            copies.append(
                remote(
                    source_of(peer),
                    target.at[hop - 1],
                    seq_send.at[kind, hop - 1],
                    seq_recv.at[kind, hop - 1],
                    "seq",
                    peer,
                )
            )
        return copies

    def to_places(kind, source_of, target):
        copies = []
        for hop in range(1, places):
            peer = (place + hop) % places
            copies.append(
                remote(
                    source_of(peer),
                    target.at[hop - 1],
                    dp_send.at[kind, hop - 1],
                    dp_recv.at[kind, hop - 1],
                    "dp",
                    peer,
                )
            )
        return copies

    def to_heads(kind, source_of, target):
        return [
            remote(
                source_of(slot),
                target.at[slot - 1],
                mp_send.at[kind, slot - 1],
                mp_recv.at[kind, slot - 1],
                "mp",
                (me, across, down, far)[slot],
            )
            for slot in range(1, 4)
        ]

    def share_of(ref):
        return lambda peer: ref.at[:, pl.ds(peer * share_rows, share_rows)]

    def shard_of(ref):
        return lambda peer: ref.at[:, pl.ds(peer * shard_rows, shard_rows)]

    hidden_to_sides = to_sides(0, share_of(hidden_grads), hidden_seq)
    output_to_sides = to_sides(1, share_of(output_parts), output_seq)
    state_to_sides = to_sides(2, lambda peer: state_grad, state_seq)
    mixer_to_sides = to_sides(
        3, lambda peer: mixer_grad.at[pl.ds(peer * share_rows, share_rows)], mixer_seq
    )
    small_to_sides = to_sides(4, lambda peer: small_low.at[0], small_seq)
    edge_copy = remote(
        edge_out,
        edge_in,
        seq_send.at[5, 0],
        seq_recv.at[5, 0],
        "seq",
        (side + sides - 1) % sides,
    )
    hidden_to_places = to_places(0, shard_of(hidden_kept), hidden_dp)

    def own_share(peer):
        return pl.ds(pl.multiple_of(side * share_rows + peer * shard_rows, 16), shard_rows)

    mixer_to_places = to_places(1, lambda peer: mixer_grad.at[own_share(peer)], mixer_dp)
    output_to_places = to_places(
        2, lambda peer: output_kept.at[0, pl.ds(peer * shard_rows, shard_rows)], output_dp
    )
    small_to_places = to_places(3, lambda peer: small_low.at[1], small_dp)
    output_to_heads = to_heads(0, lambda slot: output_kept.at[slot], output_mp)
    small_to_heads = to_heads(1, lambda slot: small_low.at[2], small_mp)

    def scatter(turn, index, forward):
        part = part_f if forward else part_g
        if forward:
            via_across, via_down, from_across, from_down = (
                f_via_across, f_via_down, f_across, f_down,
            )
            send, recv = f_send, f_recv
        else:
            via_across, via_down, from_across, from_down = (
                g_via_across, g_via_down, g_across, g_down,
            )
            send, recv = g_send, g_recv
        s, h = turn // halves, turn % halves
        low, high = pl.ds(h * PIECE, HALF), pl.ds(h * PIECE + HALF, HALF)
        source, target, device = (
            (part.at[s, far, low], via_across.at[turn], across),
            (part.at[s, far, high], via_down.at[turn], down),
            (part.at[s, across, low], from_across.at[turn, first], across),
            (part.at[s, down, high], from_down.at[turn, second], down),
            (part.at[s, across, high], from_across.at[turn, second], across),
            (part.at[s, down, low], from_down.at[turn, first], down),
        )[index]
        return remote(source, target, send.at[index, turn], recv.at[index, turn], "mp", device)

    def pass_on(turn, forward):
        part = part_f if forward else part_g
        via_across, via_down = (
            (f_via_across, f_via_down) if forward else (g_via_across, g_via_down)
        )
        s, h = turn // halves, turn % halves
        low = pl.ds(h * PIECE, HALF)
        high = pl.ds(h * PIECE + HALF, HALF)
        scatter(turn, 0, forward).wait_recv()
        part[s, down, low] = part[s, down, low] + via_across[turn]
        scatter(turn, 5, forward).start()
        scatter(turn, 1, forward).wait_recv()
        part[s, across, high] = part[s, across, high] + via_down[turn]
        scatter(turn, 4, forward).start()

    def summed(turn, forward):
        part = part_f if forward else part_g
        from_across, from_down = (f_across, f_down) if forward else (g_across, g_down)
        for index in range(2, 6):
            scatter(turn, index, forward).wait_recv()
        s, h = turn // halves, turn % halves
        total = part[s, me, h * PIECE : (h + 1) * PIECE].astype(F32)
        return total + from_across[turn].astype(F32) + from_down[turn].astype(F32)

    def store(turn, kind):
        source, target = ((out_stage, output), (grad_residual, token_grads))[kind]
        return pltpu.make_async_copy(source.at[turn], target.at[turn], store_sem.at[kind, turn])


    barrier = pltpu.get_barrier_semaphore()
    for copy in loads:
        copy.start()
    for axis, peers in (
        ("seq", [(side + hop) % sides for hop in range(1, sides)]),
        ("mp", [across, down, far]),
        ("dp", [(place + hop) % places for hop in range(1, places)]),
    ):
        for peer in peers:
            pl.semaphore_signal(barrier, inc=1, device_id={axis: peer}, device_id_type=MESH)
    small[...] = jnp.zeros_like(small)
    state_grad[...] = jnp.zeros_like(state_grad)
    small[33:34, :] = channel_part[...]
    pl.semaphore_wait(barrier, sides - 1 + 3 + places - 1)
    for copy in hidden_to_sides + output_to_sides:
        copy.start()
    loads[4].wait()
    for turn in range(turns):
        for index in range(2):
            scatter(turn, index, True).start()
    loads[5].wait()
    for copy in hidden_to_sides:
        copy.wait_recv()
    hidden_sum = hidden_kept[...]
    for hop in range(sides - 1):
        hidden_sum = hidden_sum + hidden_seq[hop]
    hidden_kept[...] = hidden_sum
    for copy in hidden_to_places:
        copy.start()
    for copy in loads[0:4]:
        copy.wait()


    scale = dk ** (-0.5)
    head_gain = params[HEAD_GAIN : HEAD_GAIN + 1, :dv]
    mixer_gain = params[MIXER_GAIN : MIXER_GAIN + 1, :]

    def ungate(index, carry):
        rows = pl.ds(pl.multiple_of(index * STEP, STEP), STEP)
        for s in range(sequences):
            upper = grad_gated[s, rows, :].astype(F32)
            head_rows_here = head[s, rows, :].astype(F32)
            inverse = lax.rsqrt(
                jnp.mean(head_rows_here * head_rows_here, axis=-1, keepdims=True) + EPS_HEAD
            )
            unit = head_rows_here * inverse
            logits = out_gate[s, rows, :].astype(F32)
            share = sigmoid(logits)
            slope = share * (1.0 + logits * (1.0 - share))
            grad_out_gate[s, rows, :] = (upper * unit * head_gain * slope).astype(BF16)
            grad_normed = upper * (logits * share)
            small[34:35, :dv] += jnp.sum(grad_normed * unit, axis=0, keepdims=True)
            scaled = grad_normed * head_gain
            through = inverse * (scaled - unit * jnp.mean(scaled * unit, axis=-1, keepdims=True))
            rounded = (through * scale).astype(BF16)
            grad_head[s, rows, :] = rounded
            state_grad[:, s * dk : (s + 1) * dk] += mm_tn(rounded, profile[s, rows, :])
        return carry

    lax.fori_loop(0, steps, ungate, 0)
    for copy in state_to_sides:
        copy.start()
    for turn in range(turns):
        for index in range(2, 4):
            scatter(turn, index, True).start()
    loads[6].wait()
    for copy in output_to_sides:
        copy.wait_recv()
    output_sum = output_kept[...]
    for hop in range(sides - 1):
        output_sum = output_sum + output_seq[hop]
    output_kept[...] = output_sum
    for copy in output_to_heads:
        copy.start()
    for copy in loads[7:11]:
        copy.wait()
    for copy in state_to_sides:
        copy.wait_recv()
    total = jnp.zeros_like(upstream)
    for ahead in range(sides - 1, 0, -1):
        source = side + ahead
        decay = decays[source % sides]
        longer = state_seq[sides - ahead - 1] + jnp.exp(decay) * total
        total = jnp.where(source < sides, longer, total)
    upstream[...] = total
    grad_extended[:, STEP : STEP + 8, :] = jnp.zeros_like(grad_extended[:, STEP : STEP + 8, :])


    taps = params[TAPS : TAPS + CONV, :c3]
    causal = triangle(True)

    def backward_step(back, carry):
        step = steps - 1 - back
        start = pl.multiple_of(step * STEP, STEP)

        @pl.when(back > 0)
        def _():
            grad_extended[:, STEP : STEP + 8, :] = grad_extended[:, 0:8, :]

        @pl.when(step == 0)
        def _():
            extended[:, 0:8, :] = halo[...]

        @pl.when(step > 0)
        def _():
            earlier = projected[:, pl.ds(pl.multiple_of(jnp.maximum(start - 16, 0), 16), 16), :]
            extended[:, 0:8, :] = earlier.astype(F32)[:, 8:16, :]

        for s in range(sequences):
            here = pl.ds(start, STEP)
            extended[s, 8 : 8 + STEP, :] = projected[s, here, :].astype(F32)
            filtered = filter_rows(extended.at[s], taps, STEP)
            share = sigmoid(filtered)
            convolved = (filtered * share).astype(BF16)
            slope = share * (1.0 + filtered * (1.0 - share))
            low_rows = low_rank[s, here, :]
            logit = mm(low_rows, rank_up[...]) + params[BIAS : BIAS + 1, :dk]
            logit_grads = [None] * per_step
            for piece in reversed(range(per_step)):
                rows = slice(piece * CHUNK, (piece + 1) * CHUNK)
                there = pl.ds(start + piece * CHUNK, CHUNK)
                queries = convolved[rows, :dk].astype(F32)
                keys = convolved[rows, dk : 2 * dk].astype(F32)
                values = convolved[rows, 2 * dk :]
                grad_rows = grad_head[s, there, :]
                total = cumulative[s, there, :]
                middle, last = total[CHUNK // 2 - 1 : CHUNK // 2], total[CHUNK - 1 : CHUNK]
                lift, lower = jnp.exp(total - middle), jnp.exp(middle - total)
                inner, outer = jnp.exp(total), jnp.exp(last - total)
                whole_decay = jnp.exp(last)
                lifted, lowered = (queries * lift).astype(BF16), (keys * lower).astype(BF16)
                inside, tails = (queries * inner).astype(BF16), (keys * outer).astype(BF16)
                own = slice(s * dk, (s + 1) * dk)
                previous = before[step * per_step + piece, :, own]
                state = states[step * per_step + piece, :, own].astype(F32)
                state = state + entering[:, own] * jnp.exp(previous)
                scores = jnp.where(causal, mm_nt(lifted, lowered), 0.0).astype(BF16)
                grad_scores = jnp.where(causal, mm_nt(grad_rows, values), 0.0).astype(BF16)
                later = upstream[:, own]
                later_low = later.astype(BF16)
                grad_values = mm_tn(scores, grad_rows) + mm_nt(tails, later_low)
                grad_lifted = mm(grad_scores, lowered)
                grad_lowered = mm_tn(grad_scores, lifted)
                grad_inside = mm(grad_rows, state.astype(BF16))
                grad_tails = mm(values, later_low)
                upstream[:, own] = later * whole_decay + mm_tn(grad_rows, inside)
                tail_terms = tails.astype(F32) * grad_tails
                grad_total = (
                    lifted.astype(F32) * grad_lifted
                    - lowered.astype(F32) * grad_lowered
                    + inside.astype(F32) * grad_inside
                    - tail_terms
                )
                grad_last = jnp.sum(tail_terms, axis=0, keepdims=True) + whole_decay * jnp.sum(
                    later * state, axis=0, keepdims=True
                )
                grad_decay = running_sums([grad_total], False)[0] + grad_last
                logit_grads[piece] = grad_decay / GATE_NORMALIZER * sigmoid(-logit[rows])
                grad_extended[s, rows, :dk] = (
                    grad_lifted * lift + grad_inside * inner
                ) * slope[rows, :dk]
                grad_extended[s, rows, dk : 2 * dk] = (
                    grad_lowered * lower + grad_tails * outer
                ) * slope[rows, dk : 2 * dk]
                grad_extended[s, rows, 2 * dk :] = grad_values * slope[rows, 2 * dk :]
            logit_grad = jnp.concatenate(logit_grads, axis=0)
            logit_low = logit_grad.astype(BF16)
            small[35:36, :dk] += jnp.sum(logit_grad, axis=0, keepdims=True)
            small[16 : 16 + rank, :dk] += mm_tn(low_rows, logit_low)
            grad_low_rank[s, here, :] = mm_nt(logit_low, rank_up[...]).astype(BF16)
            total_rows = taps[EDGE : EDGE + 1, :] * grad_extended[s, 0:STEP, :]
            for offset in range(EDGE):
                total_rows = total_rows + taps[offset : offset + 1, :] * grad_extended[
                    s, pl.ds(EDGE - offset, STEP), :
                ]
            grad_projected[s, here, :] = total_rows.astype(BF16)
            grad_filtered = grad_extended[s, 0:STEP, :]
            for offset in range(CONV):
                small[16 + offset : 17 + offset, dk : dk + c3] += jnp.sum(
                    grad_filtered * extended[s, pl.ds(8 - EDGE + offset, STEP), :],
                    axis=0,
                    keepdims=True,
                )
        for turn in range(turns):

            @pl.when(back == turn % steps)
            def _():
                pass_on(turn, True)

        return carry

    lax.fori_loop(0, steps, backward_step, 0)


    edge_out[...] = jnp.zeros_like(edge_out)
    for s in range(sequences):
        rows = grad_extended[s, 0:8, :]
        for i in range(EDGE):
            edge_row = taps[0:1] * rows[i : i + 1]
            for j in range(1, i + 1):
                edge_row = edge_row + taps[j : j + 1] * rows[i - j : i - j + 1]
            edge_out[s, 16 - EDGE + i : 17 - EDGE + i, :] = edge_row
    edge_copy.start()

    edge_copy.wait_recv()
    for s in range(sequences):
        tail = grad_projected[s, length - 16 :, :].astype(F32)
        tail = tail + jnp.where(side < sides - 1, edge_in[s], 0.0)
        grad_projected[s, length - 16 :, :] = tail.astype(BF16)


    flat = sequences * length
    tile = 256

    def weight_tile(index, carry):
        columns = pl.ds(pl.multiple_of(index * tile, tile), tile)
        left = normed[:, :, columns].reshape(flat, tile)
        mixer_grad[columns, :c3] = mm_tn(left, grad_projected[...].reshape(flat, c3)).astype(BF16)
        mixer_grad[columns, c3:] = mm_tn(left, grad_out_gate[...].reshape(flat, dv)).astype(BF16)
        small[0:rank, columns] = mm_tn(grad_low_rank[...].reshape(flat, rank), left)
        return carry

    lax.fori_loop(0, width // tile, weight_tile, 0)
    for copy in mixer_to_sides:
        copy.start()


    loads[12].wait()
    loads[13].wait()

    def input_grad(turn):
        s, h = turn // halves, turn % halves
        quarter = length // 4

        def rows_of_turn(ref):
            blocks = [
                ref[s, q * quarter + h * PIECE : q * quarter + (h + 1) * PIECE, :]
                for q in range(4)
            ]
            return jnp.concatenate(blocks, axis=0)

        total = mm_nt(rows_of_turn(grad_projected), w_proj[...])
        total = total + mm_nt(rows_of_turn(grad_out_gate), w_gate[...])
        total = total + mm(rows_of_turn(grad_low_rank), w_rank[...])
        rounded = total.astype(BF16)
        for q in range(4):
            part_g[s, q, h * PIECE : (h + 1) * PIECE] = rounded[q * PIECE : (q + 1) * PIECE]
        for index in range(2):
            scatter(turn, index, False).start()
        small[32:33, :] += jnp.sum(
            total * rows_of_turn(normed).astype(F32), axis=0, keepdims=True
        )

    for turn in range(turns):
        input_grad(turn)
    for turn in range(turns):
        for index in range(2, 4):
            scatter(turn, index, False).start()


    packed[...] = jnp.zeros_like(packed)
    packed[0:rank, :] = small[0:rank, :]
    packed[16:17, :] = small[32:33, :]
    packed[17:18, :] = small[33:34, :]
    packed[18:19, :dv] = small[34:35, :dv]
    packed[18:19, dv : dv + dk] = small[35:36, :dk]
    taps_in_row, ranks_in_row = width // c3, width // dk
    for j in range(CONV):
        row, column = 19 + j // taps_in_row, (j % taps_in_row) * c3
        packed[row : row + 1, column : column + c3] = small[16 + j : 17 + j, dk : dk + c3]
    for j in range(rank):
        row, column = 22 + j // ranks_in_row, (j % ranks_in_row) * dk
        packed[row : row + 1, column : column + dk] = small[16 + j : 17 + j, :dk]
    small_low[0] = packed[...].astype(BF16)
    for copy in small_to_sides:
        copy.start()
    for copy in small_to_sides:
        copy.wait_recv()
    small_low[1] = paired_sum(small_low[0], small_seq, range(sides - 1)).astype(BF16)
    for copy in small_to_places:
        copy.start()
    for copy in mixer_to_sides:
        copy.wait_recv()
    own = pl.ds(pl.multiple_of(side * share_rows, 16), share_rows)
    mixer_sum = mixer_grad[own, :]
    for hop in range(sides - 1):
        mixer_sum = mixer_sum + mixer_seq[hop]
    mixer_grad[own, :] = mixer_sum
    for copy in mixer_to_places:
        copy.start()
    for copy in output_to_heads:
        copy.wait_recv()
    output_kept[0] = output_kept[0] + output_mp[0] + output_mp[1] + output_mp[2]
    for copy in output_to_places:
        copy.start()

    loads[11].wait()
    for turn in range(turns):
        s, h = turn // halves, turn % halves
        total = residual[turn] + summed(turn, True)
        position = side * length + me * (length // 4) + h * PIECE
        position = position + lax.broadcasted_iota(jnp.int32, (PIECE, 1), 0)
        limit = params[HEAD_GAIN : HEAD_GAIN + 1, dv + s : dv + s + 1]
        out_stage[turn] = jnp.where(position.astype(F32) < limit, total, 0.0).astype(BF16)
        store(turn, 0).start()
    for turn in range(turns):
        pass_on(turn, False)
    for copy in small_to_places:
        copy.wait_recv()
    summed_here = paired_sum(small_low[1], small_dp, range(places - 1))
    small_low[2] = summed_here.astype(BF16)
    for copy in small_to_heads:
        copy.start()
    shard, shards = side * places + place, sides * places

    def own_columns(values):
        size = values.shape[1] // shards
        total = values[:, 0:size]
        for index in range(1, shards):
            total = jnp.where(shard == index, values[:, index * size : (index + 1) * size], total)
        return total

    for j in range(CONV):
        row, column = 19 + j // taps_in_row, (j % taps_in_row) * c3
        small_out[j : j + 1, : c3 // shards] = own_columns(
            summed_here[row : row + 1, column : column + c3]
        )
    for j in range(rank):
        row, column = 22 + j // ranks_in_row, (j % ranks_in_row) * dk
        small_out[8 + j : 9 + j, : dk // shards] = own_columns(
            summed_here[row : row + 1, column : column + dk]
        )
    small_out[24:25, : dk // shards] = own_columns(summed_here[18:19, dv : dv + dk])
    for copy in hidden_to_places:
        copy.wait_recv()
    own_shard = pl.ds(pl.multiple_of(place * shard_rows, 16), shard_rows)
    for kind in range(3):
        total = hidden_kept[kind, own_shard, :].astype(F32)
        for hop in range(places - 1):
            total = total + hidden_dp[hop, kind].astype(F32)
        hidden_out[kind] = total


    loads[14].wait()
    loads[15].wait()
    for turn in range(turns):
        s, h = turn // halves, turn % halves
        grad_normed = summed(turn, False)
        rows = tok[s, h * PIECE : (h + 1) * PIECE].astype(F32)
        inverse = lax.rsqrt(jnp.mean(rows * rows, axis=-1, keepdims=True) + EPS_NORM)
        unit = rows * inverse
        scaled = grad_normed * mixer_gain
        through = inverse * (scaled - unit * jnp.mean(scaled * unit, axis=-1, keepdims=True))
        grad_residual[turn] = grad_residual[turn] + through
        store(turn, 1).start()
    for copy in small_to_heads:
        copy.wait_recv()
    shared = paired_sum(small_low[2], small_mp, (1, 0, 2))
    shared_out[...] = shared
    shared_out[16:17, :] = shared[16:17, :] / mixer_gain
    for copy in mixer_to_places + output_to_places:
        copy.wait_recv()
    total = mixer_grad[own_share(place), :].astype(F32)
    for hop in range(places - 1):
        total = total + mixer_dp[hop].astype(F32)
    mixer_out[:, : c3 + dv] = total
    total = output_kept[0, own_shard, :].astype(F32)
    for hop in range(places - 1):
        total = total + output_dp[hop].astype(F32)
    mixer_out[:, c3 + dv :] = total


    for copies in (
        hidden_to_sides, output_to_sides, state_to_sides, mixer_to_sides, small_to_sides,
        [edge_copy], hidden_to_places, mixer_to_places, output_to_places, small_to_places,
        output_to_heads, small_to_heads,
    ):
        for copy in copies:
            copy.wait_send()
    for turn in range(turns):
        for index in range(6):
            scatter(turn, index, True).wait_send()
            scatter(turn, index, False).wait_send()
        store(turn, 0).wait()
        store(turn, 1).wait()


def mixer_back(
    grad_gated, head, profile, out_gate, projected, cumulative, states, normed, tok, residual,
    grad_residual, out_part, hidden_grads, output_parts, w_proj, w_gate, low_rank, halo, params,
    rank_up, w_rank, before, entering, decays, channel_part, seq_count, dp_count,
):
    sequences, length, width = normed.shape
    dv, c3 = grad_gated.shape[-1], projected.shape[-1]
    rank, dk = rank_up.shape
    units = hidden_grads.shape[-1]
    quarter = length // 4
    turns = sequences * quarter // PIECE
    share_rows = width // seq_count
    shard_rows = share_rows // dp_count
    peers, others = seq_count - 1, dp_count - 1
    anywhere = pl.BlockSpec(memory_space=pl.ANY)
    vmem = pl.BlockSpec(memory_space=pltpu.VMEM)
    dma = pltpu.SemaphoreType.DMA

    def low(*shape):
        return pltpu.VMEM(shape, BF16)

    def full(*shape):
        return pltpu.VMEM(shape, F32)

    hops = [
        low(turns, HALF, width),
        low(turns, HALF, width),
        low(turns, PIECE, width),
        low(turns, PIECE, width),
    ]
    return pl.pallas_call(
        mixer_back_body,
        in_specs=[anywhere] * 16 + [vmem] * 9,
        out_specs=[anywhere] * 2 + [vmem] * 4,
        out_shape=[
            shape_of((turns, PIECE, width), BF16),
            shape_of((turns, PIECE, width), F32),
            shape_of((3, shard_rows, units), F32),
            shape_of((shard_rows, c3 + 2 * dv), F32),
            shape_of((32, 128), F32),
            shape_of((PACKED, width), F32),
        ],
        scratch_shapes=[
            low(sequences, length, dv),
            low(sequences, length, dv),
            low(sequences, length, dk),
            low(sequences, length, dv),
            low(sequences, length, c3),
            full(sequences, length, dk),
            low(length // CHUNK, dv, sequences * dk),
            low(sequences, length, width),
            low(sequences, quarter, width),
            full(turns, PIECE, width),
            full(turns, PIECE, width),
            low(sequences, 4, quarter, width),
            low(sequences, 4, quarter, width),
            low(width, c3),
            low(width, dv),
            low(3, share_rows, units),
            low(peers, 3, share_rows, units),
            low(others, 3, shard_rows, units),
            low(4, share_rows, dv),
            low(peers, 4, share_rows, dv),
            low(3, share_rows, dv),
            low(others, shard_rows, dv),
            *hops,
            *hops,
            low(sequences, length, dv),
            low(sequences, length, dv),
            low(sequences, length, c3),
            low(sequences, length, rank),
            low(width, c3 + dv),
            low(peers, share_rows, c3 + dv),
            low(others, shard_rows, c3 + dv),
            full(dv, sequences * dk),
            full(peers, dv, sequences * dk),
            full(dv, sequences * dk),
            full(sequences, STEP + 8, c3),
            full(sequences, STEP + 8, c3),
            full(sequences, 16, c3),
            full(sequences, 16, c3),
            full(SMALL, width),
            full(PACKED, width),
            low(3, PACKED, width),
            low(peers, PACKED, width),
            low(others, PACKED, width),
            low(3, PACKED, width),
            low(turns, PIECE, width),
            dma((16,)),
            dma((6, peers)),
            dma((6, peers)),
            dma((4, others)),
            dma((4, others)),
            dma((2, 3)),
            dma((2, 3)),
            dma((6, turns)),
            dma((6, turns)),
            dma((6, turns)),
            dma((6, turns)),
            dma((2, turns)),
        ],
        compiler_params=pltpu.CompilerParams(
            collective_id=1, has_side_effects=True, vmem_limit_bytes=64 * 2**20
        ),
        cost_estimate=pl.CostEstimate(
            flops=2 * sequences * length * width * 2 * (c3 + dv) * 2,
            bytes_accessed=sequences * length * width * 16,
            transcendentals=0,
        ),
        name="mixer_back",
    )(
        grad_gated, head, profile, out_gate, projected, cumulative, states, normed, tok, residual,
        grad_residual, out_part, hidden_grads, output_parts, w_proj, w_gate, low_rank, halo,
        params, rank_up, w_rank, before, entering, decays, channel_part,
    )


def finish_body(
    outputs, token_grads, hidden, mixer, small, shared,
    output, tokens_grad, mixer_gain, project, filters, rank_down, rank_up, bias, w_gate,
    head_gain, w_out, channel_gain, hidden_gate, hidden_up, hidden_down,
):
    output[...] = jnp.swapaxes(outputs[:, 0], 0, 1)
    tokens_grad[...] = jnp.swapaxes(token_grads[:, 0], 0, 1)

    @pl.when(pl.program_id(0) == 0)
    def _():
        c3, dv = project.shape[-1], w_gate.shape[-1]
        project[:, 0, :] = mixer[:, :c3]
        w_gate[...] = mixer[:, c3 : c3 + dv]
        w_out[...] = mixer[:, c3 + dv :].T
        for s in range(filters.shape[0]):
            filters[s] = small[s : s + 1, : filters.shape[-1]]
        for s in range(rank_up.shape[0]):
            rank_up[s] = small[8 + s : 9 + s, : rank_up.shape[-1]]
        bias[...] = small[24:25, : bias.shape[-1]]
        rank_down[...] = shared[: rank_down.shape[0], :]
        mixer_gain[...] = shared[16:17, :]
        channel_gain[...] = shared[17:18, :]
        head_gain[...] = shared[18:19, :dv]
        for target, kind in ((hidden_gate, 0), (hidden_up, 1), (hidden_down, 2)):
            target[...] = hidden[kind].T


def finish(outputs, token_grads, hidden, mixer, small, shared, sequences, c3, dv, dk, rank, shards):
    turns, piece, width = outputs.shape
    halves = turns // sequences
    rows, units = hidden.shape[1:]

    def by_half(values):
        return values.reshape(sequences, halves, piece, width)

    half = pl.BlockSpec((sequences, 1, piece, width), lambda i: (0, i, 0, 0))
    placed = pl.BlockSpec((piece, sequences, width), lambda i: (i, 0, 0))
    shapes = [
        (1, width),
        (rows, 1, c3),
        (CONV, 1, c3 // shards),
        (rank, width),
        (rank, 1, dk // shards),
        (1, dk // shards),
        (rows, dv),
        (1, dv),
        (dv, rows),
        (1, width),
        (units, rows),
        (units, rows),
        (units, rows),
    ]
    return pl.pallas_call(
        finish_body,
        grid=(halves,),
        in_specs=[half, half] + [whole(v.shape) for v in (hidden, mixer, small, shared)],
        out_specs=[placed, placed] + [whole(shape) for shape in shapes],
        out_shape=[
            shape_of((halves * piece, sequences, width), BF16),
            shape_of((halves * piece, sequences, width), F32),
        ]
        + [shape_of(shape, F32) for shape in shapes],
        compiler_params=pltpu.CompilerParams(
            dimension_semantics=("arbitrary",), vmem_limit_bytes=VMEM_LIMIT
        ),
        name="finish",
    )(by_half(outputs), by_half(token_grads), hidden, mixer, small, shared)


def on_device(
    tokens, lengths, mixer_gain, project_weight, filter_weight, rank_down, rank_up, decay_bias,
    gate_weight, head_gain, output_weight, channel_gain, hidden_gate, hidden_up, hidden_down,
    cotangent,
):
    length, sequences, width = tokens.shape
    seq_count, dp_count = lax.axis_size("seq"), lax.axis_size("dp")
    shards = seq_count * dp_count
    own_rows = length // lax.axis_size("mp")
    w_proj, rank_up_here = project_weight[:, 0], rank_up[:, 0]
    c3, dv = w_proj.shape[1], gate_weight.shape[1]
    rank, dk = rank_up_here.shape
    w_rank = rank_down.T
    (
        params, tok, normed, projected, low_rank, cumulative, states, before, out_gate, profile,
        gated, head, halo, entering, decays, w_others,
    ) = front(
        tokens, mixer_gain, channel_gain, head_gain, filter_weight[:, 0], decay_bias, lengths,
        w_proj, gate_weight, w_rank, rank_up_here, output_weight, seq_count,
    )
    (
        out_part, hidden_grads, output_parts, grad_gated, residual, grad_residual, channel_part,
    ) = feed_forward(
        gated, output_weight, w_others, tok, params, hidden_gate.T, hidden_up.T, hidden_down,
        cotangent,
    )
    results = mixer_back(
        grad_gated, head, profile, out_gate, projected, cumulative, states, normed,
        tok.reshape(sequences, 4, own_rows, width), residual, grad_residual, out_part,
        hidden_grads, output_parts, w_proj, gate_weight, low_rank, halo, params, rank_up_here,
        w_rank, before, entering, decays, channel_part, seq_count, dp_count,
    )
    (
        output, tokens_grad, mixer_gain_grad, project_grad, filter_grad, rank_down_grad,
        rank_up_grad, decay_bias_grad, gate_grad, head_gain_grad, output_weight_grad,
        channel_gain_grad, hidden_gate_grad, hidden_up_grad, hidden_down_grad,
    ) = finish(*results, sequences, c3, dv, dk, rank, shards)
    return (
        output,
        tokens_grad,
        mixer_gain_grad[0],
        project_grad,
        filter_grad,
        rank_down_grad.T,
        rank_up_grad,
        decay_bias_grad,
        gate_grad,
        head_gain_grad[0],
        output_weight_grad,
        channel_gain_grad[0],
        hidden_gate_grad.T,
        hidden_up_grad.T,
        hidden_down_grad,
    )


def solution(mesh):
    in_specs = (
        P("seq", "dp", None),
        P("dp"),
        P(),
        P(None, "mp", None),
        P(None, "mp", None),
        P(),
        P(None, "mp", None),
        P("mp", None),
        P(None, "mp"),
        P(),
        P("mp", None),
        P(),
        P(None, "mp"),
        P(None, "mp"),
        P("mp", None),
        P("seq", "dp", None),
    )
    out_specs = (
        P(("seq", "mp"), "dp", None),
        P(("seq", "mp"), "dp", None),
        P(),
        P(("seq", "dp"), "mp", None),
        P(None, "mp", ("seq", "dp")),
        P(),
        P(None, "mp", ("seq", "dp")),
        P("mp", ("seq", "dp")),
        P(("seq", "dp"), "mp"),
        P(),
        P("mp", ("seq", "dp")),
        P(),
        P(("seq", "dp"), "mp"),
        P(("seq", "dp"), "mp"),
        P("mp", ("seq", "dp")),
    )
    return jax.shard_map(
        on_device, mesh=mesh, in_specs=in_specs, out_specs=out_specs, check_vma=False
    )
```
